32 devices in a mesh: shard: 4 (over x, core), ctx: 2 (over y), tensor: 4 (over z).
Axes of the slice: x: 2, y: 2, z: 4, core: 2. Of those that a mesh axis runs over, the one named last changes fastest.
Arguments:
- layer_input: float32 [4, 2048, 768], P('shard', 'ctx'), may hold values from -6 to 6
- encoder_out: float32 [4, 1024, 768], P('shard', 'ctx'), may hold values from -6 to 6
- enc_length: int32 [4], P('shard'), may hold values from 256 to 1024, as said below
- parent_ids: int32 [4, 16], P('shard'), may hold values from -1 to 15, as said below
- token_segment: int32 [4, 2048], P('shard'), may hold values from 0 to 15, as said below
- self_query: bfloat16 [768, 768], P('shard', 'tensor'), may hold values from -0.21875 to 0.21875
- self_key: bfloat16 [768, 768], P('shard', 'tensor'), may hold values from -0.21875 to 0.21875
- self_value: bfloat16 [768, 768], P('shard', 'tensor'), may hold values from -0.21875 to 0.21875
- self_output: bfloat16 [768, 768], P('tensor', 'shard'), may hold values from -3 to 3
- cross_query: bfloat16 [768, 768], P('shard', 'tensor'), may hold values from -0.21875 to 0.21875
- cross_key: bfloat16 [768, 768], P('shard', 'tensor'), may hold values from -0.21875 to 0.21875
- cross_value: bfloat16 [768, 768], P('shard', 'tensor'), may hold values from -0.21875 to 0.21875
- cross_output: bfloat16 [768, 768], P('tensor', 'shard'), may hold values from -3 to 3
- ffn_up: bfloat16 [768, 3072], P('shard', 'tensor'), may hold values from -0.21875 to 0.21875
- ffn_down: bfloat16 [3072, 768], P('tensor', 'shard'), may hold values from -0.109375 to 0.109375
- self_qbias: float32 [768], P('tensor'), may hold values from -3 to 3
- self_vbias: float32 [768], P('tensor'), may hold values from -3 to 3
- self_obias: float32 [768], replicated, may hold values from -3 to 3
- cross_qbias: float32 [768], P('tensor'), may hold values from -3 to 3
- cross_vbias: float32 [768], P('tensor'), may hold values from -3 to 3
- cross_obias: float32 [768], replicated, may hold values from -3 to 3
- ffn_upbias: float32 [3072], P('tensor'), may hold values from -3 to 3
- ffn_downbias: float32 [768], replicated, may hold values from -3 to 3
- norm1_gain: float32 [768], replicated, may hold values from 0.5 to 1.5
- norm1_shift: float32 [768], replicated, may hold values from -2 to 2
- norm2_gain: float32 [768], replicated, may hold values from 0.5 to 1.5
- norm2_shift: float32 [768], replicated, may hold values from -2 to 2
- norm3_gain: float32 [768], replicated, may hold values from 0.5 to 1.5
- norm3_shift: float32 [768], replicated, may hold values from -2 to 2
- out_grad: float32 [4, 2048, 768], P('shard', 'ctx'), may hold values from -6 to 6
Outputs:
- out_hidden: float32 [4, 2048, 768], P('shard', 'ctx')
- grad_input: float32 [4, 2048, 768], P('shard', 'ctx')
- grad_encoder: float32 [4, 1024, 768], P('shard', 'ctx')
- grad_self_query: float32 [768, 768], P('shard', 'tensor')
- grad_self_key: float32 [768, 768], P('shard', 'tensor')
- grad_self_value: float32 [768, 768], P('shard', 'tensor')
- grad_self_output: float32 [768, 768], P('tensor', 'shard')
- grad_cross_query: float32 [768, 768], P('shard', 'tensor')
- grad_cross_key: float32 [768, 768], P('shard', 'tensor')
- grad_cross_value: float32 [768, 768], P('shard', 'tensor')
- grad_cross_output: float32 [768, 768], P('tensor', 'shard')
- grad_ffn_up: float32 [768, 3072], P('shard', 'tensor')
- grad_ffn_down: float32 [3072, 768], P('tensor', 'shard')
- grad_self_qbias: float32 [768], P('tensor')
- grad_self_vbias: float32 [768], P('tensor')
- grad_self_obias: float32 [768], replicated
- grad_cross_qbias: float32 [768], P('tensor')
- grad_cross_vbias: float32 [768], P('tensor')
- grad_cross_obias: float32 [768], replicated
- grad_ffn_upbias: float32 [3072], P('tensor')
- grad_ffn_downbias: float32 [768], replicated
- grad_norm1_gain: float32 [768], replicated
- grad_norm1_shift: float32 [768], replicated
- grad_norm2_gain: float32 [768], replicated
- grad_norm2_shift: float32 [768], replicated
- grad_norm3_gain: float32 [768], replicated
- grad_norm3_shift: float32 [768], replicated
The draws below stay inside these ranges and needn't reach their ends.
Inputs may be any that keep to these rules, and one draw needn't show every extreme that they name: `enc_length`: some tree uses all 1024 encoder positions. `parent_ids`: in each tree the 16 segment labels form a trunk chain of 8 segments from a root whose parent is -1, then 4 branches whose parent is the trunk's last segment, each the parent of one leaf. `token_segment`: each segment fills exactly one aligned block of 128 tokens of its tree; the trunk's segments come first in chain order, then each branch followed by its leaf.
All inputs are finite; a program needn't handle non-finite values.
Results may differ from the reference program's by a relative error of at most 0.025.
The reference program's roundings to bfloat16 on the way count: a program that leaves them out, or rounds other values in their place, can miss the bound.
Values may be sent and summed in bfloat16 or wider, within the bound.
No kernel may reach another device: no remote copies, remote signals or barrier semaphores. Data moves between devices by JAX's collectives and lax.ppermute only.
A program may use at most 256 MiB of HBM per device.

```python
import jax
import jax.numpy as jnp
from jax import lax

D = 768
HEADS = 12
HEAD_DIM = 64
FF = 3072
SEG = 128
TRUNK = 1024
BRANCHES = 4
ENC = 1024
TREE_LEN = 2048
TREES = 4


def tree_layout(base_key):
    trunk_count = TRUNK // SEG
    role_count = trunk_count + 2 * BRANCHES
    role_ids = jnp.arange(role_count, dtype=jnp.int32)
    parent_role = jnp.where(role_ids < trunk_count, role_ids - 1, jnp.where(role_ids < trunk_count + BRANCHES, trunk_count - 1, role_ids - BRANCHES))
    tree_keys = jax.random.split(base_key, TREES)
    labels = jax.vmap(lambda one_key: jax.random.permutation(one_key, role_count))(tree_keys).astype(jnp.int32)
    parent_label = jnp.where(parent_role[None, :] >= 0, jnp.take(labels, jnp.maximum(parent_role, 0), axis=1), -1).astype(jnp.int32)
    parents = jax.vmap(lambda label_row, parent_row: jnp.zeros((role_count,), jnp.int32).at[label_row].set(parent_row))(labels, parent_label)
    blocks = jnp.arange(role_count, dtype=jnp.int32)
    pair_index = (blocks - trunk_count) // 2
    block_role = jnp.where(blocks < trunk_count, blocks, jnp.where((blocks - trunk_count) % 2 == 0, trunk_count + pair_index, trunk_count + BRANCHES + pair_index))
    block_labels = jnp.take(labels, block_role, axis=1)
    segments = jnp.repeat(block_labels, SEG, axis=1).astype(jnp.int32)
    return (parents, segments)


def draw_parent_ids(key, part):
    return tree_layout(jax.random.fold_in(key, 7))[0]


def draw_token_segment(key, part):
    return tree_layout(jax.random.fold_in(key, 7))[1]


def draw_enc_length(key, part):
    lengths = jax.random.randint(jax.random.fold_in(key, 11), (TREES,), ENC // 4, ENC + 1, dtype=jnp.int32)
    return lengths.at[0].set(ENC)


def shard_levels(key, extent, cuts, least, high):
    def one(position, blocks):
        steps = jax.random.uniform(jax.random.fold_in(jax.random.fold_in(key, 6), position), (blocks,), jnp.float32, least / len(cuts), high / len(cuts))
        return jnp.repeat(jnp.exp(steps), extent[position] // blocks).reshape((-1,) + (1,) * (len(extent) - position - 1))

    loudness = one(*cuts[0])
    for cut in cuts[1:]:
        loudness = loudness * one(*cut)
    return loudness


def gaussian(key, extent, spread, reach, shards=(), held_as=jnp.bfloat16):
    values = jax.random.normal(key, extent, jnp.float32) * spread
    if len(shards) > 0:
        values = shard_levels(key, extent, shards, -0.22, 0.18) * values
    return jnp.clip(values, min=-reach, max=reach).astype(held_as)


def setup_inputs(seed: int = 0) -> dict:
    keys = jax.random.split(jax.random.key(seed), 31)
    layer_input = gaussian(keys[0], (TREES, TREE_LEN, D), 1.0, 6.0, ((0, 4), (1, 2)), jnp.float32)
    encoder_out = gaussian(keys[1], (TREES, ENC, D), 1.0, 6.0, ((0, 4), (1, 2)), jnp.float32)
    enc_length = draw_enc_length(jax.random.fold_in(keys[30], 71), 0)
    parent_ids = draw_parent_ids(jax.random.fold_in(keys[30], 71), 0)
    token_segment = draw_token_segment(jax.random.fold_in(keys[30], 71), 0)
    self_query = gaussian(keys[5], (D, D), D ** -0.5, 0.21875, ((0, 4), (1, 4)))
    self_key = gaussian(keys[6], (D, D), D ** -0.5, 0.21875, ((0, 4), (1, 4)))
    self_value = gaussian(keys[7], (D, D), D ** -0.5, 0.21875, ((0, 4), (1, 4)))
    self_output = gaussian(keys[8], (D, D), 4 ** -0.5, 3.0, ((0, 4), (1, 4)))
    cross_query = gaussian(keys[9], (D, D), D ** -0.5, 0.21875, ((0, 4), (1, 4)))
    cross_key = gaussian(keys[10], (D, D), D ** -0.5, 0.21875, ((0, 4), (1, 4)))
    cross_value = gaussian(keys[11], (D, D), D ** -0.5, 0.21875, ((0, 4), (1, 4)))
    cross_output = gaussian(keys[12], (D, D), 4 ** -0.5, 3.0, ((0, 4), (1, 4)))
    ffn_up = gaussian(keys[13], (D, FF), D ** -0.5, 0.21875, ((0, 4), (1, 4)))
    ffn_down = gaussian(keys[14], (FF, D), FF ** -0.5, 0.109375, ((0, 4), (1, 4)))
    self_qbias = gaussian(keys[15], (D,), 0.5, 3.0, ((0, 4),), jnp.float32)
    self_vbias = gaussian(keys[16], (D,), 0.5, 3.0, ((0, 4),), jnp.float32)
    self_obias = gaussian(keys[17], (D,), 0.5, 3.0, (), jnp.float32)
    cross_qbias = gaussian(keys[18], (D,), 0.5, 3.0, ((0, 4),), jnp.float32)
    cross_vbias = gaussian(keys[19], (D,), 0.5, 3.0, ((0, 4),), jnp.float32)
    cross_obias = gaussian(keys[20], (D,), 0.5, 3.0, (), jnp.float32)
    ffn_upbias = gaussian(keys[21], (FF,), 0.5, 3.0, ((0, 4),), jnp.float32)
    ffn_downbias = gaussian(keys[22], (D,), 0.5, 3.0, (), jnp.float32)
    norm1_gain = jnp.clip(1.0 + 0.1 * jax.random.normal(keys[23], (D,), jnp.float32), 0.5, 1.5)
    norm1_shift = gaussian(keys[24], (D,), 0.3, 2.0, (), jnp.float32)
    norm2_gain = jnp.clip(1.0 + 0.1 * jax.random.normal(keys[25], (D,), jnp.float32), 0.5, 1.5)
    norm2_shift = gaussian(keys[26], (D,), 0.3, 2.0, (), jnp.float32)
    norm3_gain = jnp.clip(1.0 + 0.1 * jax.random.normal(keys[27], (D,), jnp.float32), 0.5, 1.5)
    norm3_shift = gaussian(keys[28], (D,), 0.3, 2.0, (), jnp.float32)
    out_grad = gaussian(keys[29], (TREES, TREE_LEN, D), 1.0, 6.0, ((0, 4), (1, 2)), jnp.float32)
    return {"layer_input": layer_input, "encoder_out": encoder_out, "enc_length": enc_length, "parent_ids": parent_ids, "token_segment": token_segment, "self_query": self_query, "self_key": self_key, "self_value": self_value, "self_output": self_output, "cross_query": cross_query, "cross_key": cross_key, "cross_value": cross_value, "cross_output": cross_output, "ffn_up": ffn_up, "ffn_down": ffn_down, "self_qbias": self_qbias, "self_vbias": self_vbias, "self_obias": self_obias, "cross_qbias": cross_qbias, "cross_vbias": cross_vbias, "cross_obias": cross_obias, "ffn_upbias": ffn_upbias, "ffn_downbias": ffn_downbias, "norm1_gain": norm1_gain, "norm1_shift": norm1_shift, "norm2_gain": norm2_gain, "norm2_shift": norm2_shift, "norm3_gain": norm3_gain, "norm3_shift": norm3_shift, "out_grad": out_grad}


@jax.custom_vjp
def low(v):
    return lax.optimization_barrier(v.astype(jnp.bfloat16)).astype(jnp.float32)

@jax.custom_vjp
def low_back(v):
    return v

def low_keep(v):
    return (low(v), None)

def low_pass(kept, grad):
    return (grad,)

def back_keep(v):
    return (v, None)

def back_low(kept, grad):
    return (low(grad),)
low.defvjp(low_keep, low_pass)
low_back.defvjp(back_keep, back_low)
eps_norm = 1e-05
row_block = 512

def matmul(left_side, right_side):
    return jnp.dot(left_side, right_side, precision=lax.Precision.HIGHEST, preferred_element_type=jnp.float32)

def layer_norm(values, gain_row, shift_row):
    center = values - lax.optimization_barrier(jnp.mean(values, axis=-1, keepdims=True))
    inverse = lax.rsqrt(lax.optimization_barrier(jnp.mean(center * center, axis=-1, keepdims=True)) + eps_norm)
    return center * inverse * gain_row + shift_row

def closure_of(parent_row):
    segment_count = parent_row.shape[0]
    labels = jnp.arange(segment_count, dtype=jnp.int32)
    closure = (parent_row[:, None] == labels[None, :]).astype(jnp.float32)
    for squaring in range(max(1, segment_count.bit_length())):
        closure = jnp.minimum(closure + matmul(closure, closure), 1.0)
    return closure

def path_allowed(query_seg, query_pos, key_seg, closure):
    segment_count = closure.shape[0]
    labels = jnp.arange(segment_count, dtype=jnp.int32)
    query_hot = (query_seg[:, None] == labels[None, :]).astype(jnp.float32)
    key_hot = (key_seg[:, None] == labels[None, :]).astype(jnp.float32)
    ancestor_rows = matmul(query_hot, closure)
    strict = matmul(ancestor_rows, key_hot.T) > 0.5
    same_seg = matmul(query_hot, key_hot.T) > 0.5
    key_pos = jnp.arange(key_seg.shape[0], dtype=jnp.int32)
    return strict | same_seg & (key_pos[None, :] <= query_pos[:, None])

def attend(queries, keys_all, values_all, allowed):
    scores = low_back(jnp.einsum('qhd,khd->hqk', queries, keys_all, precision=lax.Precision.HIGHEST))
    scores = jnp.where(allowed[None], scores, -jnp.inf)
    row_peak = lax.optimization_barrier(jnp.max(scores, axis=-1, keepdims=True))
    exponent = jnp.exp(scores - row_peak)
    weights_soft = low(exponent / lax.optimization_barrier(jnp.sum(exponent, axis=-1, keepdims=True)))
    return jnp.einsum('hqk,khd->qhd', weights_soft, values_all, precision=lax.Precision.HIGHEST)

def blocked_attention(queries, keys_all, values_all, allow_fn):
    tree_rows = queries.shape[0]
    block_rows = min(row_block, tree_rows)
    block_count = tree_rows // block_rows
    positions = jnp.arange(tree_rows, dtype=jnp.int32)

    def one_block(block_args):
        block_queries, block_positions = block_args
        return attend(block_queries, keys_all, values_all, allow_fn(block_positions))
    outputs = lax.map(jax.checkpoint(one_block), (queries.reshape((block_count, block_rows) + queries.shape[1:]), positions.reshape(block_count, block_rows)))
    return outputs.reshape(queries.shape)

def tree_forward(tree_input, tree_encoder, weights_all, segments, closure, length):
    self_query, self_key, self_value, self_output, cross_query, cross_key, cross_value, cross_output, ffn_up, ffn_down, self_qbias, self_vbias, self_obias, cross_qbias, cross_vbias, cross_obias, ffn_upbias, ffn_downbias, norm1_gain, norm1_shift, norm2_gain, norm2_shift, norm3_gain, norm3_shift = weights_all
    scaling = HEAD_DIM ** (-0.5)
    tree_rows = tree_input.shape[0]
    enc_total = tree_encoder.shape[0]
    head_shape = (tree_rows, HEADS, HEAD_DIM)
    enc_shape = (enc_total, HEADS, HEAD_DIM)
    input_reduced = low(tree_input)
    queries = low((low_back(matmul(input_reduced, self_query)) + self_qbias) * scaling)
    keys_self = low(low_back(matmul(input_reduced, self_key)))
    values_self = low(low_back(matmul(input_reduced, self_value)) + self_vbias)

    def self_allow(block_positions):
        return path_allowed(segments[block_positions], block_positions, segments, closure)
    mixture = blocked_attention(queries.reshape(head_shape), keys_self.reshape(head_shape), values_self.reshape(head_shape), self_allow)
    mix_low = low(low_back(mixture.reshape(tree_rows, HEADS * HEAD_DIM)))
    sum_one = tree_input + low_back(matmul(mix_low, self_output)) + self_obias
    hidden_one = layer_norm(sum_one, norm1_gain, norm1_shift)
    hidden_low = low(hidden_one)
    enc_low = low(tree_encoder)
    cross_queries = low((low_back(matmul(hidden_low, cross_query)) + cross_qbias) * scaling)
    cross_keys = low(low_back(matmul(enc_low, cross_key)))
    cross_values = low(low_back(matmul(enc_low, cross_value)) + cross_vbias)
    valid_keys = jnp.arange(enc_total, dtype=jnp.int32) < length

    def cross_allow(block_positions):
        return jnp.broadcast_to(valid_keys[None, :], (block_positions.shape[0], enc_total))
    cross_mixture = blocked_attention(cross_queries.reshape(head_shape), cross_keys.reshape(enc_shape), cross_values.reshape(enc_shape), cross_allow)
    cross_low = low(low_back(cross_mixture.reshape(tree_rows, HEADS * HEAD_DIM)))
    sum_two = hidden_one + low_back(matmul(cross_low, cross_output)) + cross_obias
    hidden_two = layer_norm(sum_two, norm2_gain, norm2_shift)
    hidden_two_low = low(hidden_two)
    ffn_pre = low_back(matmul(hidden_two_low, ffn_up)) + ffn_upbias
    ffn_act = low(jax.nn.gelu(ffn_pre, approximate=False))
    sum_three = hidden_two + low_back(matmul(ffn_act, ffn_down)) + ffn_downbias
    return layer_norm(sum_three, norm3_gain, norm3_shift)

def reference(layer_input, encoder_out, enc_length, parent_ids, token_segment, self_query, self_key, self_value, self_output, cross_query, cross_key, cross_value, cross_output, ffn_up, ffn_down, self_qbias, self_vbias, self_obias, cross_qbias, cross_vbias, cross_obias, ffn_upbias, ffn_downbias, norm1_gain, norm1_shift, norm2_gain, norm2_shift, norm3_gain, norm3_shift, out_grad):
    weights_all = tuple((operand.astype(jnp.float32) for operand in (self_query, self_key, self_value, self_output, cross_query, cross_key, cross_value, cross_output, ffn_up, ffn_down, self_qbias, self_vbias, self_obias, cross_qbias, cross_vbias, cross_obias, ffn_upbias, ffn_downbias, norm1_gain, norm1_shift, norm2_gain, norm2_shift, norm3_gain, norm3_shift)))
    zero_grads = jax.tree.map(jnp.zeros_like, weights_all)

    def one_tree(grad_sums, tree_args):
        tree_input, tree_encoder, length, parent_row, segments, tree_grad = tree_args
        closure = closure_of(parent_row)

        def forward(input_value, encoder_value, weights_value):
            return tree_forward(input_value, encoder_value, weights_value, segments, closure, length)
        result, pullback = jax.vjp(forward, tree_input.astype(jnp.float32), tree_encoder.astype(jnp.float32), weights_all)
        grad_tree, grad_enc, grad_weights = pullback(tree_grad.astype(jnp.float32))
        return (jax.tree.map(jnp.add, grad_sums, grad_weights), (result, grad_tree, grad_enc))
    totals, (results, input_grads, encoder_grads) = lax.scan(one_tree, zero_grads, (layer_input, encoder_out, enc_length, parent_ids, token_segment, out_grad))
    return (results, input_grads, encoder_grads, totals[0], totals[1], totals[2], totals[3], totals[4], totals[5], totals[6], totals[7], totals[8], totals[9], totals[10], totals[11], totals[12], totals[13], totals[14], totals[15], totals[16], totals[17], totals[18], totals[19], totals[20], totals[21], totals[22], totals[23])
```

```python
import functools

import jax
import jax.numpy as jnp
from jax import lax
from jax.experimental import pallas as pl
from jax.experimental.pallas import tpu as pltpu
from jax.sharding import PartitionSpec as P

HEAD_DIM = 64
LANES = 128
TILE = 256
NEG = -1e30
EPS = 1e-05
F32 = jnp.float32
BF16 = jnp.bfloat16
VMEM_LIMIT = 56 * 1024 * 1024


def dot_of(a, b, a_dim, b_dim):
    return lax.dot_general(a, b, (((a_dim,), (b_dim,)), ((), ())), preferred_element_type=F32)


def nn(a, b):
    return dot_of(a, b, 1, 0)


def nt(a, b):
    return dot_of(a, b, 1, 1)


def tn(a, b):
    return dot_of(a, b, 0, 0)


def head_lanes(rows, half):
    lane = lax.broadcasted_iota(jnp.int32, (rows, LANES), 1)
    return (lane < HEAD_DIM) if half == 0 else (lane >= HEAD_DIM)


def flags_of(rows, seg):
    lane = lax.broadcasted_iota(jnp.int32, (rows, LANES), 1) % HEAD_DIM
    row = lax.broadcasted_iota(jnp.int32, (rows, LANES), 0)
    return jnp.where(lane == row // seg, 1.0, 0.0).astype(BF16)


def causal_keep(size, seg):
    key = lax.broadcasted_iota(jnp.int32, (size, size), 0)
    query = lax.broadcasted_iota(jnp.int32, (size, size), 1)
    return (key // seg != query // seg) | (key <= query)


def flip(a):
    return a.astype(F32).T.astype(a.dtype)


def fold_forward(state, queries, key_tile, value_tile, bias_tile, heads, keep):
    out = []
    for h in range(heads):
        g, half = divmod(h, 2)
        lanes = slice(g * LANES, (g + 1) * LANES)
        if half == 0:
            value_rows = flip(value_tile[:, lanes])
        keys = jnp.where(head_lanes(TILE, half), key_tile[:, lanes], bias_tile)
        scores = nt(keys, queries[h])
        if keep is not None:
            scores = jnp.where(keep, scores, NEG)
        peak, total, mix = state[3 * h : 3 * h + 3]
        new_peak = jnp.maximum(peak, jnp.max(scores, axis=0, keepdims=True))
        weights = jnp.exp(scores - new_peak)
        shrink = jnp.exp(peak - new_peak)
        total = total * shrink + jnp.sum(weights, axis=0, keepdims=True)
        mix = mix * shrink + nn(
            value_rows[half * HEAD_DIM : (half + 1) * HEAD_DIM], weights.astype(BF16)
        )
        out += [new_peak, total, mix]
    return tuple(out)


def fresh_state(heads, rows):
    state = []
    for _ in range(heads):
        state += [
            jnp.full((1, rows), NEG, F32),
            jnp.zeros((1, rows), F32),
            jnp.zeros((HEAD_DIM, rows), F32),
        ]
    return tuple(state)


def flagged_queries(q, heads, seg):
    rows = q.shape[0]
    flags = flags_of(rows, seg)
    return [
        jnp.where(
            head_lanes(rows, h % 2), q[:, (h // 2) * LANES : (h // 2 + 1) * LANES], flags
        )
        for h in range(heads)
    ]


def put_mix(state, heads, groups, mix_ref, log_ref):
    rows = mix_ref.shape[0]
    for g in range(groups):
        parts = []
        for h in (2 * g, 2 * g + 1):
            if h < heads:
                parts.append(state[3 * h + 2] / state[3 * h + 1])
            else:
                parts.append(jnp.zeros((HEAD_DIM, rows), F32))
        mix_ref[:, g * LANES : (g + 1) * LANES] = jnp.concatenate(parts, axis=0).T.astype(BF16)
    for h in range(heads):
        log_ref[h : h + 1, :] = state[3 * h] + jnp.log(state[3 * h + 1])


def self_forward_kernel(
    count_ref, q_ref, k_ref, v_ref, trunk_ref, bias_ref, mix_ref, log_ref, *, heads, seg
):
    groups = (heads + 1) // 2
    width = groups * LANES
    queries = flagged_queries(q_ref[...], heads, seg)
    prefix = bias_ref.shape[1] - TILE
    state = fold_forward(
        fresh_state(heads, TILE),
        queries,
        k_ref[...],
        v_ref[...],
        bias_ref[0, prefix:, :],
        heads,
        causal_keep(TILE, seg),
    )

    def body(c, state):
        rows = pl.ds(pl.multiple_of(c * TILE, TILE), TILE)
        return fold_forward(
            state,
            queries,
            trunk_ref[rows, :width],
            trunk_ref[rows, width:],
            bias_ref[0, rows, :],
            heads,
            None,
        )

    state = lax.fori_loop(0, count_ref[pl.program_id(0)], body, state)
    log_ref[...] = jnp.zeros_like(log_ref)
    put_mix(state, heads, groups, mix_ref, log_ref)


def self_forward(counts, qkv, trunk, bias, heads, seg):
    rows = qkv.shape[0]
    width = qkv.shape[1] // 3
    blocks = rows // TILE
    keys = bias.shape[1]
    return pl.pallas_call(
        functools.partial(self_forward_kernel, heads=heads, seg=seg),
        grid_spec=pltpu.PrefetchScalarGridSpec(
            num_scalar_prefetch=1,
            grid=(blocks,),
            in_specs=[
                pl.BlockSpec((TILE, width), lambda b, n: (b, 0)),
                pl.BlockSpec((TILE, width), lambda b, n: (b, 1)),
                pl.BlockSpec((TILE, width), lambda b, n: (b, 2)),
                pl.BlockSpec(trunk.shape, lambda b, n: (0, 0)),
                pl.BlockSpec((1, keys, LANES), lambda b, n: (b, 0, 0)),
            ],
            out_specs=[
                pl.BlockSpec((TILE, width), lambda b, n: (b, 0)),
                pl.BlockSpec((8, TILE), lambda b, n: (0, b)),
            ],
        ),
        out_shape=[
            jax.ShapeDtypeStruct((rows, width), BF16),
            jax.ShapeDtypeStruct((8, rows), F32),
        ],
        compiler_params=pltpu.CompilerParams(vmem_limit_bytes=VMEM_LIMIT),
        cost_estimate=pl.CostEstimate(
            flops=rows * keys * heads * HEAD_DIM * 16,
            bytes_accessed=rows * width * 12 + trunk.size * 2,
            transcendentals=rows * keys * heads,
        ),
    )(counts, qkv, qkv, qkv, trunk, bias)


def fold_backward(
    queries, plain, grads, logs, deltas, key_tile, value_tile, bias_tile, heads, keep
):
    grad_keys, grad_values, grad_queries = [], [], []
    for h in range(heads):
        g, half = divmod(h, 2)
        lanes = slice(g * LANES, (g + 1) * LANES)
        if half == 0:
            key_rows = flip(key_tile[:, lanes])
        keys = jnp.where(head_lanes(TILE, half), key_tile[:, lanes], bias_tile)
        scores = nt(keys, queries[h])
        if keep is not None:
            scores = jnp.where(keep, scores, NEG)
        probs = jnp.exp(scores - logs[h])
        grad_probs = nt(value_tile[:, lanes], grads[h])
        grad_scores = (probs * (grad_probs - deltas[h])).astype(BF16)
        part_values = nn(probs.astype(BF16), grads[h])
        part_keys = nn(grad_scores, plain[h])
        if half == 0:
            grad_values.append(part_values)
            grad_keys.append(part_keys)
        else:
            grad_values[g] = grad_values[g] + part_values
            grad_keys[g] = grad_keys[g] + part_keys
        grad_queries.append(
            nn(key_rows[half * HEAD_DIM : (half + 1) * HEAD_DIM], grad_scores)
        )
    return grad_keys, grad_values, tuple(grad_queries)


def backward_sides(q, grad, mix, heads, seg):
    rows = q.shape[0]
    queries = flagged_queries(q, heads, seg)
    plain, grads, deltas = [], [], []
    for h in range(heads):
        g, half = divmod(h, 2)
        lanes = slice(g * LANES, (g + 1) * LANES)
        mask = head_lanes(rows, half)
        plain.append(jnp.where(mask, q[:, lanes], jnp.zeros((), BF16)))
        grads.append(jnp.where(mask, grad[:, lanes], jnp.zeros((), BF16)))
        if half == 0:
            product = (grad[:, lanes].astype(F32) * mix[:, lanes].astype(F32)).T
        deltas.append(
            jnp.sum(product[half * HEAD_DIM : (half + 1) * HEAD_DIM], axis=0, keepdims=True)
        )
    return queries, plain, grads, deltas


def put_queries(grad_queries, heads, groups, scale, dq_ref):
    rows = dq_ref.shape[0]
    for g in range(groups):
        parts = [
            grad_queries[h] if h < heads else jnp.zeros((HEAD_DIM, rows), F32)
            for h in (2 * g, 2 * g + 1)
        ]
        dq_ref[:, g * LANES : (g + 1) * LANES] = (
            jnp.concatenate(parts, axis=0).T * scale
        ).astype(BF16)


def self_backward_kernel(
    count_ref,
    q_ref,
    k_ref,
    v_ref,
    trunk_ref,
    bias_ref,
    grad_ref,
    mix_ref,
    log_ref,
    dq_ref,
    dk_ref,
    dv_ref,
    dtrunk_ref,
    *,
    heads,
    seg,
    scale,
):
    groups = (heads + 1) // 2
    width = groups * LANES
    prefix = bias_ref.shape[1] - TILE
    queries, plain, grads, deltas = backward_sides(
        q_ref[...], grad_ref[...], mix_ref[...], heads, seg
    )
    logs = [log_ref[h : h + 1, :] for h in range(heads)]

    @pl.when(pl.program_id(0) == 0)
    def _():
        dtrunk_ref[...] = jnp.zeros_like(dtrunk_ref)

    grad_keys, grad_values, grad_queries = fold_backward(
        queries,
        plain,
        grads,
        logs,
        deltas,
        k_ref[...],
        v_ref[...],
        bias_ref[0, prefix:, :],
        heads,
        causal_keep(TILE, seg),
    )
    for g in range(groups):
        lanes = slice(g * LANES, (g + 1) * LANES)
        dk_ref[:, lanes] = grad_keys[g]
        dv_ref[:, lanes] = grad_values[g]

    def body(c, grad_queries):
        rows = pl.ds(pl.multiple_of(c * TILE, TILE), TILE)
        grad_keys, grad_values, more = fold_backward(
            queries,
            plain,
            grads,
            logs,
            deltas,
            trunk_ref[rows, :width],
            trunk_ref[rows, width:],
            bias_ref[0, rows, :],
            heads,
            None,
        )
        for g in range(groups):
            lanes = slice(g * LANES, (g + 1) * LANES)
            late = slice(width + g * LANES, width + (g + 1) * LANES)
            dtrunk_ref[rows, lanes] += grad_keys[g]
            dtrunk_ref[rows, late] += grad_values[g]
        return tuple(a + b for a, b in zip(grad_queries, more))

    grad_queries = lax.fori_loop(0, count_ref[pl.program_id(0)], body, grad_queries)
    put_queries(grad_queries, heads, groups, scale, dq_ref)


def self_backward(counts, qkv, trunk, bias, grad, mix, logs, heads, seg, scale):
    rows = qkv.shape[0]
    width = qkv.shape[1] // 3
    blocks = rows // TILE
    keys = bias.shape[1]
    tile = pl.BlockSpec((TILE, width), lambda b, n: (b, 0))
    return pl.pallas_call(
        functools.partial(self_backward_kernel, heads=heads, seg=seg, scale=scale),
        grid_spec=pltpu.PrefetchScalarGridSpec(
            num_scalar_prefetch=1,
            grid=(blocks,),
            in_specs=[
                tile,
                pl.BlockSpec((TILE, width), lambda b, n: (b, 1)),
                pl.BlockSpec((TILE, width), lambda b, n: (b, 2)),
                pl.BlockSpec(trunk.shape, lambda b, n: (0, 0)),
                pl.BlockSpec((1, keys, LANES), lambda b, n: (b, 0, 0)),
                tile,
                tile,
                pl.BlockSpec((8, TILE), lambda b, n: (0, b)),
            ],
            out_specs=[tile, tile, tile, pl.BlockSpec(trunk.shape, lambda b, n: (0, 0))],
        ),
        out_shape=[
            jax.ShapeDtypeStruct((rows, width), BF16),
            jax.ShapeDtypeStruct((rows, width), F32),
            jax.ShapeDtypeStruct((rows, width), F32),
            jax.ShapeDtypeStruct(trunk.shape, F32),
        ],
        compiler_params=pltpu.CompilerParams(vmem_limit_bytes=VMEM_LIMIT),
        cost_estimate=pl.CostEstimate(
            flops=rows * keys * heads * HEAD_DIM * 40,
            bytes_accessed=rows * width * 24 + trunk.size * 6,
            transcendentals=rows * keys * heads,
        ),
    )(counts, qkv, qkv, qkv, trunk, bias, grad, mix, logs)


def cross_forward_kernel(q_ref, k_ref, v_ref, bias_ref, mix_ref, log_ref):
    rows = q_ref.shape[0]
    queries = flagged_queries(q_ref[...], 2, rows)
    state = fresh_state(2, rows)
    for c in range(k_ref.shape[0] // TILE):
        part = slice(c * TILE, (c + 1) * TILE)
        state = fold_forward(
            state, queries, k_ref[part, :], v_ref[part, :], bias_ref[part, :], 2, None
        )
    log_ref[...] = jnp.zeros_like(log_ref)
    put_mix(state, 2, 1, mix_ref, log_ref)


def cross_forward(q, k, v, bias):
    rows, width = q.shape
    keys = k.shape[0]
    groups = width // LANES
    part = pl.BlockSpec((rows, LANES), lambda g: (0, g))
    side = pl.BlockSpec((keys, LANES), lambda g: (0, g))
    return pl.pallas_call(
        cross_forward_kernel,
        grid=(groups,),
        in_specs=[part, side, side, pl.BlockSpec((keys, LANES), lambda g: (0, 0))],
        out_specs=[part, pl.BlockSpec((8, rows), lambda g: (g, 0))],
        out_shape=[
            jax.ShapeDtypeStruct((rows, width), BF16),
            jax.ShapeDtypeStruct((8 * groups, rows), F32),
        ],
        compiler_params=pltpu.CompilerParams(vmem_limit_bytes=VMEM_LIMIT),
        cost_estimate=pl.CostEstimate(
            flops=rows * keys * width * 16,
            bytes_accessed=rows * width * 4 + keys * width * 4,
            transcendentals=rows * keys * groups * 2,
        ),
    )(q, k, v, bias)


def cross_backward_kernel(
    q_ref, k_ref, v_ref, bias_ref, grad_ref, mix_ref, log_ref, dq_ref, dk_ref, dv_ref, *, scale
):
    rows = q_ref.shape[0]
    queries, plain, grads, deltas = backward_sides(
        q_ref[...], grad_ref[...], mix_ref[...], 2, rows
    )
    logs = [log_ref[h : h + 1, :] for h in range(2)]
    total = (jnp.zeros((HEAD_DIM, rows), F32),) * 2
    for c in range(k_ref.shape[0] // TILE):
        part = slice(c * TILE, (c + 1) * TILE)
        grad_keys, grad_values, more = fold_backward(
            queries,
            plain,
            grads,
            logs,
            deltas,
            k_ref[part, :],
            v_ref[part, :],
            bias_ref[part, :],
            2,
            None,
        )
        dk_ref[part, :] = grad_keys[0].astype(BF16)
        dv_ref[part, :] = grad_values[0].astype(BF16)
        total = tuple(a + b for a, b in zip(total, more))
    put_queries(total, 2, 1, scale, dq_ref)


def cross_backward(q, k, v, bias, grad, mix, logs, scale):
    rows, width = q.shape
    keys = k.shape[0]
    groups = width // LANES
    part = pl.BlockSpec((rows, LANES), lambda g: (0, g))
    side = pl.BlockSpec((keys, LANES), lambda g: (0, g))
    return pl.pallas_call(
        functools.partial(cross_backward_kernel, scale=scale),
        grid=(groups,),
        in_specs=[
            part,
            side,
            side,
            pl.BlockSpec((keys, LANES), lambda g: (0, 0)),
            part,
            part,
            pl.BlockSpec((8, rows), lambda g: (g, 0)),
        ],
        out_specs=[part, side, side],
        out_shape=[
            jax.ShapeDtypeStruct((rows, width), BF16),
            jax.ShapeDtypeStruct((keys, width), BF16),
            jax.ShapeDtypeStruct((keys, width), BF16),
        ],
        compiler_params=pltpu.CompilerParams(vmem_limit_bytes=VMEM_LIMIT),
        cost_estimate=pl.CostEstimate(
            flops=rows * keys * width * 40,
            bytes_accessed=rows * width * 8 + keys * width * 8,
            transcendentals=rows * keys * groups * 2,
        ),
    )(q, k, v, bias, grad, mix, logs)


def gelu_exact(values):
    return jax.nn.gelu(values, approximate=False)


def norm_parts(values):
    center = values - jnp.mean(values, axis=-1, keepdims=True)
    inverse = lax.rsqrt(jnp.mean(center * center, axis=-1, keepdims=True) + EPS)
    return center * inverse, inverse


def layer_norm(values, gain, shift):
    return norm_parts(values)[0] * gain + shift


def norm_back(pre_sum, gain, grad_out):
    normed, inverse = norm_parts(pre_sum)
    grad_normed = grad_out * gain
    grad_pre = inverse * (
        grad_normed
        - jnp.mean(grad_normed, axis=-1, keepdims=True)
        - normed * jnp.mean(grad_normed * normed, axis=-1, keepdims=True)
    )
    return grad_pre, jnp.sum(grad_out * normed, axis=0), jnp.sum(grad_out, axis=0)


def closure_of(parent_row):
    count = parent_row.shape[0]
    labels = jnp.arange(count, dtype=jnp.int32)
    closure = (parent_row[:, None] == labels[None, :]).astype(F32)
    for _ in range(max(1, count.bit_length())):
        closure = jnp.minimum(closure + nn(closure, closure), 1.0)
    return closure


def pick(a, index, dim):
    return lax.dynamic_index_in_dim(a, index, dim, keepdims=False)


def local(sizes, *args):
    (
        layer_input,
        encoder_out,
        enc_length,
        parent_ids,
        token_segment,
        self_query,
        self_key,
        self_value,
        self_output,
        cross_query,
        cross_key,
        cross_value,
        cross_output,
        ffn_up,
        ffn_down,
        self_qbias,
        self_vbias,
        self_obias,
        cross_qbias,
        cross_vbias,
        cross_obias,
        ffn_upbias,
        ffn_downbias,
        norm1_gain,
        norm1_shift,
        norm2_gain,
        norm2_shift,
        norm3_gain,
        norm3_shift,
        out_grad,
    ) = args
    place = {axis: lax.axis_index(axis) for axis in sizes}
    shards, ctxs, tensors = sizes["shard"], sizes["ctx"], sizes["tensor"]
    me_ctx, me_tensor = place["ctx"], place["tensor"]
    scale = HEAD_DIM ** (-0.5)

    def bits_of(axis):
        return [1 << k for k in reversed(range(sizes[axis].bit_length() - 1))]

    def swap(a, axis, bit):
        return lax.ppermute(a, axis, [(i, i ^ bit) for i in range(sizes[axis])])

    def is_high(axis, bit):
        return (place[axis] & bit) != 0

    def grow(a, axis, bit, dim):
        other = swap(a, axis, bit)
        high = is_high(axis, bit)
        return jnp.concatenate([jnp.where(high, other, a), jnp.where(high, a, other)], axis=dim)

    row_dims = [("shard", bit) for bit in bits_of("shard")] + [
        ("ctx", bit) for bit in bits_of("ctx")
    ]
    outer = [d for d in row_dims if d != ("shard", 1)]
    shard_outer = [d for d in outer if d[0] == "shard"]
    ctx_dims = [d for d in outer if d[0] == "ctx"]
    ctx_first = ctx_dims + shard_outer
    shard_first = shard_outer + ctx_dims

    def climb(a, order, dims):
        rows, width = a.shape
        a = a.reshape((1,) * len(dims) + (rows, width))
        for axis, bit in order:
            a = grow(a, axis, bit, dims.index((axis, bit)))
        return a.reshape(-1, width)

    def spread(pieces, order):
        packed = jnp.concatenate(pieces, axis=1)
        share = packed.shape[0] // ctxs
        mine = lax.dynamic_slice_in_dim(packed, me_ctx * share, share, 0)
        parts = [mine] + [swap(mine, "tensor", j) for j in range(1, tensors)]
        columns, start = [], 0
        for piece in pieces:
            columns += [part[:, start : start + piece.shape[1]] for part in parts]
            start += piece.shape[1]
        whole = climb(jnp.concatenate(columns, axis=1), order + [("shard", 1)], row_dims)
        out, start = [], 0
        for piece in pieces:
            out.append(whole[:, start : start + tensors * piece.shape[1]])
            start += tensors * piece.shape[1]
        return out

    def reduce_rows(sides, order):
        core = place["shard"] & 1
        kept, sent = [], []
        for left, right in sides:
            left = left.reshape(left.shape[0], shards // 2, 2, -1)
            near = pick(left, core, 2).reshape(left.shape[0], -1)
            away = pick(left, 1 - core, 2).reshape(left.shape[0], -1)
            sent.append(tn(away, right).astype(BF16))
            kept.append(tn(near, right))
        arrived = swap(jnp.concatenate(sent, axis=1), "shard", 1)
        total = (jnp.concatenate(kept, axis=1) + arrived.astype(F32)).astype(BF16)
        dims = list(outer)
        width = total.shape[1]
        total = total.reshape((2,) * len(dims) + (-1, width))
        for axis, bit in reversed(order):
            dim = dims.index((axis, bit))
            at = is_high(axis, bit).astype(jnp.int32)
            arrived = swap(pick(total, 1 - at, dim), axis, bit)
            total = (pick(total, at, dim).astype(F32) + arrived.astype(F32)).astype(BF16)
            del dims[dim]
        return total

    def finish_rows(total, widths):
        whole = climb(total.astype(BF16), ctx_dims, ctx_dims).astype(F32)
        out, start = [], 0
        for width in widths:
            out.append(whole[:, start : start + width])
            start += width
        return out

    def collect(sides, order):
        total = reduce_rows(sides, order)
        widths = [right.shape[1] // tensors for _, right in sides]

        def block(j):
            parts, start = [], 0
            for width in widths:
                parts.append(total[:, start + j * width : start + (j + 1) * width])
                start += tensors * width
            return jnp.concatenate(parts, axis=1)

        mine = block(0).astype(F32)
        for j in range(1, tensors):
            mine = mine + swap(block(j), "tensor", j).astype(F32)
        return finish_rows(mine, widths)

    def spread_vector(vector):
        return jnp.concatenate(
            [vector] + [swap(vector, "tensor", j) for j in range(1, tensors)], axis=0
        )

    def by_tensor(parts):
        stacked = jnp.stack(parts)
        return jnp.concatenate([pick(stacked, me_tensor ^ i, 0) for i in range(tensors)], axis=0)

    def gather_rows(rows):
        return by_tensor([rows] + [swap(rows, "tensor", j) for j in range(1, tensors)])

    local_rows, model_width = layer_input.shape[1:]
    head_columns = self_query.shape[1]
    heads = head_columns // HEAD_DIM
    padded = -(-head_columns // LANES) * LANES
    pad = padded - head_columns
    quarter = local_rows // tensors
    seg_count = parent_ids.shape[1]
    seg = token_segment.shape[1] // seg_count
    blocks = local_rows // TILE

    qkv_piece = jnp.concatenate([self_query, self_key, self_value], axis=1)
    shard_dims = [("shard", bit) for bit in bits_of("shard")]
    qkv_weights = climb(qkv_piece, shard_dims, shard_dims)
    zeros = jnp.zeros((model_width, pad), BF16)
    qkv_weights = jnp.concatenate(
        [
            part
            for i in range(3)
            for part in (qkv_weights[:, i * head_columns : (i + 1) * head_columns], zeros)
        ],
        axis=1,
    )
    enc_low = climb(encoder_out[0].astype(BF16), ctx_dims, ctx_dims)
    weight_ck, weight_cv = spread([cross_key, cross_value], shard_first)
    weight_o, weight_cq = spread([self_output.T, cross_query], ctx_first)
    weight_co, weight_up = spread([cross_output.T, ffn_up], shard_first)
    (weight_down,) = spread([ffn_down.T], ctx_first)
    bias_all = spread_vector(jnp.concatenate([cross_qbias, cross_vbias, ffn_upbias]))
    bias_all = bias_all.reshape(tensors, -1)
    cq_bias = bias_all[:, :head_columns].reshape(-1)
    cv_bias = bias_all[:, head_columns : 2 * head_columns].reshape(-1)
    up_bias = bias_all[:, 2 * head_columns :].reshape(-1)

    block_label = token_segment[0].reshape(seg_count, seg)[:, 0]
    closure = closure_of(parent_ids[0])
    hot = (block_label[:, None] == jnp.arange(seg_count)[None, :]).astype(F32)
    ancestor = nt(nn(hot, closure), hot) > 0.5
    seg_bias = jnp.where(ancestor, 0.0, NEG)
    own_segs = local_rows // seg
    mine = lax.dynamic_slice_in_dim(seg_bias, me_ctx * own_segs, own_segs, 0)
    own = lax.dynamic_slice_in_dim(mine, me_ctx * own_segs, own_segs, 1)
    own = jnp.where(jnp.eye(own_segs, dtype=bool), 0.0, own)
    per = TILE // seg
    own = jnp.stack([own[b * per : (b + 1) * per, b * per : (b + 1) * per] for b in range(blocks)])
    trunk_bias = mine[:, :own_segs].reshape(blocks, per, own_segs)
    seg_rows = jnp.swapaxes(jnp.concatenate([trunk_bias, own], axis=2), 1, 2)
    seg_rows = jnp.pad(seg_rows, ((0, 0), (0, 0), (0, HEAD_DIM - per))).astype(BF16)
    seg_rows = jnp.concatenate([seg_rows, seg_rows], axis=2)
    self_bias = jnp.repeat(seg_rows, seg, axis=1)
    counts = jnp.where(me_ctx == 0, jnp.arange(blocks, dtype=jnp.int32), blocks).astype(jnp.int32)
    enc_total = enc_low.shape[0]
    lane = jnp.arange(LANES) % HEAD_DIM
    cross_bias = jnp.where(
        (jnp.arange(enc_total)[:, None] >= enc_length[0]) & (lane[None, :] == 0), NEG, 0.0
    ).astype(BF16)

    input_low = layer_input[0].astype(BF16)
    gap = jnp.zeros((pad,), F32)
    none = jnp.zeros((padded,), F32)
    qkv_bias = jnp.concatenate([self_qbias, gap, none, self_vbias, gap])
    qkv_scale = jnp.concatenate([none + scale, none + 1.0, none + 1.0])
    qkv = ((nn(input_low, qkv_weights) + qkv_bias) * qkv_scale).astype(BF16)
    own_kv = qkv[:, padded:]
    sent_kv = lax.ppermute(own_kv, "ctx", [(0, 1)])
    trunk = jnp.where(me_ctx == 0, own_kv, sent_kv)
    mix, self_logs = self_forward(counts, qkv, trunk, self_bias, heads, seg)

    def row_part(a, index):
        return lax.dynamic_slice_in_dim(a, index * quarter, quarter, 0)

    def to_rows(a):
        parts = [row_part(a, me_tensor)] + [
            swap(row_part(a, me_tensor ^ j), "tensor", j) for j in range(1, tensors)
        ]
        return jnp.concatenate(parts, axis=1)

    def to_heads(a):
        width = a.shape[1] // tensors
        parts = [a[:, j * width : (j + 1) * width] for j in range(tensors)]
        return by_tensor(parts[:1] + [swap(parts[j], "tensor", j) for j in range(1, tensors)])

    mix_rows = to_rows(mix[:, :head_columns])
    sum_one = row_part(layer_input[0], me_tensor) + nt(mix_rows, weight_o) + self_obias
    hidden_one = layer_norm(sum_one, norm1_gain, norm1_shift)
    one_low = hidden_one.astype(BF16)

    cq = ((nn(one_low, weight_cq) + cq_bias) * scale).astype(BF16)
    ck = nn(enc_low, weight_ck).astype(BF16)
    cv = (nn(enc_low, weight_cv) + cv_bias).astype(BF16)
    cross_mix, cross_logs = cross_forward(cq, ck, cv, cross_bias)
    sum_two = hidden_one + nt(cross_mix, weight_co) + cross_obias
    hidden_two = layer_norm(sum_two, norm2_gain, norm2_shift)
    two_low = hidden_two.astype(BF16)

    pre = nn(two_low, weight_up) + up_bias
    act = gelu_exact(pre).astype(BF16)
    sum_three = hidden_two + nt(act, weight_down) + ffn_downbias
    result = layer_norm(sum_three, norm3_gain, norm3_shift)
    result_all = gather_rows(result.astype(BF16)).astype(F32)

    grad_three, gain3, shift3 = norm_back(sum_three, norm3_gain, row_part(out_grad[0], me_tensor))
    downbias = jnp.sum(grad_three, axis=0)
    three_low = grad_three.astype(BF16)
    (grad_down,) = collect([(three_low, act)], ctx_first)
    grad_act = nn(three_low, weight_down)
    grad_pre = jax.vjp(gelu_exact, pre)[1](grad_act)[0]
    upbias = jnp.sum(grad_pre, axis=0)
    pre_low = grad_pre.astype(BF16)
    (grad_up,) = collect([(two_low, pre_low)], shard_first)
    grad_hidden_two = grad_three + nt(pre_low, weight_up)

    grad_two, gain2, shift2 = norm_back(sum_two, norm2_gain, grad_hidden_two)
    cobias = jnp.sum(grad_two, axis=0)
    two_grad_low = grad_two.astype(BF16)
    grad_cmix = nn(two_grad_low, weight_co).astype(BF16)
    dcq, dck, dcv = cross_backward(cq, ck, cv, cross_bias, grad_cmix, cross_mix, cross_logs, scale)
    cqbias = jnp.sum(dcq.astype(F32), axis=0)
    cvbias = jnp.sum(dcv.astype(F32), axis=0)
    grad_co, grad_cq, grad_ck, grad_cv = collect(
        [(two_grad_low, cross_mix), (one_low, dcq), (enc_low, dck), (enc_low, dcv)], ctx_first
    )
    enc_part = nt(dck, weight_ck) + nt(dcv, weight_cv)
    enc_half = enc_part.reshape(ctxs, -1, model_width)
    arrived = swap(pick(enc_half, 1 - me_ctx, 0).astype(BF16), "ctx", 1)
    enc_half = (pick(enc_half, me_ctx, 0) + arrived.astype(F32)).astype(BF16)
    enc_share = enc_half.shape[0] // tensors
    enc_mine = lax.dynamic_slice_in_dim(enc_half, me_tensor * enc_share, enc_share, 0).astype(F32)
    for j in range(1, tensors):
        away = lax.dynamic_slice_in_dim(enc_half, (me_tensor ^ j) * enc_share, enc_share, 0)
        enc_mine = enc_mine + swap(away, "tensor", j).astype(F32)
    grad_encoder = gather_rows(enc_mine.astype(BF16)).astype(F32)
    grad_hidden_one = grad_two + nt(dcq, weight_cq)

    grad_one, gain1, shift1 = norm_back(sum_one, norm1_gain, grad_hidden_one)
    obias = jnp.sum(grad_one, axis=0)
    one_grad_low = grad_one.astype(BF16)
    grad_smix = to_heads(nn(one_grad_low, weight_o).astype(BF16))
    grad_smix = jnp.pad(grad_smix, ((0, 0), (0, pad)))
    (grad_o,) = collect([(one_grad_low, mix_rows)], shard_first)
    dq, dk, dv, dtrunk = self_backward(
        counts, qkv, trunk, self_bias, grad_smix, mix, self_logs, heads, seg, scale
    )
    arrived = lax.ppermute(dtrunk.astype(BF16), "ctx", [(1, 0)]).astype(F32)
    dkv = jnp.concatenate([dk, dv], axis=1) + jnp.where(me_ctx == 0, dtrunk + arrived, 0.0)
    dqkv = jnp.concatenate([dq, dkv.astype(BF16)], axis=1)
    part = nt(dqkv, qkv_weights)
    part_low = part.astype(BF16)
    input_mine = grad_one + row_part(part, me_tensor)
    for j in range(1, tensors):
        input_mine = input_mine + swap(row_part(part_low, me_tensor ^ j), "tensor", j).astype(F32)
    grad_input = gather_rows(input_mine.astype(BF16)).astype(F32)
    packed = jnp.concatenate(
        [dqkv[:, i * padded : i * padded + head_columns] for i in range(3)], axis=1
    )
    grad_q, grad_k, grad_v = finish_rows(
        reduce_rows([(input_low, packed)], ctx_first), [head_columns] * 3
    )
    qkv_sums = jnp.sum(packed.astype(F32), axis=0)

    every = jnp.concatenate(
        [obias, cobias, downbias, gain1, shift1, gain2, shift2, gain3, shift3]
    )
    rel = jnp.concatenate(
        [cqbias.reshape(tensors, -1), cvbias.reshape(tensors, -1), upbias.reshape(tensors, -1)],
        axis=1,
    )
    sums = jnp.concatenate([every, rel[0]])
    for j in range(1, tensors):
        sums = sums + swap(jnp.concatenate([every, rel[j]]), "tensor", j)
    sums = jnp.concatenate([sums, qkv_sums])
    for axis, bit in row_dims:
        sums = sums + swap(sums, axis, bit)

    def cut(index):
        return sums[index * model_width : (index + 1) * model_width]

    tail = sums[9 * model_width :]
    sizes_tail = [head_columns, head_columns, ffn_upbias.shape[0]] + [head_columns] * 3
    tails, start = [], 0
    for size in sizes_tail:
        tails.append(tail[start : start + size])
        start += size
    cq_sum, cv_sum, up_sum, q_sum, _, v_sum = tails

    return (
        result_all[None],
        grad_input[None],
        grad_encoder[None],
        grad_q,
        grad_k,
        grad_v,
        grad_o.T,
        grad_cq,
        grad_ck,
        grad_cv,
        grad_co.T,
        grad_up,
        grad_down.T,
        q_sum,
        v_sum,
        cut(0),
        cq_sum,
        cv_sum,
        cut(1),
        up_sum,
        cut(2),
        cut(3),
        cut(4),
        cut(5),
        cut(6),
        cut(7),
        cut(8),
    )


def solution(mesh):
    sizes = {axis: mesh.shape[axis] for axis in ("shard", "ctx", "tensor")}
    rows = P("shard", "ctx", None)
    tall, wide = P("shard", "tensor"), P("tensor", "shard")
    mats = (tall, tall, tall, wide, tall, tall, tall, wide, tall, wide)
    part = P("tensor")
    vectors = (part, part, P(), part, part, P(), part) + (P(),) * 7
    tree = P("shard", None)
    return jax.shard_map(
        functools.partial(local, sizes),
        mesh=mesh,
        in_specs=(rows, rows, P("shard"), tree, tree) + mats + vectors + (rows,),
        out_specs=(rows, rows, rows) + mats + vectors,
        check_vma=False,
    )
```

```python
import functools

import jax
import jax.numpy as jnp
from jax import lax
from jax.experimental import pallas as pl
from jax.experimental.pallas import tpu as pltpu
from jax.sharding import PartitionSpec as P

HEAD_DIM = 64
LANES = 128
TILE = 256
NEG = -1e30
EPS = 1e-05
F32 = jnp.float32
BF16 = jnp.bfloat16
VMEM_LIMIT = 56 * 1024 * 1024
WEIGHT = 0.01


def dot_of(a, b, a_dim, b_dim):
    return lax.dot_general(a, b, (((a_dim,), (b_dim,)), ((), ())), preferred_element_type=F32)


def nn(a, b):
    return dot_of(a, b, 1, 0)


def nt(a, b):
    return dot_of(a, b, 1, 1)


def tn(a, b):
    return dot_of(a, b, 0, 0)


def head_lanes(rows, half):
    lane = lax.broadcasted_iota(jnp.int32, (rows, LANES), 1)
    return (lane < HEAD_DIM) if half == 0 else (lane >= HEAD_DIM)


def flags_of(rows, seg):
    lane = lax.broadcasted_iota(jnp.int32, (rows, LANES), 1) % HEAD_DIM
    row = lax.broadcasted_iota(jnp.int32, (rows, LANES), 0)
    return jnp.where(lane == row // seg, 1.0, 0.0).astype(BF16)


def causal_keep(size, seg):
    key = lax.broadcasted_iota(jnp.int32, (size, size), 0)
    query = lax.broadcasted_iota(jnp.int32, (size, size), 1)
    return (key // seg != query // seg) | (key <= query)


def flip(a):
    return a.astype(F32).T.astype(a.dtype)


def lane_pad(a):
    gap = -a.shape[1] % LANES
    return jnp.concatenate([a, jnp.zeros((a.shape[0], gap), a.dtype)], axis=1) if gap else a


def fold_forward(state, queries, key_tile, value_tile, bias_tile, heads, keep):
    out = []
    for h in range(heads):
        g, half = divmod(h, 2)
        lanes = slice(g * LANES, (g + 1) * LANES)
        if half == 0:
            value_rows = flip(value_tile[:, lanes])
        keys = jnp.where(head_lanes(TILE, half), key_tile[:, lanes], bias_tile)
        scores = nt(keys, queries[h])
        if keep is not None:
            scores = jnp.where(keep, scores, NEG)
        peak, total, mix = state[3 * h : 3 * h + 3]
        new_peak = jnp.maximum(peak, jnp.max(scores, axis=0, keepdims=True))
        weights = jnp.exp(scores - new_peak)
        shrink = jnp.exp(peak - new_peak)
        total = total * shrink + jnp.sum(weights, axis=0, keepdims=True)
        mix = mix * shrink + nn(
            value_rows[half * HEAD_DIM : (half + 1) * HEAD_DIM], weights.astype(BF16)
        )
        out += [new_peak, total, mix]
    return tuple(out)


def fresh_state(heads, rows):
    state = []
    for _ in range(heads):
        state += [
            jnp.full((1, rows), NEG, F32),
            jnp.zeros((1, rows), F32),
            jnp.zeros((HEAD_DIM, rows), F32),
        ]
    return tuple(state)


def flagged_queries(q, heads, seg):
    rows = q.shape[0]
    flags = flags_of(rows, seg)
    return [
        jnp.where(head_lanes(rows, h % 2), q[:, (h // 2) * LANES : (h // 2 + 1) * LANES], flags)
        for h in range(heads)
    ]


def mixed(state, heads):
    parts = [state[3 * h + 2] / state[3 * h + 1] for h in range(heads)]
    if heads % 2:
        parts.append(jnp.zeros_like(parts[0]))
    return jnp.concatenate(
        [jnp.concatenate(parts[h : h + 2], axis=0).T for h in range(0, len(parts), 2)], axis=1
    ).astype(BF16)


def put_logs(state, heads, log_ref):
    log_ref[...] = jnp.zeros_like(log_ref)
    for h in range(heads):
        log_ref[h : h + 1, :] = state[3 * h] + jnp.log(state[3 * h + 1])


def ancestors(parent_ref, label, count):
    def step(_, carry):
        at, bits = carry
        found = at >= 0
        safe = jnp.maximum(at, 0)
        return jnp.where(found, parent_ref[safe], at), jnp.where(
            found, bits | (jnp.int32(1) << safe), bits
        )

    return lax.fori_loop(0, count, step, (parent_ref[label], jnp.int32(0)))[1]


def seg_terms(bits, labels, same, seg):
    lane = lax.broadcasted_iota(jnp.int32, (TILE, LANES), 1) % HEAD_DIM
    row = lax.broadcasted_iota(jnp.int32, (TILE, LANES), 0) // seg
    out = jnp.zeros((TILE, LANES), F32)
    for i, mask in enumerate(bits):
        for t, label in enumerate(labels):
            if same and i == t:
                continue
            term = jnp.where(((mask >> label) & 1) == 1, 0.0, NEG)
            out = jnp.where((lane == i) & (row == t), term, out)
    return out.astype(BF16)


def unpack_kv(tile):
    half = tile.shape[1] // 2
    return lane_pad(tile[:, :half]), lane_pad(tile[:, half:])


def fill_trunk(info_ref, own_ref, sent_ref, trunk_ref):
    def fill(ref):
        keys, values = unpack_kv(ref[...])
        trunk_ref[:, : keys.shape[1]] = keys
        trunk_ref[:, keys.shape[1] :] = values

    @pl.when((pl.program_id(0) == 0) & (info_ref[1] == 0))
    def _():
        fill(own_ref)

    @pl.when((pl.program_id(0) == 0) & (info_ref[1] != 0))
    def _():
        fill(sent_ref)


def tile_rows(c):
    return pl.ds(pl.multiple_of(c * TILE, TILE), TILE)


def block_masks(info_ref, parent_ref, label_ref, seg, rows):
    b = pl.program_id(0)
    per = TILE // seg
    first = info_ref[1] * rows + b * TILE
    own = [label_ref[first + i * seg] for i in range(per)]
    bits = [ancestors(parent_ref, label, parent_ref.shape[0]) for label in own]

    def terms(c):
        return seg_terms(bits, [label_ref[c * TILE + t * seg] for t in range(per)], False, seg)

    count = jnp.where(info_ref[1] == 0, b, rows // TILE)
    return seg_terms(bits, own, True, seg), terms, count


def put_slot(slot, value, refs):
    for j, ref in enumerate(refs):

        @pl.when(slot == j)
        def _(ref=ref):
            ref[...] = value.astype(ref.dtype)


def take_slot(slot, refs):
    value = refs[0][...]
    for j, ref in enumerate(refs[1:], 1):
        value = jnp.where(slot == j, ref[...], value)
    return value


def self_forward_kernel(
    info_ref, parent_ref, label_ref, q_ref, own_ref, sent_ref, *rest, heads, seg
):
    mix_refs, (log_ref, trunk_ref) = rest[:-2], rest[-2:]
    b = pl.program_id(0)
    fill_trunk(info_ref, own_ref, sent_ref, trunk_ref)
    width = trunk_ref.shape[1] // 2
    queries = flagged_queries(lane_pad(q_ref[...]), heads, seg)
    own_terms, terms, count = block_masks(
        info_ref, parent_ref, label_ref, seg, own_ref.shape[0]
    )
    keys, values = unpack_kv(own_ref[tile_rows(b), :])
    state = fold_forward(
        fresh_state(heads, TILE), queries, keys, values, own_terms, heads, causal_keep(TILE, seg)
    )

    def body(c, state):
        rows = tile_rows(c)
        return fold_forward(
            state,
            queries,
            trunk_ref[rows, :width],
            trunk_ref[rows, width:],
            terms(c),
            heads,
            None,
        )

    state = lax.fori_loop(0, count, body, state)
    put_logs(state, heads, log_ref)
    put_slot(b ^ info_ref[2], mixed(state, heads)[:, : mix_refs[0].shape[1]], mix_refs)


def params():
    return pltpu.CompilerParams(vmem_limit_bytes=VMEM_LIMIT)


def cost(flops, bytes_accessed, transcendentals=0):
    return pl.CostEstimate(
        flops=int(flops * WEIGHT),
        bytes_accessed=int(bytes_accessed * WEIGHT),
        transcendentals=int(transcendentals * WEIGHT),
    )


def whole(shape):
    return pl.BlockSpec(shape, lambda *_: (0,) * len(shape))


def shape_of(shape, dtype):
    return jax.ShapeDtypeStruct(shape, dtype)


def self_forward(scalars, q, own, sent, tensors, heads, seg):
    rows, columns = q.shape
    blocks = rows // TILE
    width = -(-columns // LANES) * LANES
    return pl.pallas_call(
        functools.partial(self_forward_kernel, heads=heads, seg=seg),
        grid_spec=pltpu.PrefetchScalarGridSpec(
            num_scalar_prefetch=3,
            grid=(blocks,),
            in_specs=[
                pl.BlockSpec((TILE, columns), lambda b, *_: (b, 0)),
                whole(own.shape),
                whole(own.shape),
            ],
            out_specs=[whole((TILE, columns))] * tensors
            + [pl.BlockSpec((8, TILE), lambda b, *_: (0, b))],
            scratch_shapes=[pltpu.VMEM((rows, 2 * width), BF16)],
        ),
        out_shape=[shape_of((TILE, columns), BF16)] * tensors + [shape_of((8, rows), F32)],
        compiler_params=params(),
        cost_estimate=cost(rows * rows * columns * 8, rows * columns * 16, rows * rows * heads),
        name="self_forward",
    )(*scalars, q, own, sent)


def fold_backward(
    queries, plain, grads, logs, deltas, key_tile, value_tile, bias_tile, heads, keep
):
    grad_keys, grad_values, grad_queries = [], [], []
    for h in range(heads):
        g, half = divmod(h, 2)
        lanes = slice(g * LANES, (g + 1) * LANES)
        if half == 0:
            key_rows = flip(key_tile[:, lanes])
        keys = jnp.where(head_lanes(TILE, half), key_tile[:, lanes], bias_tile)
        scores = nt(keys, queries[h])
        if keep is not None:
            scores = jnp.where(keep, scores, NEG)
        probs = jnp.exp(scores - logs[h])
        grad_probs = nt(value_tile[:, lanes], grads[h])
        grad_scores = (probs * (grad_probs - deltas[h])).astype(BF16)
        part_values = nn(probs.astype(BF16), grads[h])
        part_keys = nn(grad_scores, plain[h])
        if half == 0:
            grad_values.append(part_values)
            grad_keys.append(part_keys)
        else:
            grad_values[g] = grad_values[g] + part_values
            grad_keys[g] = grad_keys[g] + part_keys
        grad_queries.append(nn(key_rows[half * HEAD_DIM : (half + 1) * HEAD_DIM], grad_scores))
    return grad_keys, grad_values, tuple(grad_queries)


def backward_sides(q, grad, mix, heads, seg):
    rows = q.shape[0]
    queries = flagged_queries(q, heads, seg)
    plain, grads, deltas = [], [], []
    for h in range(heads):
        g, half = divmod(h, 2)
        lanes = slice(g * LANES, (g + 1) * LANES)
        mask = head_lanes(rows, half)
        plain.append(jnp.where(mask, q[:, lanes], jnp.zeros((), BF16)))
        grads.append(jnp.where(mask, grad[:, lanes], jnp.zeros((), BF16)))
        if half == 0:
            product = (grad[:, lanes].astype(F32) * mix[:, lanes].astype(F32)).T
        deltas.append(
            jnp.sum(product[half * HEAD_DIM : (half + 1) * HEAD_DIM], axis=0, keepdims=True)
        )
    return queries, plain, grads, deltas


def query_grads(grad_queries, scale):
    parts = list(grad_queries)
    if len(parts) % 2:
        parts.append(jnp.zeros_like(parts[0]))
    return (
        jnp.concatenate(
            [jnp.concatenate(parts[h : h + 2], axis=0).T for h in range(0, len(parts), 2)], axis=1
        )
        * scale
    ).astype(BF16)


def self_backward_kernel(
    info_ref, parent_ref, label_ref, q_ref, own_ref, sent_ref, *rest, heads, seg, scale, tensors
):
    grad_refs, mix_refs, rest = rest[:tensors], rest[tensors : 2 * tensors], rest[2 * tensors :]
    log_ref, dq_ref, down_ref, dtrunk_ref, sums_ref, trunk_ref, sum_ref, vector_ref = rest
    b = pl.program_id(0)
    slot = b ^ info_ref[2]
    fill_trunk(info_ref, own_ref, sent_ref, trunk_ref)
    width = trunk_ref.shape[1] // 2
    half_columns = own_ref.shape[1] // 2
    queries, plain, grads, deltas = backward_sides(
        lane_pad(q_ref[...]),
        lane_pad(take_slot(slot, grad_refs)),
        lane_pad(take_slot(slot, mix_refs)),
        heads,
        seg,
    )
    logs = [log_ref[h : h + 1, :] for h in range(heads)]
    own_terms, terms, count = block_masks(
        info_ref, parent_ref, label_ref, seg, own_ref.shape[0]
    )

    @pl.when(b == 0)
    def _():
        sum_ref[...] = jnp.zeros_like(sum_ref)
        vector_ref[...] = jnp.zeros_like(vector_ref)

    keys, values = unpack_kv(own_ref[tile_rows(b), :])
    grad_keys, grad_values, grad_queries = fold_backward(
        queries, plain, grads, logs, deltas, keys, values, own_terms, heads, causal_keep(TILE, seg)
    )
    down_ref[:, :half_columns] = jnp.concatenate(grad_keys, axis=1)[:, :half_columns]
    down_ref[:, half_columns:] = jnp.concatenate(grad_values, axis=1)[:, :half_columns]

    def body(c, grad_queries):
        rows = tile_rows(c)
        grad_keys, grad_values, more = fold_backward(
            queries,
            plain,
            grads,
            logs,
            deltas,
            trunk_ref[rows, :width],
            trunk_ref[rows, width:],
            terms(c),
            heads,
            None,
        )
        for g in range(len(grad_keys)):
            sum_ref[rows, g * LANES : (g + 1) * LANES] += grad_keys[g]
            sum_ref[rows, width + g * LANES : width + (g + 1) * LANES] += grad_values[g]
        return tuple(x + y for x, y in zip(grad_queries, more))

    grad_queries = lax.fori_loop(0, count, body, grad_queries)
    dq = query_grads(grad_queries, scale)[:, :half_columns]
    dq_ref[...] = dq
    vector_ref[0:1, :] += jnp.sum(dq.astype(F32), axis=0, keepdims=True)
    vector_ref[1:2, :] += jnp.sum(down_ref[:, half_columns:], axis=0, keepdims=True)

    @pl.when(b == pl.num_programs(0) - 1)
    def _():
        trunk_sum = jnp.sum(sum_ref[:, width : width + half_columns], axis=0, keepdims=True)
        sums_ref[...] = jnp.zeros_like(sums_ref)
        sums_ref[pl.ds(info_ref[2], 1), :half_columns] = vector_ref[0:1, :]
        sums_ref[pl.ds(tensors + info_ref[2], 1), :half_columns] = (
            vector_ref[1:2, :] + trunk_sum
        )
        dtrunk_ref[:, :half_columns] = sum_ref[:, :half_columns].astype(BF16)
        dtrunk_ref[:, half_columns:] = sum_ref[:, width : width + half_columns].astype(BF16)


def self_backward(scalars, q, own, sent, grads, mixes, logs, heads, seg, scale, model_width):
    rows, columns = q.shape
    blocks = rows // TILE
    width = -(-columns // LANES) * LANES
    tensors = len(grads)
    tile = pl.BlockSpec((TILE, columns), lambda b, *_: (b, 0))
    return pl.pallas_call(
        functools.partial(
            self_backward_kernel, heads=heads, seg=seg, scale=scale, tensors=tensors
        ),
        grid_spec=pltpu.PrefetchScalarGridSpec(
            num_scalar_prefetch=3,
            grid=(blocks,),
            in_specs=[tile, whole(own.shape), whole(own.shape)]
            + [whole((TILE, columns))] * (2 * tensors)
            + [pl.BlockSpec((8, TILE), lambda b, *_: (0, b))],
            out_specs=[
                tile,
                pl.BlockSpec((TILE, 2 * columns), lambda b, *_: (b, 0)),
                whole((rows, 2 * columns)),
                whole((2 * tensors, model_width)),
            ],
            scratch_shapes=[
                pltpu.VMEM((rows, 2 * width), BF16),
                pltpu.VMEM((rows, 2 * width), F32),
                pltpu.VMEM((8, columns), F32),
            ],
        ),
        out_shape=[
            shape_of((rows, columns), BF16),
            shape_of((rows, 2 * columns), F32),
            shape_of((rows, 2 * columns), BF16),
            shape_of((2 * tensors, model_width), F32),
        ],
        compiler_params=params(),
        cost_estimate=cost(rows * rows * columns * 20, rows * columns * 40, rows * rows * heads),
        name="self_backward",
    )(*scalars, q, own, sent, *grads, *mixes, logs)


def length_terms(info_ref, length_ref, c, half_rows):
    row = lax.broadcasted_iota(jnp.int32, (TILE, LANES), 0)
    lane = lax.broadcasted_iota(jnp.int32, (TILE, LANES), 1) % HEAD_DIM
    half, start = divmod(c * TILE, half_rows)
    place = row + ((half ^ info_ref[1]) * half_rows + start)
    return jnp.where((place >= length_ref[0]) & (lane == 0), NEG, 0.0).astype(BF16)


def cross_forward_kernel(info_ref, length_ref, q_ref, k_ref, v_ref, mix_ref, log_ref):
    rows, keys = q_ref.shape[0], k_ref.shape[0]
    queries = flagged_queries(q_ref[...], 2, rows)
    state = fresh_state(2, rows)
    for c in range(keys // TILE):
        part = slice(c * TILE, (c + 1) * TILE)
        terms = length_terms(info_ref, length_ref, c, keys // 2)
        state = fold_forward(state, queries, k_ref[part, :], v_ref[part, :], terms, 2, None)
    put_logs(state, 2, log_ref)
    mix_ref[...] = mixed(state, 2)


def cross_specs(rows, keys, groups):
    part = pl.BlockSpec((rows, LANES), lambda g, *_: (0, g))
    return (
        part,
        pl.BlockSpec((keys, LANES), lambda g, *_: (0, g)),
        pl.BlockSpec((keys, LANES), lambda g, *_: (0, groups + g)),
        pl.BlockSpec((8, rows), lambda g, *_: (g, 0)),
    )


def cross_forward(scalars, q, kv):
    rows, width = q.shape
    keys = kv.shape[0]
    groups = width // LANES
    part, key_side, value_side, log_side = cross_specs(rows, keys, groups)
    return pl.pallas_call(
        cross_forward_kernel,
        grid_spec=pltpu.PrefetchScalarGridSpec(
            num_scalar_prefetch=2,
            grid=(groups,),
            in_specs=[part, key_side, value_side],
            out_specs=[part, log_side],
        ),
        out_shape=[shape_of((rows, width), BF16), shape_of((8 * groups, rows), F32)],
        compiler_params=params(),
        cost_estimate=cost(
            rows * keys * width * 8, (rows + keys) * width * 4, rows * keys * groups * 2
        ),
        name="cross_forward",
    )(*scalars, q, kv, kv)


def cross_backward_kernel(
    info_ref,
    length_ref,
    q_ref,
    k_ref,
    v_ref,
    grad_ref,
    mix_ref,
    log_ref,
    dq_ref,
    dk_ref,
    dv_ref,
    *,
    scale,
):
    rows, keys = q_ref.shape[0], k_ref.shape[0]
    queries, plain, grads, deltas = backward_sides(
        q_ref[...], grad_ref[...], mix_ref[...], 2, rows
    )
    logs = [log_ref[h : h + 1, :] for h in range(2)]
    total = (jnp.zeros((HEAD_DIM, rows), F32),) * 2
    for c in range(keys // TILE):
        part = slice(c * TILE, (c + 1) * TILE)
        terms = length_terms(info_ref, length_ref, c, keys // 2)
        grad_keys, grad_values, more = fold_backward(
            queries, plain, grads, logs, deltas, k_ref[part, :], v_ref[part, :], terms, 2, None
        )
        dk_ref[part, :] = grad_keys[0].astype(BF16)
        dv_ref[part, :] = grad_values[0].astype(BF16)
        total = tuple(x + y for x, y in zip(total, more))
    dq_ref[...] = query_grads(total, scale)


def cross_backward(scalars, q, kv, grad, mix, logs, scale):
    rows, width = q.shape
    keys = kv.shape[0]
    groups = width // LANES
    part, key_side, value_side, log_side = cross_specs(rows, keys, groups)
    return pl.pallas_call(
        functools.partial(cross_backward_kernel, scale=scale),
        grid_spec=pltpu.PrefetchScalarGridSpec(
            num_scalar_prefetch=2,
            grid=(groups,),
            in_specs=[part, key_side, value_side, part, part, log_side],
            out_specs=[part, key_side, key_side],
        ),
        out_shape=[
            shape_of((rows, width), BF16),
            shape_of((keys, width), BF16),
            shape_of((keys, width), BF16),
        ],
        compiler_params=params(),
        cost_estimate=cost(
            rows * keys * width * 20, (rows * 4 + keys * 4) * width * 2, rows * keys * groups * 2
        ),
        name="cross_backward",
    )(*scalars, q, kv, kv, grad, mix, logs)


def norm_parts(values):
    center = values - jnp.mean(values, axis=-1, keepdims=True)
    inverse = lax.rsqrt(jnp.mean(center * center, axis=-1, keepdims=True) + EPS)
    return center * inverse, inverse


def norm_back(pre_sum, gain, grad_out):
    normed, inverse = norm_parts(pre_sum)
    grad_normed = grad_out * gain
    grad_pre = inverse * (
        grad_normed
        - jnp.mean(grad_normed, axis=-1, keepdims=True)
        - normed * jnp.mean(grad_normed * normed, axis=-1, keepdims=True)
    )
    return (
        grad_pre,
        jnp.sum(grad_out * normed, axis=0, keepdims=True),
        jnp.sum(grad_out, axis=0, keepdims=True),
    )


def project_kernel(x_ref, w_ref, qb_ref, vb_ref, q_ref, kv_ref, low_ref, *, scale):
    columns = q_ref.shape[1]
    low = x_ref[0].astype(BF16)
    low_ref[...] = low
    out = nn(low, w_ref[...])
    q_ref[...] = ((out[:, :columns] + qb_ref[...]) * scale).astype(BF16)
    kv_ref[:, :columns] = out[:, columns : 2 * columns].astype(BF16)
    kv_ref[:, columns:] = (out[:, 2 * columns :] + vb_ref[...]).astype(BF16)


def project(x, w, qb, vb, scale):
    _, rows, width = x.shape
    columns = qb.shape[1]
    return pl.pallas_call(
        functools.partial(project_kernel, scale=scale),
        grid=(rows // TILE,),
        in_specs=[
            pl.BlockSpec((1, TILE, width), lambda b: (0, b, 0)),
            whole(w.shape),
            whole(qb.shape),
            whole(vb.shape),
        ],
        out_specs=[
            pl.BlockSpec((TILE, columns), lambda b: (b, 0)),
            pl.BlockSpec((TILE, 2 * columns), lambda b: (b, 0)),
            pl.BlockSpec((TILE, width), lambda b: (b, 0)),
        ],
        out_shape=[
            shape_of((rows, columns), BF16),
            shape_of((rows, 2 * columns), BF16),
            shape_of((rows, width), BF16),
        ],
        compiler_params=params(),
        cost_estimate=cost(rows * width * columns * 6, rows * width * 8),
        name="project",
    )(x, w, qb, vb)


def assemble_kernel(info_ref, near_ref, far_ref, ckv_ref, o_ref, cq_ref, bias_ref):
    tensors, _, columns = o_ref.shape
    width = tensors * columns
    rows = near_ref.shape[2] - bias_ref.shape[1]

    def put(ref):
        for z in range(tensors):
            part = slice(z * columns, (z + 1) * columns)
            late = slice(width + z * columns, width + (z + 1) * columns)
            ckv_ref[:, part] = ref[0, z, :rows, :columns]
            ckv_ref[:, late] = ref[0, z, :rows, columns : 2 * columns]
            o_ref[z] = ref[0, z, :rows, 2 * columns : 3 * columns]
            cq_ref[:, part] = ref[0, z, :rows, 3 * columns :]
        bias_ref[...] = ref[0, :, rows:, :]

    other = (pl.program_id(0) & 1) ^ (info_ref[0] & 1)

    @pl.when(other == 0)
    def _():
        put(near_ref)

    @pl.when(other != 0)
    def _():
        put(far_ref)


def assemble(info, near, far, shards, columns, bias_rows):
    _, tensors, rows, packed = near.shape
    rows -= bias_rows
    width = tensors * columns
    height = shards * rows
    side = pl.BlockSpec((1,) + near.shape[1:], lambda s, i: ((s >> 1) ^ (i[0] >> 1), 0, 0, 0))
    bias = (tensors, bias_rows, packed)
    return pl.pallas_call(
        assemble_kernel,
        grid_spec=pltpu.PrefetchScalarGridSpec(
            num_scalar_prefetch=1,
            grid=(shards,),
            in_specs=[side, side],
            out_specs=[
                pl.BlockSpec((rows, 2 * width), lambda s, i: (s, 0)),
                pl.BlockSpec((tensors, rows, columns), lambda s, i: (0, s, 0)),
                pl.BlockSpec((rows, width), lambda s, i: (s, 0)),
                whole(bias),
            ],
        ),
        out_shape=[
            shape_of((height, 2 * width), BF16),
            shape_of((tensors, height, columns), BF16),
            shape_of((height, width), BF16),
            shape_of(bias, BF16),
        ],
        compiler_params=params(),
        cost_estimate=cost(0, near.size * 8),
        name="assemble",
    )(info, near, far)


def bias_part(bias_ref, j, start, columns):
    width = bias_ref.shape[2]
    row, lane = divmod(start, width)
    tall = bias_ref[j].astype(F32)
    full = tall[:2] + tall[2:4]
    if lane + columns <= width:
        return full[row : row + 1, lane : lane + columns]
    return jnp.concatenate(
        [full[row : row + 1, lane:], full[row + 1 : row + 2, : lane + columns - width]], axis=1
    )


def tensor_row(bias_ref, start, columns):
    return jnp.concatenate(
        [bias_part(bias_ref, j, start, columns) for j in range(bias_ref.shape[0])], axis=1
    )


def after_self_kernel(
    info_ref, x_ref, o_ref, cq_ref, ob_ref, gain_ref, shift_ref, bias_ref, *rest, scale
):
    mix_refs, (sum_ref, low_ref, q_ref, joined_ref) = rest[:-4], rest[-4:]
    joined_ref[...] = jnp.concatenate([mix_ref[...] for mix_ref in mix_refs], axis=1)
    total = x_ref[0] + ob_ref[...]
    for j, mix_ref in enumerate(mix_refs):
        total = total + nt(mix_ref[...], o_ref[j])
    sum_ref[...] = total
    hidden = norm_parts(total)[0] * gain_ref[...] + shift_ref[...]
    low = hidden.astype(BF16)
    low_ref[...] = low
    bias = tensor_row(bias_ref, 0, mix_refs[0].shape[1])
    q_ref[...] = ((nn(low, cq_ref[...]) + bias) * scale).astype(BF16)


def after_self(info, x, o, cq, ob, gain, shift, bias, mixes, scale):
    width = x.shape[2]
    rows = mixes[0].shape[0]
    return pl.pallas_call(
        functools.partial(after_self_kernel, scale=scale),
        grid_spec=pltpu.PrefetchScalarGridSpec(
            num_scalar_prefetch=1,
            grid=(1,),
            in_specs=[pl.BlockSpec((1, rows, width), lambda s, i: (0, i[2], 0))]
            + [whole(a.shape) for a in (o, cq, ob, gain, shift, bias) + tuple(mixes)],
            out_specs=[whole((rows, width))] * 4,
        ),
        out_shape=[shape_of((rows, width), F32)] + [shape_of((rows, width), BF16)] * 3,
        compiler_params=params(),
        cost_estimate=cost(rows * width * width * 4, width * width * 4 + rows * width * 12),
        name="after_self",
    )(info, x, o, cq, ob, gain, shift, bias, *mixes)


def encode_kernel(info_ref, own_ref, sent_ref, w_ref, bias_ref, low_ref, kv_ref, *, columns):
    width = low_ref.shape[1]
    half = pl.num_programs(0) // 2

    @pl.when(pl.program_id(0) < half)
    def _():
        low_ref[...] = own_ref[0].astype(BF16)

    @pl.when(pl.program_id(0) >= half)
    def _():
        low_ref[...] = sent_ref[...]

    out = nn(low_ref[...], w_ref[...])
    kv_ref[:, :width] = out[:, :width].astype(BF16)
    kv_ref[:, width:] = (
        out[:, width:] + tensor_row(bias_ref, columns, columns)
    ).astype(BF16)


def encode(info, own, sent, w, bias, columns):
    _, rows, width = own.shape
    half = rows // TILE
    return pl.pallas_call(
        functools.partial(encode_kernel, columns=columns),
        grid_spec=pltpu.PrefetchScalarGridSpec(
            num_scalar_prefetch=1,
            grid=(2 * half,),
            in_specs=[
                pl.BlockSpec((1, TILE, width), lambda b, i: (0, jnp.minimum(b, half - 1), 0)),
                pl.BlockSpec((TILE, width), lambda b, i: (jnp.maximum(b - half, 0), 0)),
                whole(w.shape),
                whole(bias.shape),
            ],
            out_specs=[
                pl.BlockSpec((TILE, width), lambda b, i: (b, 0)),
                pl.BlockSpec((TILE, 2 * width), lambda b, i: (b, 0)),
            ],
        ),
        out_shape=[shape_of((2 * rows, width), BF16), shape_of((2 * rows, 2 * width), BF16)],
        compiler_params=params(),
        cost_estimate=cost(rows * width * width * 8, rows * width * 14),
        name="encode",
    )(info, own, sent, w, bias)


def gelu_parts(values):
    half = 0.5 * (1.0 + lax.erf(values * (0.5**0.5)))
    slope = half + values * (jnp.exp(-0.5 * values * values) * (0.5 / jnp.pi) ** 0.5)
    return values * half, slope


def feed_kernel(
    info_ref,
    sum_ref,
    vectors_ref,
    mix_ref,
    packed_ref,
    bias_ref,
    goal_ref,
    w_ref,
    result_ref,
    dw_ref,
    grad_ref,
    grad_low_ref,
    grad_mix_ref,
    sums_ref,
    two_ref,
    low_ref,
    low_t_ref,
    act_ref,
    slope_ref,
    acc_ref,
    three_low_ref,
    three_t_ref,
    co_ref,
):
    phase, z = pl.program_id(0), pl.program_id(1)
    tensors = pl.num_programs(1)
    rows, width = sum_ref.shape
    hidden_units = w_ref.shape[3]
    piece = width // w_ref.shape[1]
    up = w_ref[0, :, :piece].reshape(width, hidden_units)
    down = w_ref[0, :, piece : 2 * piece].reshape(width, hidden_units)
    gain1, shift1, cob, gain2, shift2, downb, gain3, shift3 = (
        vectors_ref[i : i + 1, :] for i in range(1, 9)
    )

    @pl.when((phase == 0) & (z == 0))
    def _():
        _, shards, chunk, _ = packed_ref.shape
        columns = co_ref.shape[2]
        for t in range(co_ref.shape[0]):
            for s in range(shards):
                for i in range(piece // chunk):
                    start = s * piece + i * chunk
                    co_ref[t, start : start + chunk, :] = packed_ref[
                        t, s, :, i * columns : (i + 1) * columns
                    ]
        hidden_one = norm_parts(sum_ref[...])[0] * gain1 + shift1
        sum_two = hidden_one + cob
        for j in range(co_ref.shape[0]):
            part = mix_ref[:, j * columns : (j + 1) * columns]
            sum_two = sum_two + nt(part, co_ref[info_ref[2] ^ j])
        two_ref[...] = sum_two
        hidden_two = norm_parts(sum_two)[0] * gain2 + shift2
        low_ref[...] = hidden_two.astype(BF16)
        low_t_ref[...] = hidden_two.T.astype(BF16)
        acc_ref[...] = hidden_two + downb
        sums_ref[...] = jnp.zeros_like(sums_ref)

    @pl.when(phase == 0)
    def _():
        bias = bias_part(bias_ref, z ^ info_ref[2], 2 * co_ref.shape[2], hidden_units)
        pre = nn(low_ref[...], up) + bias
        value, slope = gelu_parts(pre)
        act = value.astype(BF16)
        act_ref[z] = act
        slope_ref[z] = slope
        acc_ref[...] += nt(act, down)

    @pl.when((phase == 0) & (z == tensors - 1))
    def _():
        sum_three = acc_ref[...]
        result = norm_parts(sum_three)[0] * gain3 + shift3
        result_ref[...] = result.astype(BF16)
        grad_three, *both = norm_back(sum_three, gain3, goal_ref[0])
        sums_ref[0:1, :] = both[0]
        sums_ref[1:2, :] = both[1]
        sums_ref[2:3, :] = jnp.sum(grad_three, axis=0, keepdims=True)
        acc_ref[...] = grad_three
        three_low_ref[...] = grad_three.astype(BF16)
        three_t_ref[...] = grad_three.T.astype(BF16)

    @pl.when(phase == 1)
    def _():
        grad_pre = nn(three_low_ref[...], down) * slope_ref[z]
        sums_ref[pl.ds(8 + z, 1), :hidden_units] = jnp.sum(grad_pre, axis=0, keepdims=True)
        pre_low = grad_pre.astype(BF16)
        acc_ref[...] += nt(pre_low, up)
        shards = dw_ref.shape[1]
        dw_ref[0, :, 0] = (
            nn(low_t_ref[...], pre_low).astype(BF16).reshape(shards, piece, hidden_units)
        )
        dw_ref[0, :, 1] = (
            nn(three_t_ref[...], act_ref[z]).astype(BF16).reshape(shards, piece, hidden_units)
        )

    @pl.when((phase == 1) & (z == tensors - 1))
    def _():
        grad_two, *both = norm_back(two_ref[...], gain2, acc_ref[...])
        sums_ref[3:4, :] = both[0]
        sums_ref[4:5, :] = both[1]
        sums_ref[5:6, :] = jnp.sum(grad_two, axis=0, keepdims=True)
        grad_ref[...] = grad_two
        low = grad_two.astype(BF16)
        grad_low_ref[...] = low
        columns = co_ref.shape[2]
        for j in range(co_ref.shape[0]):
            part = nn(low, co_ref[info_ref[2] ^ j]).astype(BF16)
            grad_mix_ref[:, j * columns : (j + 1) * columns] = part


def feed(info, sum_one, vectors, mix, columns, chunk, bias, goal, w):
    rows, width = sum_one.shape
    tensors, shards, taller, hidden_units = w.shape
    piece = width // shards
    assert hidden_units == width
    grads = (tensors, shards, 2, piece, hidden_units)
    head = (sum_one, vectors, mix)
    last = 2 * piece // chunk
    return pl.pallas_call(
        feed_kernel,
        grid_spec=pltpu.PrefetchScalarGridSpec(
            num_scalar_prefetch=1,
            grid=(2, tensors),
            in_specs=[whole(a.shape) for a in head]
            + [
                pl.BlockSpec(
                    (tensors, shards, chunk, hidden_units), lambda p, z, i: (0, 0, last, 0)
                ),
                whole(bias.shape),
                pl.BlockSpec((1, rows, width), lambda p, z, i: (0, i[2], 0)),
                pl.BlockSpec((1, shards, taller, hidden_units), lambda p, z, i: (z, 0, 0, 0)),
            ],
            out_specs=[
                whole((rows, width)),
                pl.BlockSpec((1,) + grads[1:], lambda p, z, i: (p * z, 0, 0, 0, 0)),
                whole((rows, width)),
                whole((rows, width)),
                whole((rows, width)),
                whole((16, width)),
            ],
            scratch_shapes=[
                pltpu.VMEM((rows, width), F32),
                pltpu.VMEM((rows, width), BF16),
                pltpu.VMEM((width, rows), BF16),
                pltpu.VMEM((tensors, rows, hidden_units), BF16),
                pltpu.VMEM((tensors, rows, hidden_units), F32),
                pltpu.VMEM((rows, width), F32),
                pltpu.VMEM((rows, width), BF16),
                pltpu.VMEM((width, rows), BF16),
                pltpu.VMEM((tensors, width, columns), BF16),
            ],
        ),
        out_shape=[
            shape_of((rows, width), BF16),
            shape_of(grads, BF16),
            shape_of((rows, width), F32),
            shape_of((rows, width), BF16),
            shape_of((rows, width), BF16),
            shape_of((16, width), F32),
        ],
        compiler_params=params(),
        cost_estimate=cost(rows * w.size * 6, w.size * 6, rows * width * tensors * 2),
        name="feed",
    )(info, *head, w, bias, goal, w)


def before_self_kernel(
    info_ref, grad_ref, dq_ref, cq_ref, sum_ref, gain_ref, dv_ref, o_ref, *out_refs
):
    grad_one_ref, low_ref, sums_ref = out_refs[:3]
    mix_refs = out_refs[3:]
    tensors, _, columns = o_ref.shape
    grad_hidden = grad_ref[...] + nt(dq_ref[...], cq_ref[...])
    grad_one, gain, shift = norm_back(sum_ref[...], gain_ref[...], grad_hidden)
    grad_one_ref[...] = grad_one
    low = grad_one.astype(BF16)
    low_ref[...] = low
    for j, mix_ref in enumerate(mix_refs):
        mix_ref[...] = nn(low, o_ref[j]).astype(BF16)
    sums_ref[...] = jnp.zeros_like(sums_ref)
    sums_ref[0:1, :] = gain
    sums_ref[1:2, :] = shift
    sums_ref[2:3, :] = jnp.sum(grad_one, axis=0, keepdims=True)
    queries = jnp.sum(dq_ref[...].astype(F32), axis=0, keepdims=True)
    values = jnp.sum(dv_ref[...].astype(F32), axis=0, keepdims=True)
    for j in range(tensors):
        part = slice(j * columns, (j + 1) * columns)
        at = info_ref[2] ^ j
        sums_ref[pl.ds(8 + at, 1), :columns] = queries[:, part]
        sums_ref[pl.ds(8 + tensors + at, 1), :columns] = values[:, part]


def before_self(info, grad, dq, cq, sum_one, gain, dv, o):
    rows, width = grad.shape
    tensors, _, columns = o.shape
    args = (grad, dq, cq, sum_one, gain, dv, o)
    return pl.pallas_call(
        before_self_kernel,
        grid_spec=pltpu.PrefetchScalarGridSpec(
            num_scalar_prefetch=1,
            grid=(1,),
            in_specs=[whole(a.shape) for a in args],
            out_specs=[whole((rows, width))] * 2
            + [whole((8 + 2 * tensors, width))]
            + [whole((rows, columns))] * tensors,
        ),
        out_shape=[
            shape_of((rows, width), F32),
            shape_of((rows, width), BF16),
            shape_of((8 + 2 * tensors, width), F32),
        ]
        + [shape_of((rows, columns), BF16)] * tensors,
        compiler_params=params(),
        cost_estimate=cost(rows * width * width * 4, width * width * 6 + rows * width * 14),
        name="before_self",
    )(info, *args)


def encoder_grad_kernel(dk_ref, dv_ref, w_ref, keep_ref, send_ref):
    width = dk_ref.shape[1]
    part = nt(dk_ref[...], w_ref[:, :width]) + nt(dv_ref[...], w_ref[:, width:])
    half = pl.num_programs(0) // 2

    @pl.when(pl.program_id(0) < half)
    def _():
        send_ref[...] = part.astype(BF16)

    @pl.when(pl.program_id(0) >= half)
    def _():
        keep_ref[...] = part


def encoder_grad(dk, dv, w):
    keys, width = dk.shape
    half = keys // TILE // 2
    side = pl.BlockSpec((TILE, width), lambda b: (jnp.where(b < half, b + half, b - half), 0))
    return pl.pallas_call(
        encoder_grad_kernel,
        grid=(2 * half,),
        in_specs=[side, side, whole(w.shape)],
        out_specs=[
            pl.BlockSpec((TILE, width), lambda b: (jnp.maximum(b - half, 0), 0)),
            pl.BlockSpec((TILE, width), lambda b: (jnp.minimum(b, half - 1), 0)),
        ],
        out_shape=[shape_of((keys // 2, width), F32), shape_of((keys // 2, width), BF16)],
        compiler_params=params(),
        cost_estimate=cost(keys * width * width * 4, keys * width * 10),
        name="encoder_grad",
    )(dk, dv, w)


def square_grads_kernel(info_ref, *refs, ctxs, groups):
    count = sum(groups)
    left_refs, right_refs = refs[:count], refs[count : 2 * count]
    flipped = refs[-count:]
    outs = refs[2 * count : -count]
    i, other = pl.program_id(0), pl.program_id(1)
    _, _, tensors, share, packed = outs[0].shape
    piece = share * ctxs
    columns = packed // groups[0]

    @pl.when((i == 0) & (other == 0))
    def _():
        for left_ref, flipped_ref in zip(left_refs, flipped):
            flipped_ref[...] = flip(left_ref[...])

    s = ((i ^ (info_ref[0] >> 1)) << 1) + ((info_ref[0] & 1) ^ other)
    rows = pl.ds(pl.multiple_of(s * piece, piece), piece)
    grads = [
        nn(flipped_ref[rows, :], right_ref[...]).astype(BF16)
        for flipped_ref, right_ref in zip(flipped, right_refs)
    ]

    def put(refs):
        for z in range(tensors):
            part = slice(z * columns, (z + 1) * columns)
            start = 0
            for ref, size in zip(refs, groups):
                tile = jnp.concatenate(
                    [grad[:, part] for grad in grads[start : start + size]], axis=1
                )
                start += size
                for r in range(ctxs):
                    chosen = tile[:share]
                    for c in range(1, ctxs):
                        chosen = jnp.where(
                            (info_ref[1] ^ r) == c, tile[c * share : (c + 1) * share], chosen
                        )
                    ref[0, r, z] = chosen

    @pl.when(other == 0)
    def _():
        put(outs[: len(groups)])

    @pl.when(other != 0)
    def _():
        put(outs[len(groups) :])


def square_grads(info, pairs, groups, sizes):
    shards, ctxs, tensors = sizes
    width = pairs[0][0].shape[1]
    share = width // shards // ctxs
    args = [left for left, _ in pairs] + [right for _, right in pairs]
    sides = [
        (shards // 2, ctxs, tensors, share, size * width // tensors) for size in groups
    ] * 2
    return pl.pallas_call(
        functools.partial(square_grads_kernel, ctxs=ctxs, groups=groups),
        grid_spec=pltpu.PrefetchScalarGridSpec(
            num_scalar_prefetch=1,
            grid=(shards // 2, 2),
            in_specs=[whole(a.shape) for a in args],
            out_specs=[
                pl.BlockSpec((1,) + side[1:], lambda i, c, n: (i, 0, 0, 0, 0)) for side in sides
            ],
            scratch_shapes=[pltpu.VMEM((width, left.shape[0]), BF16) for left, _ in pairs],
        ),
        out_shape=[shape_of(side, BF16) for side in sides],
        compiler_params=params(),
        cost_estimate=cost(2 * width * sum(a.size for a in args), width * width * 8),
        name="square_grads",
    )(info, *args)


def input_grad_kernel(
    info_ref, dq_ref, down_ref, dtrunk_ref, came_ref, low_ref, w_ref, *rest, ctxs, tensors
):
    part_refs = rest[:tensors]
    near_ref, far_ref, dw_ref = rest[tensors:]
    b = pl.program_id(0)

    @pl.when(b == 0)
    def _():
        dw_ref[...] = jnp.zeros_like(dw_ref)

    trunk = dtrunk_ref[...].astype(F32) + came_ref[...].astype(F32)
    dkv = (down_ref[...] + jnp.where(info_ref[1] == 0, trunk, 0.0)).astype(BF16)
    grads = jnp.concatenate([dq_ref[...], dkv], axis=1)
    dw_ref[...] += tn(low_ref[...], grads)
    put_slot(b ^ info_ref[2], nt(grads, w_ref[...]), part_refs)

    @pl.when(b == pl.num_programs(0) - 1)
    def _():
        halves, _, share, _ = near_ref.shape
        for other, ref in ((0, near_ref), (1, far_ref)):
            for i in range(halves):
                s = ((i ^ (info_ref[0] >> 1)) << 1) + ((info_ref[0] & 1) ^ other)
                for r in range(ctxs):
                    start = (s * ctxs + (info_ref[1] ^ r)) * share
                    ref[i, r] = dw_ref[pl.ds(pl.multiple_of(start, share), share), :].astype(BF16)


def input_grad(info, dq, down, dtrunk, came, low, w, sizes):
    shards, ctxs, tensors = sizes
    rows, columns = dq.shape
    width = low.shape[1]
    share = width // shards // ctxs
    side = (shards // 2, ctxs, share, 3 * columns)

    def tile(n):
        return pl.BlockSpec((TILE, n), lambda b, i: (b, 0))

    return pl.pallas_call(
        functools.partial(input_grad_kernel, ctxs=ctxs, tensors=tensors),
        grid_spec=pltpu.PrefetchScalarGridSpec(
            num_scalar_prefetch=1,
            grid=(rows // TILE,),
            in_specs=[
                tile(columns),
                tile(2 * columns),
                tile(2 * columns),
                tile(2 * columns),
                tile(width),
                whole(w.shape),
            ],
            out_specs=[whole((TILE, width))] * tensors
            + [whole(side), whole(side)],
            scratch_shapes=[pltpu.VMEM((width, 3 * columns), F32)],
        ),
        out_shape=[shape_of((TILE, width), F32)]
        + [shape_of((TILE, width), BF16)] * (tensors - 1)
        + [shape_of(side, BF16)] * 2,
        compiler_params=params(),
        cost_estimate=cost(rows * width * columns * 12, rows * width * 14),
        name="input_grad",
    )(info, dq, down, dtrunk, came, low, w)


def lay_rows_kernel(info_ref, *refs):
    in_refs, out_ref = refs[:-1], refs[-1]
    out_ref[...] = take_slot(pl.program_id(0) ^ info_ref[2], in_refs).astype(F32)


def lay_rows(info, parts):
    rows, width = parts[0].shape
    return pl.pallas_call(
        lay_rows_kernel,
        grid_spec=pltpu.PrefetchScalarGridSpec(
            num_scalar_prefetch=1,
            grid=(len(parts),),
            in_specs=[whole((rows, width))] * len(parts),
            out_specs=pl.BlockSpec((rows, width), lambda b, i: (b, 0)),
        ),
        out_shape=shape_of((rows * len(parts), width), F32),
        compiler_params=params(),
        cost_estimate=cost(0, rows * width * len(parts) * 6),
        name="lay_rows",
    )(info, *parts)


def local(sizes, *args):
    (
        layer_input,
        encoder_out,
        enc_length,
        parent_ids,
        token_segment,
        self_query,
        self_key,
        self_value,
        self_output,
        cross_query,
        cross_key,
        cross_value,
        cross_output,
        ffn_up,
        ffn_down,
        self_qbias,
        self_vbias,
        self_obias,
        cross_qbias,
        cross_vbias,
        cross_obias,
        ffn_upbias,
        ffn_downbias,
        norm1_gain,
        norm1_shift,
        norm2_gain,
        norm2_shift,
        norm3_gain,
        norm3_shift,
        out_grad,
    ) = args
    shards, ctxs, tensors = sizes["shard"], sizes["ctx"], sizes["tensor"]
    me_ctx = lax.axis_index("ctx")
    info = jnp.stack([lax.axis_index("shard"), me_ctx, lax.axis_index("tensor")]).astype(jnp.int32)
    scale = HEAD_DIM ** (-0.5)
    local_rows, width = layer_input.shape[1:]
    piece, columns = self_query.shape
    heads = columns // HEAD_DIM
    seg = token_segment.shape[1] // parent_ids.shape[1]
    assert local_rows == tensors * TILE and ctxs == 2

    def swap(a, axis, bit):
        return lax.ppermute(a, axis, [(i, i ^ bit) for i in range(sizes[axis])])

    shard_bits = [("shard", 1 << k) for k in range(1, shards.bit_length() - 1)]

    def over_tensor(a):
        return [a] + [swap(a, "tensor", j) for j in range(1, tensors)]

    def grow(a, axis, bit, *others):
        return jnp.stack(tie([a, swap(a, axis, bit)], *others))

    def add(a, b):
        return (a.astype(F32) + b.astype(F32)).astype(BF16)

    def reduce_levels(near, far):
        came = swap(far, "shard", 1)
        lead = (2,) * len(shard_bits) + near.shape[1:]
        near, came = near.reshape(lead), came.reshape(lead)

        for axis, bit in list(reversed(shard_bits)) + [("ctx", 1)]:
            send = add(near[1], came[1])
            near, came = add(near[0], came[0]), swap(send, axis, bit)
        return add(near, came)

    def join_ctx(mine):
        other = swap(mine, "ctx", 1)
        first = me_ctx == 0
        return jnp.concatenate([jnp.where(first, mine, other), jnp.where(first, other, mine)])

    def row(vector):
        return vector.reshape(1, -1)

    def tie(a, *others):
        return lax.optimization_barrier((a,) + others)[0]

    vectors = jnp.stack(
        [
            self_obias,
            norm1_gain,
            norm1_shift,
            cross_obias,
            norm2_gain,
            norm2_shift,
            ffn_downbias,
            norm3_gain,
            norm3_shift,
        ]
    )

    pack = tensors if piece % (16 * tensors) == 0 else 1
    chunk = piece // pack
    packed_co = jnp.concatenate(
        [cross_output.T[i * chunk : (i + 1) * chunk] for i in range(pack)], axis=1
    )
    packed_co = jnp.pad(packed_co, ((0, 0), (0, width - packed_co.shape[1])))
    ffn_piece = jnp.concatenate([ffn_up, ffn_down.T, packed_co], axis=0)
    bias = jnp.concatenate([cross_qbias, cross_vbias, ffn_upbias])
    bias = jnp.pad(bias, (0, -bias.shape[0] % width)).reshape(-1, width)
    bias_high = lax.reduce_precision(bias, 8, 7)
    bias_rows = 16
    bias = jnp.concatenate([bias_high, bias - bias_high]).astype(BF16)
    bias = jnp.pad(bias, ((0, bias_rows - bias.shape[0]), (0, 0)))
    squares = over_tensor(
        jnp.concatenate(
            [
                jnp.concatenate([cross_key, cross_value, self_output.T, cross_query], axis=1),
                bias,
            ],
            axis=0,
        )
    )
    enc_sent = swap(encoder_out[0].astype(BF16), "ctx", 1)
    qkv_weights = lax.all_gather(
        jnp.concatenate([self_query, self_key, self_value], axis=1), "shard", axis=0, tiled=True
    )

    scalars = (info, parent_ids[0], token_segment[0])
    q, kv, input_low = project(layer_input, qkv_weights, row(self_qbias), row(self_vbias), scale)
    squares = jnp.stack(tie(squares, q))
    ffn_all = lax.all_gather(tie(ffn_piece, squares), ("tensor", "shard"), axis=0, tiled=True)
    kv_sent = lax.ppermute(tie(kv, squares), "ctx", [(0, 1)])
    for axis, bit in shard_bits[:-1]:
        squares = grow(squares, axis, bit, kv_sent)
    kv_sent = tie(kv_sent, squares)
    *mixes, self_logs = self_forward(scalars, q, kv, kv_sent, tensors, heads, seg)
    squares = grow(squares, *shard_bits[-1], self_logs)
    near = squares.reshape((shards // 2,) + squares.shape[-3:])
    far = swap(near, "shard", 1)
    all_heads = mixes[:1] + [swap(mixes[j], "tensor", j) for j in range(1, tensors)]
    weight_ckv, weight_o, weight_cq, bias = assemble(info, near, far, shards, columns, bias_rows)
    enc_low, ckv = encode(info, encoder_out, enc_sent, weight_ckv, bias, columns)
    all_heads = all_heads[:1] + list(tie(all_heads[1:], ckv))
    sum_one, one_low, cq, self_mix = after_self(
        info,
        layer_input,
        weight_o,
        weight_cq,
        vectors[0:1],
        vectors[1:2],
        vectors[2:3],
        bias,
        all_heads,
        scale,
    )

    cross_scalars = (info, enc_length)
    cross_mix, cross_logs = cross_forward(cross_scalars, cq, ckv)

    result, ffn_grads, grad_two, two_grad_low, grad_cmix, feed_sums = feed(
        info,
        sum_one,
        vectors,
        cross_mix,
        columns,
        chunk,
        bias,
        out_grad,
        ffn_all.reshape(tensors, shards, -1, width),
    )
    ffn_grads = lax.psum_scatter(
        ffn_grads.reshape(-1, ffn_grads.shape[-1]),
        ("tensor", "shard"),
        scatter_dimension=0,
        tiled=True,
    )
    result_parts = [result] + [swap(result, "tensor", j) for j in range(1, tensors - 1)]

    dcq, dck, dcv = cross_backward(cross_scalars, cq, ckv, grad_cmix, cross_mix, cross_logs, scale)
    grad_one, one_grad_low, self_sums, *grad_mixes = before_self(
        info, grad_two, dcq, weight_cq, sum_one, vectors[1:2], dcv, weight_o
    )
    head_grads = grad_mixes[:1] + [swap(grad_mixes[j], "tensor", j) for j in range(1, tensors)]
    mesh_sizes = (shards, ctxs, tensors)
    result_parts = result_parts[:1] + list(tie(result_parts[1:], one_grad_low))
    enc_keep, enc_send = encoder_grad(tie(dck, result_parts[1:]), dcv, weight_ckv)
    enc_send, head_grads = tie((enc_send, head_grads), enc_send)
    result_parts.append(swap(tie(result, head_grads), "tensor", tensors - 1))

    dq, down, dtrunk, late_sums = self_backward(
        scalars, q, kv, kv_sent, head_grads, mixes, self_logs, heads, seg, scale, width
    )
    trunk_came = lax.ppermute(dtrunk, "ctx", [(1, 0)])
    enc_came, result_parts = tie((swap(enc_send, "ctx", 1), result_parts), dtrunk)
    enc_mine = (enc_keep + enc_came.astype(F32)).astype(BF16)
    near_a, near_b, far_a, far_b = square_grads(
        info,
        [
            (tie(enc_low, enc_mine), dck),
            (enc_low, dcv),
            (one_grad_low, self_mix),
            (one_low, dcq),
            (two_grad_low, cross_mix),
        ],
        (2, 3),
        mesh_sizes,
    )
    result_all = lay_rows(info, tie(result_parts, near_a))

    def path(near, far, order):
        lead = (2,) * len(shard_bits) + near.shape[1:]
        dims = list(reversed(shard_bits)) + [("ctx", 1)]
        came = yield swap(far, "shard", 1)
        near, came = near.reshape(lead), came.reshape(lead)
        for axis, bit in order:
            dim = dims.index((axis, bit))
            dims.pop(dim)
            index = (slice(None),) * dim
            send = add(near[index + (1,)], came[index + (1,)])
            keep = add(near[index + (0,)], came[index + (0,)])
            near, came = keep, (yield swap(send, axis, bit))
        return add(near, came)

    high = list(reversed(shard_bits))
    paths = [path(near_a, far_a, [("ctx", 1)] + high), path(near_b, far_b, high + [("ctx", 1)])]
    waits = tie([next(p) for p in paths], result_all)
    waits = [p.send(w) for p, w in zip(paths, waits)]
    sums = jnp.concatenate([feed_sums, self_sums, late_sums], axis=0)
    for axis, bit in [("shard", 1)] + shard_bits:
        sums = sums + swap(sums, axis, bit)
    trunk_came = tie(trunk_came, far_a, far_b)
    *parts, near, far = input_grad(
        info, dq, down, dtrunk, trunk_came, input_low, qkv_weights, mesh_sizes
    )
    part_came = [swap(parts[j], "tensor", j) for j in range(1, tensors)]
    waits, ffn_grads = tie((waits, ffn_grads), parts[0])
    grad_encoder = lax.psum(tie(enc_mine, ffn_grads), "tensor").astype(F32)
    ffn_grads = ffn_grads.astype(F32) + swap(ffn_grads, "ctx", 1).astype(F32)
    for _ in range(len(high)):
        waits = [p.send(w) for p, w in zip(paths, waits)]
    blocks = []
    for p, w in zip(paths, waits):
        try:
            p.send(w)
        except StopIteration as end:
            blocks.append(end.value)
    qkv_grads = join_ctx(reduce_levels(near, far)).astype(F32)
    grad_q, grad_k, grad_v = (qkv_grads[:, i * columns : (i + 1) * columns] for i in range(3))
    sums = sums + swap(tie(sums, parts[0]), "ctx", 1)
    part_came = tie(part_came, sums, qkv_grads, ffn_grads, blocks)
    input_mine = grad_one + parts[0]
    for part in part_came:
        input_mine = input_mine + part.astype(F32)
    input_mine = input_mine.astype(BF16)
    input_all = over_tensor(input_mine)
    sums, blocks = tie((sums, blocks), input_mine)
    others = over_tensor(sums)
    square_sums = []
    for block in blocks:
        total = block[0].astype(F32)
        for j in range(1, tensors):
            total = total + swap(block[j], "tensor", j).astype(F32)
        square_sums.append(total.astype(BF16))
    sums = others[0]
    for other in tie(others[1:], input_all):
        sums = sums + other
    squares = join_ctx(jnp.concatenate(square_sums, axis=1)).astype(F32)
    grad_ck, grad_cv, grad_o, grad_cq, grad_co = (
        squares[:, i * columns : (i + 1) * columns] for i in range(5)
    )
    grad_input = lay_rows(info, input_all)
    me_tensor = info[2]

    def mine(start, size):
        return lax.dynamic_slice(sums, (start + me_tensor, 0), (1, size)).reshape(-1)

    base = 16 + 8
    later = base + 2 * tensors

    return (
        result_all[None],
        grad_input[None],
        grad_encoder[None],
        grad_q,
        grad_k,
        grad_v,
        grad_o.T,
        grad_cq,
        grad_ck,
        grad_cv,
        grad_co.T,
        ffn_grads[:piece],
        ffn_grads[piece:].T,
        mine(later, columns),
        mine(later + tensors, columns),
        sums[18],
        mine(base, columns),
        mine(base + tensors, columns),
        sums[5],
        mine(8, ffn_upbias.shape[0]),
        sums[2],
        sums[16],
        sums[17],
        sums[3],
        sums[4],
        sums[0],
        sums[1],
    )


def solution(mesh):
    sizes = {axis: mesh.shape[axis] for axis in ("shard", "ctx", "tensor")}
    rows = P("shard", "ctx", None)
    tall, wide = P("shard", "tensor"), P("tensor", "shard")
    mats = (tall, tall, tall, wide, tall, tall, tall, wide, tall, wide)
    part = P("tensor")
    vectors = (part, part, P(), part, part, P(), part) + (P(),) * 7
    tree = P("shard", None)
    return jax.shard_map(
        functools.partial(local, sizes),
        mesh=mesh,
        in_specs=(rows, rows, P("shard"), tree, tree) + mats + vectors + (rows,),
        out_specs=(rows, rows, rows) + mats + vectors,
        check_vma=False,
    )
```

```python
import functools

import jax
import jax.numpy as jnp
from jax import lax
from jax.experimental import pallas as pl
from jax.experimental.pallas import tpu as pltpu
from jax.sharding import PartitionSpec as P

HEAD_DIM = 64
LANES = 128
TILE = 256
NEG = -1e30
EPS = 1e-05
F32 = jnp.float32
BF16 = jnp.bfloat16
VMEM_LIMIT = 56 * 1024 * 1024
WEIGHT = 0.01


def dot_of(a, b, a_dim, b_dim):
    return lax.dot_general(a, b, (((a_dim,), (b_dim,)), ((), ())), preferred_element_type=F32)


def nn(a, b):
    return dot_of(a, b, 1, 0)


def nt(a, b):
    return dot_of(a, b, 1, 1)


def tn(a, b):
    return dot_of(a, b, 0, 0)


def head_lanes(rows, half):
    lane = lax.broadcasted_iota(jnp.int32, (rows, LANES), 1)
    return (lane < HEAD_DIM) if half == 0 else (lane >= HEAD_DIM)


def flags_of(rows, seg):
    lane = lax.broadcasted_iota(jnp.int32, (rows, LANES), 1) % HEAD_DIM
    row = lax.broadcasted_iota(jnp.int32, (rows, LANES), 0)
    return jnp.where(lane == row // seg, 1.0, 0.0).astype(BF16)


def causal_keep(size, seg):
    key = lax.broadcasted_iota(jnp.int32, (size, size), 0)
    query = lax.broadcasted_iota(jnp.int32, (size, size), 1)
    return (key // seg != query // seg) | (key <= query)


def flip(a):
    return a.astype(F32).T.astype(a.dtype)


def lane_pad(a):
    gap = -a.shape[1] % LANES
    return jnp.concatenate([a, jnp.zeros((a.shape[0], gap), a.dtype)], axis=1) if gap else a


def fold_forward(state, queries, key_tile, value_tile, bias_tile, heads, keep):
    out = []
    for h in range(heads):
        g, half = divmod(h, 2)
        lanes = slice(g * LANES, (g + 1) * LANES)
        if half == 0:
            value_rows = flip(value_tile[:, lanes])
        keys = jnp.where(head_lanes(TILE, half), key_tile[:, lanes], bias_tile)
        scores = nt(keys, queries[h])
        if keep is not None:
            scores = jnp.where(keep, scores, NEG)
        peak, total, mix = state[3 * h : 3 * h + 3]
        new_peak = jnp.maximum(peak, jnp.max(scores, axis=0, keepdims=True))
        weights = jnp.exp(scores - new_peak)
        shrink = jnp.exp(peak - new_peak)
        total = total * shrink + jnp.sum(weights, axis=0, keepdims=True)
        mix = mix * shrink + nn(
            value_rows[half * HEAD_DIM : (half + 1) * HEAD_DIM], weights.astype(BF16)
        )
        out += [new_peak, total, mix]
    return tuple(out)


def fresh_state(heads, rows):
    state = []
    for _ in range(heads):
        state += [
            jnp.full((1, rows), NEG, F32),
            jnp.zeros((1, rows), F32),
            jnp.zeros((HEAD_DIM, rows), F32),
        ]
    return tuple(state)


def flagged_queries(q, heads, seg):
    rows = q.shape[0]
    flags = flags_of(rows, seg)
    return [
        jnp.where(head_lanes(rows, h % 2), q[:, (h // 2) * LANES : (h // 2 + 1) * LANES], flags)
        for h in range(heads)
    ]


def mixed(state, heads):
    parts = [state[3 * h + 2] / state[3 * h + 1] for h in range(heads)]
    if heads % 2:
        parts.append(jnp.zeros_like(parts[0]))
    return jnp.concatenate(
        [jnp.concatenate(parts[h : h + 2], axis=0).T for h in range(0, len(parts), 2)], axis=1
    ).astype(BF16)


def put_logs(state, heads, log_ref):
    log_ref[...] = jnp.zeros_like(log_ref)
    for h in range(heads):
        log_ref[h : h + 1, :] = state[3 * h] + jnp.log(state[3 * h + 1])


def ancestors(parent_ref, label, count):
    def step(_, carry):
        at, bits = carry
        found = at >= 0
        safe = jnp.maximum(at, 0)
        return jnp.where(found, parent_ref[safe], at), jnp.where(
            found, bits | (jnp.int32(1) << safe), bits
        )

    return lax.fori_loop(0, count, step, (parent_ref[label], jnp.int32(0)))[1]


def seg_terms(bits, labels, same, seg):
    lane = lax.broadcasted_iota(jnp.int32, (TILE, LANES), 1) % HEAD_DIM
    row = lax.broadcasted_iota(jnp.int32, (TILE, LANES), 0) // seg
    out = jnp.zeros((TILE, LANES), F32)
    for i, mask in enumerate(bits):
        for t, label in enumerate(labels):
            if same and i == t:
                continue
            term = jnp.where(((mask >> label) & 1) == 1, 0.0, NEG)
            out = jnp.where((lane == i) & (row == t), term, out)
    return out.astype(BF16)


def unpack_kv(tile):
    half = tile.shape[1] // 2
    return lane_pad(tile[:, :half]), lane_pad(tile[:, half:])


def fill_trunk(info_ref, own_ref, sent_ref, trunk_ref):
    def fill(ref):
        keys, values = unpack_kv(ref[...])
        trunk_ref[:, : keys.shape[1]] = keys
        trunk_ref[:, keys.shape[1] :] = values

    @pl.when((pl.program_id(0) == 0) & (info_ref[1] == 0))
    def _():
        fill(own_ref)

    @pl.when((pl.program_id(0) == 0) & (info_ref[1] != 0))
    def _():
        fill(sent_ref)


def tile_rows(c):
    return pl.ds(pl.multiple_of(c * TILE, TILE), TILE)


def block_masks(info_ref, parent_ref, label_ref, seg, rows):
    b = pl.program_id(0)
    per = TILE // seg
    first = info_ref[1] * rows + b * TILE
    own = [label_ref[first + i * seg] for i in range(per)]
    bits = [ancestors(parent_ref, label, parent_ref.shape[0]) for label in own]

    def terms(c):
        return seg_terms(bits, [label_ref[c * TILE + t * seg] for t in range(per)], False, seg)

    count = jnp.where(info_ref[1] == 0, b, rows // TILE)
    return seg_terms(bits, own, True, seg), terms, count


def put_slot(slot, value, refs):
    for j, ref in enumerate(refs):

        @pl.when(slot == j)
        def _(ref=ref):
            ref[...] = value.astype(ref.dtype)


def take_slot(slot, refs):
    value = refs[0][...]
    for j, ref in enumerate(refs[1:], 1):
        value = jnp.where(slot == j, ref[...], value)
    return value


def self_forward_kernel(
    info_ref, parent_ref, label_ref, q_ref, own_ref, sent_ref, *rest, heads, seg
):
    mix_refs, (log_ref, trunk_ref) = rest[:-2], rest[-2:]
    b = pl.program_id(0)
    fill_trunk(info_ref, own_ref, sent_ref, trunk_ref)
    width = trunk_ref.shape[1] // 2
    queries = flagged_queries(lane_pad(q_ref[...]), heads, seg)
    own_terms, terms, count = block_masks(
        info_ref, parent_ref, label_ref, seg, own_ref.shape[0]
    )
    keys, values = unpack_kv(own_ref[tile_rows(b), :])
    state = fold_forward(
        fresh_state(heads, TILE), queries, keys, values, own_terms, heads, causal_keep(TILE, seg)
    )

    def body(c, state):
        rows = tile_rows(c)
        return fold_forward(
            state,
            queries,
            trunk_ref[rows, :width],
            trunk_ref[rows, width:],
            terms(c),
            heads,
            None,
        )

    state = lax.fori_loop(0, count, body, state)
    put_logs(state, heads, log_ref)
    put_slot(b ^ info_ref[2], mixed(state, heads)[:, : mix_refs[0].shape[1]], mix_refs)


def params():
    return pltpu.CompilerParams(vmem_limit_bytes=VMEM_LIMIT)


def cost(flops, bytes_accessed, transcendentals=0):
    return pl.CostEstimate(
        flops=int(flops * WEIGHT),
        bytes_accessed=int(bytes_accessed * WEIGHT),
        transcendentals=int(transcendentals * WEIGHT),
    )


def whole(shape):
    return pl.BlockSpec(shape, lambda *_: (0,) * len(shape))


def shape_of(shape, dtype):
    return jax.ShapeDtypeStruct(shape, dtype)


def self_forward(scalars, q, own, sent, tensors, heads, seg):
    rows, columns = q.shape
    blocks = rows // TILE
    width = -(-columns // LANES) * LANES
    return pl.pallas_call(
        functools.partial(self_forward_kernel, heads=heads, seg=seg),
        grid_spec=pltpu.PrefetchScalarGridSpec(
            num_scalar_prefetch=3,
            grid=(blocks,),
            in_specs=[
                pl.BlockSpec((TILE, columns), lambda b, *_: (b, 0)),
                whole(own.shape),
                whole(own.shape),
            ],
            out_specs=[whole((TILE, columns))] * tensors
            + [pl.BlockSpec((8, TILE), lambda b, *_: (0, b))],
            scratch_shapes=[pltpu.VMEM((rows, 2 * width), BF16)],
        ),
        out_shape=[shape_of((TILE, columns), BF16)] * tensors + [shape_of((8, rows), F32)],
        compiler_params=params(),
        cost_estimate=cost(rows * rows * columns * 8, rows * columns * 16, rows * rows * heads),
        name="self_forward",
    )(*scalars, q, own, sent)


def fold_backward(
    queries, plain, grads, logs, deltas, key_tile, value_tile, bias_tile, heads, keep
):
    grad_keys, grad_values, grad_queries = [], [], []
    for h in range(heads):
        g, half = divmod(h, 2)
        lanes = slice(g * LANES, (g + 1) * LANES)
        if half == 0:
            key_rows = flip(key_tile[:, lanes])
        keys = jnp.where(head_lanes(TILE, half), key_tile[:, lanes], bias_tile)
        scores = nt(keys, queries[h])
        if keep is not None:
            scores = jnp.where(keep, scores, NEG)
        probs = jnp.exp(scores - logs[h])
        grad_probs = nt(value_tile[:, lanes], grads[h])
        grad_scores = (probs * (grad_probs - deltas[h])).astype(BF16)
        part_values = nn(probs.astype(BF16), grads[h])
        part_keys = nn(grad_scores, plain[h])
        if half == 0:
            grad_values.append(part_values)
            grad_keys.append(part_keys)
        else:
            grad_values[g] = grad_values[g] + part_values
            grad_keys[g] = grad_keys[g] + part_keys
        grad_queries.append(nn(key_rows[half * HEAD_DIM : (half + 1) * HEAD_DIM], grad_scores))
    return grad_keys, grad_values, tuple(grad_queries)


def backward_sides(q, grad, mix, heads, seg):
    rows = q.shape[0]
    queries = flagged_queries(q, heads, seg)
    plain, grads, deltas = [], [], []
    for h in range(heads):
        g, half = divmod(h, 2)
        lanes = slice(g * LANES, (g + 1) * LANES)
        mask = head_lanes(rows, half)
        plain.append(jnp.where(mask, q[:, lanes], jnp.zeros((), BF16)))
        grads.append(jnp.where(mask, grad[:, lanes], jnp.zeros((), BF16)))
        if half == 0:
            product = (grad[:, lanes].astype(F32) * mix[:, lanes].astype(F32)).T
        deltas.append(
            jnp.sum(product[half * HEAD_DIM : (half + 1) * HEAD_DIM], axis=0, keepdims=True)
        )
    return queries, plain, grads, deltas


def query_grads(grad_queries, scale):
    parts = list(grad_queries)
    if len(parts) % 2:
        parts.append(jnp.zeros_like(parts[0]))
    return (
        jnp.concatenate(
            [jnp.concatenate(parts[h : h + 2], axis=0).T for h in range(0, len(parts), 2)], axis=1
        )
        * scale
    ).astype(BF16)


def self_backward_kernel(
    info_ref, parent_ref, label_ref, q_ref, own_ref, sent_ref, *rest, heads, seg, scale, tensors
):
    grad_refs, mix_refs, rest = rest[:tensors], rest[tensors : 2 * tensors], rest[2 * tensors :]
    log_ref, dq_ref, down_ref, dtrunk_ref, sums_ref, trunk_ref, sum_ref, vector_ref = rest
    b = pl.program_id(0)
    slot = b ^ info_ref[2]
    fill_trunk(info_ref, own_ref, sent_ref, trunk_ref)
    width = trunk_ref.shape[1] // 2
    half_columns = own_ref.shape[1] // 2
    queries, plain, grads, deltas = backward_sides(
        lane_pad(q_ref[...]),
        lane_pad(take_slot(slot, grad_refs)),
        lane_pad(take_slot(slot, mix_refs)),
        heads,
        seg,
    )
    logs = [log_ref[h : h + 1, :] for h in range(heads)]
    own_terms, terms, count = block_masks(
        info_ref, parent_ref, label_ref, seg, own_ref.shape[0]
    )

    @pl.when(b == 0)
    def _():
        sum_ref[...] = jnp.zeros_like(sum_ref)
        vector_ref[...] = jnp.zeros_like(vector_ref)

    keys, values = unpack_kv(own_ref[tile_rows(b), :])
    grad_keys, grad_values, grad_queries = fold_backward(
        queries, plain, grads, logs, deltas, keys, values, own_terms, heads, causal_keep(TILE, seg)
    )
    down_ref[:, :half_columns] = jnp.concatenate(grad_keys, axis=1)[:, :half_columns]
    down_ref[:, half_columns:] = jnp.concatenate(grad_values, axis=1)[:, :half_columns]

    def body(c, grad_queries):
        rows = tile_rows(c)
        grad_keys, grad_values, more = fold_backward(
            queries,
            plain,
            grads,
            logs,
            deltas,
            trunk_ref[rows, :width],
            trunk_ref[rows, width:],
            terms(c),
            heads,
            None,
        )
        for g in range(len(grad_keys)):
            sum_ref[rows, g * LANES : (g + 1) * LANES] += grad_keys[g]
            sum_ref[rows, width + g * LANES : width + (g + 1) * LANES] += grad_values[g]
        return tuple(x + y for x, y in zip(grad_queries, more))

    grad_queries = lax.fori_loop(0, count, body, grad_queries)
    dq = query_grads(grad_queries, scale)[:, :half_columns]
    dq_ref[...] = dq
    vector_ref[0:1, :] += jnp.sum(dq.astype(F32), axis=0, keepdims=True)
    vector_ref[1:2, :] += jnp.sum(down_ref[:, half_columns:], axis=0, keepdims=True)

    @pl.when(b == pl.num_programs(0) - 1)
    def _():
        trunk_sum = jnp.sum(sum_ref[:, width : width + half_columns], axis=0, keepdims=True)
        sums_ref[...] = jnp.zeros_like(sums_ref)
        sums_ref[pl.ds(info_ref[2], 1), :half_columns] = vector_ref[0:1, :]
        sums_ref[pl.ds(tensors + info_ref[2], 1), :half_columns] = (
            vector_ref[1:2, :] + trunk_sum
        )
        dtrunk_ref[:, :half_columns] = sum_ref[:, :half_columns].astype(BF16)
        dtrunk_ref[:, half_columns:] = sum_ref[:, width : width + half_columns].astype(BF16)


def self_backward(scalars, q, own, sent, grads, mixes, logs, heads, seg, scale, model_width):
    rows, columns = q.shape
    blocks = rows // TILE
    width = -(-columns // LANES) * LANES
    tensors = len(grads)
    tile = pl.BlockSpec((TILE, columns), lambda b, *_: (b, 0))
    return pl.pallas_call(
        functools.partial(
            self_backward_kernel, heads=heads, seg=seg, scale=scale, tensors=tensors
        ),
        grid_spec=pltpu.PrefetchScalarGridSpec(
            num_scalar_prefetch=3,
            grid=(blocks,),
            in_specs=[tile, whole(own.shape), whole(own.shape)]
            + [whole((TILE, columns))] * (2 * tensors)
            + [pl.BlockSpec((8, TILE), lambda b, *_: (0, b))],
            out_specs=[
                tile,
                pl.BlockSpec((TILE, 2 * columns), lambda b, *_: (b, 0)),
                whole((rows, 2 * columns)),
                whole((2 * tensors, model_width)),
            ],
            scratch_shapes=[
                pltpu.VMEM((rows, 2 * width), BF16),
                pltpu.VMEM((rows, 2 * width), F32),
                pltpu.VMEM((8, columns), F32),
            ],
        ),
        out_shape=[
            shape_of((rows, columns), BF16),
            shape_of((rows, 2 * columns), F32),
            shape_of((rows, 2 * columns), BF16),
            shape_of((2 * tensors, model_width), F32),
        ],
        compiler_params=params(),
        cost_estimate=cost(rows * rows * columns * 20, rows * columns * 40, rows * rows * heads),
        name="self_backward",
    )(*scalars, q, own, sent, *grads, *mixes, logs)


def length_terms(info_ref, length_ref, c, half_rows):
    row = lax.broadcasted_iota(jnp.int32, (TILE, LANES), 0)
    lane = lax.broadcasted_iota(jnp.int32, (TILE, LANES), 1) % HEAD_DIM
    half, start = divmod(c * TILE, half_rows)
    place = row + ((half ^ info_ref[1]) * half_rows + start)
    return jnp.where((place >= length_ref[0]) & (lane == 0), NEG, 0.0).astype(BF16)


def cross_forward_kernel(info_ref, length_ref, q_ref, k_ref, v_ref, mix_ref, log_ref):
    rows, keys = q_ref.shape[0], k_ref.shape[0]
    queries = flagged_queries(q_ref[...], 2, rows)
    state = fresh_state(2, rows)
    for c in range(keys // TILE):
        part = slice(c * TILE, (c + 1) * TILE)
        terms = length_terms(info_ref, length_ref, c, keys // 2)
        state = fold_forward(state, queries, k_ref[part, :], v_ref[part, :], terms, 2, None)
    put_logs(state, 2, log_ref)
    mix_ref[...] = mixed(state, 2)


def cross_specs(rows, keys, groups):
    part = pl.BlockSpec((rows, LANES), lambda g, *_: (0, g))
    return (
        part,
        pl.BlockSpec((keys, LANES), lambda g, *_: (0, g)),
        pl.BlockSpec((keys, LANES), lambda g, *_: (0, groups + g)),
        pl.BlockSpec((8, rows), lambda g, *_: (g, 0)),
    )


def cross_forward(scalars, q, kv):
    rows, width = q.shape
    keys = kv.shape[0]
    groups = width // LANES
    part, key_side, value_side, log_side = cross_specs(rows, keys, groups)
    return pl.pallas_call(
        cross_forward_kernel,
        grid_spec=pltpu.PrefetchScalarGridSpec(
            num_scalar_prefetch=2,
            grid=(groups,),
            in_specs=[part, key_side, value_side],
            out_specs=[part, log_side],
        ),
        out_shape=[shape_of((rows, width), BF16), shape_of((8 * groups, rows), F32)],
        compiler_params=params(),
        cost_estimate=cost(
            rows * keys * width * 8, (rows + keys) * width * 4, rows * keys * groups * 2
        ),
        name="cross_forward",
    )(*scalars, q, kv, kv)


def cross_backward_kernel(
    info_ref,
    length_ref,
    q_ref,
    k_ref,
    v_ref,
    grad_ref,
    mix_ref,
    log_ref,
    dq_ref,
    dk_ref,
    dv_ref,
    *,
    scale,
):
    rows, keys = q_ref.shape[0], k_ref.shape[0]
    queries, plain, grads, deltas = backward_sides(
        q_ref[...], grad_ref[...], mix_ref[...], 2, rows
    )
    logs = [log_ref[h : h + 1, :] for h in range(2)]
    total = (jnp.zeros((HEAD_DIM, rows), F32),) * 2
    for c in range(keys // TILE):
        part = slice(c * TILE, (c + 1) * TILE)
        terms = length_terms(info_ref, length_ref, c, keys // 2)
        grad_keys, grad_values, more = fold_backward(
            queries, plain, grads, logs, deltas, k_ref[part, :], v_ref[part, :], terms, 2, None
        )
        dk_ref[part, :] = grad_keys[0].astype(BF16)
        dv_ref[part, :] = grad_values[0].astype(BF16)
        total = tuple(x + y for x, y in zip(total, more))
    dq_ref[...] = query_grads(total, scale)


def cross_backward(scalars, q, kv, grad, mix, logs, scale):
    rows, width = q.shape
    keys = kv.shape[0]
    groups = width // LANES
    part, key_side, value_side, log_side = cross_specs(rows, keys, groups)
    return pl.pallas_call(
        functools.partial(cross_backward_kernel, scale=scale),
        grid_spec=pltpu.PrefetchScalarGridSpec(
            num_scalar_prefetch=2,
            grid=(groups,),
            in_specs=[part, key_side, value_side, part, part, log_side],
            out_specs=[part, key_side, key_side],
        ),
        out_shape=[
            shape_of((rows, width), BF16),
            shape_of((keys, width), BF16),
            shape_of((keys, width), BF16),
        ],
        compiler_params=params(),
        cost_estimate=cost(
            rows * keys * width * 20, (rows * 4 + keys * 4) * width * 2, rows * keys * groups * 2
        ),
        name="cross_backward",
    )(*scalars, q, kv, kv, grad, mix, logs)


def norm_parts(values):
    center = values - jnp.mean(values, axis=-1, keepdims=True)
    inverse = lax.rsqrt(jnp.mean(center * center, axis=-1, keepdims=True) + EPS)
    return center * inverse, inverse


def norm_back(pre_sum, gain, grad_out):
    normed, inverse = norm_parts(pre_sum)
    grad_normed = grad_out * gain
    grad_pre = inverse * (
        grad_normed
        - jnp.mean(grad_normed, axis=-1, keepdims=True)
        - normed * jnp.mean(grad_normed * normed, axis=-1, keepdims=True)
    )
    return (
        grad_pre,
        jnp.sum(grad_out * normed, axis=0, keepdims=True),
        jnp.sum(grad_out, axis=0, keepdims=True),
    )


def project_kernel(x_ref, w_ref, qb_ref, vb_ref, q_ref, kv_ref, low_ref, *, scale):
    columns = q_ref.shape[1]
    low = x_ref[0].astype(BF16)
    low_ref[...] = low
    out = nn(low, w_ref[...])
    q_ref[...] = ((out[:, :columns] + qb_ref[...]) * scale).astype(BF16)
    kv_ref[:, :columns] = out[:, columns : 2 * columns].astype(BF16)
    kv_ref[:, columns:] = (out[:, 2 * columns :] + vb_ref[...]).astype(BF16)


def project(x, w, qb, vb, scale):
    _, rows, width = x.shape
    columns = qb.shape[1]
    return pl.pallas_call(
        functools.partial(project_kernel, scale=scale),
        grid=(rows // TILE,),
        in_specs=[
            pl.BlockSpec((1, TILE, width), lambda b: (0, b, 0)),
            whole(w.shape),
            whole(qb.shape),
            whole(vb.shape),
        ],
        out_specs=[
            pl.BlockSpec((TILE, columns), lambda b: (b, 0)),
            pl.BlockSpec((TILE, 2 * columns), lambda b: (b, 0)),
            pl.BlockSpec((TILE, width), lambda b: (b, 0)),
        ],
        out_shape=[
            shape_of((rows, columns), BF16),
            shape_of((rows, 2 * columns), BF16),
            shape_of((rows, width), BF16),
        ],
        compiler_params=params(),
        cost_estimate=cost(rows * width * columns * 6, rows * width * 8),
        name="project",
    )(x, w, qb, vb)


def assemble_kernel(info_ref, near_ref, far_ref, ckv_ref, o_ref, cq_ref, bias_ref):
    tensors, _, columns = o_ref.shape
    width = tensors * columns
    rows = near_ref.shape[2] - bias_ref.shape[1]

    def put(ref):
        for z in range(tensors):
            part = slice(z * columns, (z + 1) * columns)
            late = slice(width + z * columns, width + (z + 1) * columns)
            ckv_ref[:, part] = ref[0, z, :rows, :columns]
            ckv_ref[:, late] = ref[0, z, :rows, columns : 2 * columns]
            o_ref[z] = ref[0, z, :rows, 2 * columns : 3 * columns]
            cq_ref[:, part] = ref[0, z, :rows, 3 * columns :]
        bias_ref[...] = ref[0, :, rows:, :]

    other = (pl.program_id(0) & 1) ^ (info_ref[0] & 1)

    @pl.when(other == 0)
    def _():
        put(near_ref)

    @pl.when(other != 0)
    def _():
        put(far_ref)


def assemble(info, near, far, shards, columns, bias_rows):
    _, tensors, rows, packed = near.shape
    rows -= bias_rows
    width = tensors * columns
    height = shards * rows
    side = pl.BlockSpec((1,) + near.shape[1:], lambda s, i: ((s >> 1) ^ (i[0] >> 1), 0, 0, 0))
    bias = (tensors, bias_rows, packed)
    return pl.pallas_call(
        assemble_kernel,
        grid_spec=pltpu.PrefetchScalarGridSpec(
            num_scalar_prefetch=1,
            grid=(shards,),
            in_specs=[side, side],
            out_specs=[
                pl.BlockSpec((rows, 2 * width), lambda s, i: (s, 0)),
                pl.BlockSpec((tensors, rows, columns), lambda s, i: (0, s, 0)),
                pl.BlockSpec((rows, width), lambda s, i: (s, 0)),
                whole(bias),
            ],
        ),
        out_shape=[
            shape_of((height, 2 * width), BF16),
            shape_of((tensors, height, columns), BF16),
            shape_of((height, width), BF16),
            shape_of(bias, BF16),
        ],
        compiler_params=params(),
        cost_estimate=cost(0, near.size * 8),
        name="assemble",
    )(info, near, far)


def bias_part(bias_ref, j, start, columns):
    width = bias_ref.shape[2]
    row, lane = divmod(start, width)
    tall = bias_ref[j].astype(F32)
    full = tall[:2] + tall[2:4]
    if lane + columns <= width:
        return full[row : row + 1, lane : lane + columns]
    return jnp.concatenate(
        [full[row : row + 1, lane:], full[row + 1 : row + 2, : lane + columns - width]], axis=1
    )


def tensor_row(bias_ref, start, columns):
    return jnp.concatenate(
        [bias_part(bias_ref, j, start, columns) for j in range(bias_ref.shape[0])], axis=1
    )


def after_self_kernel(
    info_ref, x_ref, o_ref, cq_ref, ob_ref, gain_ref, shift_ref, bias_ref, *rest, scale
):
    mix_refs, (sum_ref, low_ref, q_ref, joined_ref) = rest[:-4], rest[-4:]
    joined_ref[...] = jnp.concatenate([mix_ref[...] for mix_ref in mix_refs], axis=1)
    total = x_ref[0] + ob_ref[...]
    for j, mix_ref in enumerate(mix_refs):
        total = total + nt(mix_ref[...], o_ref[j])
    sum_ref[...] = total
    hidden = norm_parts(total)[0] * gain_ref[...] + shift_ref[...]
    low = hidden.astype(BF16)
    low_ref[...] = low
    bias = tensor_row(bias_ref, 0, mix_refs[0].shape[1])
    q_ref[...] = ((nn(low, cq_ref[...]) + bias) * scale).astype(BF16)


def after_self(info, x, o, cq, ob, gain, shift, bias, mixes, scale):
    width = x.shape[2]
    rows = mixes[0].shape[0]
    return pl.pallas_call(
        functools.partial(after_self_kernel, scale=scale),
        grid_spec=pltpu.PrefetchScalarGridSpec(
            num_scalar_prefetch=1,
            grid=(1,),
            in_specs=[pl.BlockSpec((1, rows, width), lambda s, i: (0, i[2], 0))]
            + [whole(a.shape) for a in (o, cq, ob, gain, shift, bias) + tuple(mixes)],
            out_specs=[whole((rows, width))] * 4,
        ),
        out_shape=[shape_of((rows, width), F32)] + [shape_of((rows, width), BF16)] * 3,
        compiler_params=params(),
        cost_estimate=cost(rows * width * width * 4, width * width * 4 + rows * width * 12),
        name="after_self",
    )(info, x, o, cq, ob, gain, shift, bias, *mixes)


def encode_kernel(info_ref, own_ref, sent_ref, w_ref, bias_ref, low_ref, kv_ref, *, columns):
    width = low_ref.shape[1]
    half = pl.num_programs(0) // 2

    @pl.when(pl.program_id(0) < half)
    def _():
        low_ref[...] = own_ref[0].astype(BF16)

    @pl.when(pl.program_id(0) >= half)
    def _():
        low_ref[...] = sent_ref[...]

    out = nn(low_ref[...], w_ref[...])
    kv_ref[:, :width] = out[:, :width].astype(BF16)
    kv_ref[:, width:] = (
        out[:, width:] + tensor_row(bias_ref, columns, columns)
    ).astype(BF16)


def encode(info, own, sent, w, bias, columns):
    _, rows, width = own.shape
    half = rows // TILE
    return pl.pallas_call(
        functools.partial(encode_kernel, columns=columns),
        grid_spec=pltpu.PrefetchScalarGridSpec(
            num_scalar_prefetch=1,
            grid=(2 * half,),
            in_specs=[
                pl.BlockSpec((1, TILE, width), lambda b, i: (0, jnp.minimum(b, half - 1), 0)),
                pl.BlockSpec((TILE, width), lambda b, i: (jnp.maximum(b - half, 0), 0)),
                whole(w.shape),
                whole(bias.shape),
            ],
            out_specs=[
                pl.BlockSpec((TILE, width), lambda b, i: (b, 0)),
                pl.BlockSpec((TILE, 2 * width), lambda b, i: (b, 0)),
            ],
        ),
        out_shape=[shape_of((2 * rows, width), BF16), shape_of((2 * rows, 2 * width), BF16)],
        compiler_params=params(),
        cost_estimate=cost(rows * width * width * 8, rows * width * 14),
        name="encode",
    )(info, own, sent, w, bias)


def gelu_parts(values):
    half = 0.5 * (1.0 + lax.erf(values * (0.5**0.5)))
    slope = half + values * (jnp.exp(-0.5 * values * values) * (0.5 / jnp.pi) ** 0.5)
    return values * half, slope


def feed_kernel(
    info_ref,
    sum_ref,
    vectors_ref,
    mix_ref,
    packed_ref,
    bias_ref,
    goal_ref,
    w_ref,
    result_ref,
    near_ref,
    far_ref,
    grad_ref,
    grad_low_ref,
    grad_mix_ref,
    sums_ref,
    two_ref,
    low_ref,
    low_t_ref,
    act_ref,
    slope_ref,
    acc_ref,
    three_low_ref,
    three_t_ref,
    co_ref,
):
    phase, z = pl.program_id(0), pl.program_id(1)
    tensors = pl.num_programs(1)
    rows, width = sum_ref.shape
    hidden_units = w_ref.shape[3]
    piece = width // w_ref.shape[1]
    up = w_ref[0, :, :piece].reshape(width, hidden_units)
    down = w_ref[0, :, piece : 2 * piece].reshape(width, hidden_units)
    gain1, shift1, cob, gain2, shift2, downb, gain3, shift3 = (
        vectors_ref[i : i + 1, :] for i in range(1, 9)
    )

    @pl.when((phase == 0) & (z == 0))
    def _():
        _, shards, chunk, _ = packed_ref.shape
        columns = co_ref.shape[2]
        for t in range(co_ref.shape[0]):
            for s in range(shards):
                for i in range(piece // chunk):
                    start = s * piece + i * chunk
                    co_ref[t, start : start + chunk, :] = packed_ref[
                        t, s, :, i * columns : (i + 1) * columns
                    ]
        hidden_one = norm_parts(sum_ref[...])[0] * gain1 + shift1
        sum_two = hidden_one + cob
        for j in range(co_ref.shape[0]):
            part = mix_ref[:, j * columns : (j + 1) * columns]
            sum_two = sum_two + nt(part, co_ref[info_ref[2] ^ j])
        two_ref[...] = sum_two
        hidden_two = norm_parts(sum_two)[0] * gain2 + shift2
        low_ref[...] = hidden_two.astype(BF16)
        low_t_ref[...] = hidden_two.T.astype(BF16)
        acc_ref[...] = hidden_two + downb
        sums_ref[...] = jnp.zeros_like(sums_ref)

    @pl.when(phase == 0)
    def _():
        bias = bias_part(bias_ref, z ^ info_ref[2], 2 * co_ref.shape[2], hidden_units)
        pre = nn(low_ref[...], up) + bias
        value, slope = gelu_parts(pre)
        act = value.astype(BF16)
        act_ref[z] = act
        slope_ref[z] = slope
        acc_ref[...] += nt(act, down)

    @pl.when((phase == 0) & (z == tensors - 1))
    def _():
        sum_three = acc_ref[...]
        result = norm_parts(sum_three)[0] * gain3 + shift3
        result_ref[...] = result.astype(BF16)
        grad_three, *both = norm_back(sum_three, gain3, goal_ref[0])
        sums_ref[0:1, :] = both[0]
        sums_ref[1:2, :] = both[1]
        sums_ref[2:3, :] = jnp.sum(grad_three, axis=0, keepdims=True)
        acc_ref[...] = grad_three
        three_low_ref[...] = grad_three.astype(BF16)
        three_t_ref[...] = grad_three.T.astype(BF16)

    @pl.when(phase == 1)
    def _():
        grad_pre = nn(three_low_ref[...], down) * slope_ref[z]
        sums_ref[pl.ds(8 + z, 1), :hidden_units] = jnp.sum(grad_pre, axis=0, keepdims=True)
        pre_low = grad_pre.astype(BF16)
        acc_ref[...] += nt(pre_low, up)
        products = (
            nn(low_t_ref[...], pre_low).astype(BF16),
            nn(three_t_ref[...], act_ref[z]).astype(BF16),
        )
        _, _, ctxs, _, share, _ = near_ref.shape

        def put(core):
            for mat, product in enumerate(products):
                for s in range(w_ref.shape[1]):
                    ref = near_ref if (s & 1) == core else far_ref
                    for c in range(ctxs):
                        start = s * piece + c * share
                        ref[mat, (s >> 1) ^ (info_ref[0] >> 1), c ^ info_ref[1], 0] = product[
                            start : start + share
                        ]

        @pl.when((info_ref[0] & 1) == 0)
        def _():
            put(0)

        @pl.when((info_ref[0] & 1) != 0)
        def _():
            put(1)

    @pl.when((phase == 1) & (z == tensors - 1))
    def _():
        grad_two, *both = norm_back(two_ref[...], gain2, acc_ref[...])
        sums_ref[3:4, :] = both[0]
        sums_ref[4:5, :] = both[1]
        sums_ref[5:6, :] = jnp.sum(grad_two, axis=0, keepdims=True)
        grad_ref[...] = grad_two
        low = grad_two.astype(BF16)
        grad_low_ref[...] = low
        columns = co_ref.shape[2]
        for j in range(co_ref.shape[0]):
            part = nn(low, co_ref[info_ref[2] ^ j]).astype(BF16)
            grad_mix_ref[:, j * columns : (j + 1) * columns] = part


def feed(info, sum_one, vectors, mix, columns, chunk, bias, goal, w, ctxs):
    rows, width = sum_one.shape
    tensors, shards, taller, hidden_units = w.shape
    piece = width // shards
    assert hidden_units == width
    grads = (2, shards // 2, ctxs, tensors, piece // ctxs, hidden_units)
    grads_spec = pl.BlockSpec(
        grads[:3] + (1,) + grads[4:], lambda p, z, i: (0, 0, 0, (p * z) ^ i[2], 0, 0)
    )
    head = (sum_one, vectors, mix)
    last = 2 * piece // chunk
    return pl.pallas_call(
        feed_kernel,
        grid_spec=pltpu.PrefetchScalarGridSpec(
            num_scalar_prefetch=1,
            grid=(2, tensors),
            in_specs=[whole(a.shape) for a in head]
            + [
                pl.BlockSpec(
                    (tensors, shards, chunk, hidden_units), lambda p, z, i: (0, 0, last, 0)
                ),
                whole(bias.shape),
                pl.BlockSpec((1, rows, width), lambda p, z, i: (0, i[2], 0)),
                pl.BlockSpec((1, shards, taller, hidden_units), lambda p, z, i: (z, 0, 0, 0)),
            ],
            out_specs=[
                whole((rows, width)),
                grads_spec,
                grads_spec,
                whole((rows, width)),
                whole((rows, width)),
                whole((rows, width)),
                whole((16, width)),
            ],
            scratch_shapes=[
                pltpu.VMEM((rows, width), F32),
                pltpu.VMEM((rows, width), BF16),
                pltpu.VMEM((width, rows), BF16),
                pltpu.VMEM((tensors, rows, hidden_units), BF16),
                pltpu.VMEM((tensors, rows, hidden_units), F32),
                pltpu.VMEM((rows, width), F32),
                pltpu.VMEM((rows, width), BF16),
                pltpu.VMEM((width, rows), BF16),
                pltpu.VMEM((tensors, width, columns), BF16),
            ],
        ),
        out_shape=[
            shape_of((rows, width), BF16),
            shape_of(grads, BF16),
            shape_of(grads, BF16),
            shape_of((rows, width), F32),
            shape_of((rows, width), BF16),
            shape_of((rows, width), BF16),
            shape_of((16, width), F32),
        ],
        compiler_params=params(),
        cost_estimate=cost(rows * w.size * 6, w.size * 6, rows * width * tensors * 2),
        name="feed",
    )(info, *head, w, bias, goal, w)


def before_self_kernel(
    info_ref, grad_ref, dq_ref, cq_ref, sum_ref, gain_ref, dv_ref, o_ref, *out_refs
):
    grad_one_ref, low_ref, sums_ref = out_refs[:3]
    mix_refs = out_refs[3:]
    tensors, _, columns = o_ref.shape
    grad_hidden = grad_ref[...] + nt(dq_ref[...], cq_ref[...])
    grad_one, gain, shift = norm_back(sum_ref[...], gain_ref[...], grad_hidden)
    grad_one_ref[...] = grad_one
    low = grad_one.astype(BF16)
    low_ref[...] = low
    for j, mix_ref in enumerate(mix_refs):
        mix_ref[...] = nn(low, o_ref[j]).astype(BF16)
    sums_ref[...] = jnp.zeros_like(sums_ref)
    sums_ref[0:1, :] = gain
    sums_ref[1:2, :] = shift
    sums_ref[2:3, :] = jnp.sum(grad_one, axis=0, keepdims=True)
    queries = jnp.sum(dq_ref[...].astype(F32), axis=0, keepdims=True)
    values = jnp.sum(dv_ref[...].astype(F32), axis=0, keepdims=True)
    for j in range(tensors):
        part = slice(j * columns, (j + 1) * columns)
        at = info_ref[2] ^ j
        sums_ref[pl.ds(8 + at, 1), :columns] = queries[:, part]
        sums_ref[pl.ds(8 + tensors + at, 1), :columns] = values[:, part]


def before_self(info, grad, dq, cq, sum_one, gain, dv, o):
    rows, width = grad.shape
    tensors, _, columns = o.shape
    args = (grad, dq, cq, sum_one, gain, dv, o)
    return pl.pallas_call(
        before_self_kernel,
        grid_spec=pltpu.PrefetchScalarGridSpec(
            num_scalar_prefetch=1,
            grid=(1,),
            in_specs=[whole(a.shape) for a in args],
            out_specs=[whole((rows, width))] * 2
            + [whole((8 + 2 * tensors, width))]
            + [whole((rows, columns))] * tensors,
        ),
        out_shape=[
            shape_of((rows, width), F32),
            shape_of((rows, width), BF16),
            shape_of((8 + 2 * tensors, width), F32),
        ]
        + [shape_of((rows, columns), BF16)] * tensors,
        compiler_params=params(),
        cost_estimate=cost(rows * width * width * 4, width * width * 6 + rows * width * 14),
        name="before_self",
    )(info, *args)


def encoder_grad_kernel(dk_ref, dv_ref, w_ref, keep_ref, send_ref):
    width = dk_ref.shape[1]
    part = nt(dk_ref[...], w_ref[:, :width]) + nt(dv_ref[...], w_ref[:, width:])
    half = pl.num_programs(0) // 2

    @pl.when(pl.program_id(0) < half)
    def _():
        send_ref[...] = part.astype(BF16)

    @pl.when(pl.program_id(0) >= half)
    def _():
        keep_ref[...] = part


def encoder_grad(dk, dv, w):
    keys, width = dk.shape
    half = keys // TILE // 2
    side = pl.BlockSpec((TILE, width), lambda b: (jnp.where(b < half, b + half, b - half), 0))
    return pl.pallas_call(
        encoder_grad_kernel,
        grid=(2 * half,),
        in_specs=[side, side, whole(w.shape)],
        out_specs=[
            pl.BlockSpec((TILE, width), lambda b: (jnp.maximum(b - half, 0), 0)),
            pl.BlockSpec((TILE, width), lambda b: (jnp.minimum(b, half - 1), 0)),
        ],
        out_shape=[shape_of((keys // 2, width), F32), shape_of((keys // 2, width), BF16)],
        compiler_params=params(),
        cost_estimate=cost(keys * width * width * 4, keys * width * 10),
        name="encoder_grad",
    )(dk, dv, w)


def square_grads_kernel(info_ref, *refs, ctxs, groups):
    count = sum(groups)
    left_refs, right_refs = refs[:count], refs[count : 2 * count]
    flipped = refs[-count:]
    outs = refs[2 * count : -count]
    i, other = pl.program_id(0), pl.program_id(1)
    _, _, tensors, share, packed = outs[0].shape
    piece = share * ctxs
    columns = packed // groups[0]

    @pl.when((i == 0) & (other == 0))
    def _():
        for left_ref, flipped_ref in zip(left_refs, flipped):
            flipped_ref[...] = flip(left_ref[...])

    s = ((i ^ (info_ref[0] >> 1)) << 1) + ((info_ref[0] & 1) ^ other)
    rows = pl.ds(pl.multiple_of(s * piece, piece), piece)
    grads = [
        nn(flipped_ref[rows, :], right_ref[...]).astype(BF16)
        for flipped_ref, right_ref in zip(flipped, right_refs)
    ]

    def put(refs):
        for z in range(tensors):
            part = slice(z * columns, (z + 1) * columns)
            start = 0
            for ref, size in zip(refs, groups):
                tile = jnp.concatenate(
                    [grad[:, part] for grad in grads[start : start + size]], axis=1
                )
                start += size
                for r in range(ctxs):
                    chosen = tile[:share]
                    for c in range(1, ctxs):
                        chosen = jnp.where(
                            (info_ref[1] ^ r) == c, tile[c * share : (c + 1) * share], chosen
                        )
                    ref[0, r, z] = chosen

    @pl.when(other == 0)
    def _():
        put(outs[: len(groups)])

    @pl.when(other != 0)
    def _():
        put(outs[len(groups) :])


def square_grads(info, pairs, groups, sizes):
    shards, ctxs, tensors = sizes
    width = pairs[0][0].shape[1]
    share = width // shards // ctxs
    args = [left for left, _ in pairs] + [right for _, right in pairs]
    sides = [
        (shards // 2, ctxs, tensors, share, size * width // tensors) for size in groups
    ] * 2
    return pl.pallas_call(
        functools.partial(square_grads_kernel, ctxs=ctxs, groups=groups),
        grid_spec=pltpu.PrefetchScalarGridSpec(
            num_scalar_prefetch=1,
            grid=(shards // 2, 2),
            in_specs=[whole(a.shape) for a in args],
            out_specs=[
                pl.BlockSpec((1,) + side[1:], lambda i, c, n: (i, 0, 0, 0, 0)) for side in sides
            ],
            scratch_shapes=[pltpu.VMEM((width, left.shape[0]), BF16) for left, _ in pairs],
        ),
        out_shape=[shape_of(side, BF16) for side in sides],
        compiler_params=params(),
        cost_estimate=cost(2 * width * sum(a.size for a in args), width * width * 8),
        name="square_grads",
    )(info, *args)


def input_grad_kernel(
    info_ref, dq_ref, down_ref, dtrunk_ref, came_ref, low_ref, w_ref, *rest, ctxs, tensors
):
    part_refs = rest[:tensors]
    near_ref, far_ref, dw_ref = rest[tensors:]
    b = pl.program_id(0)

    @pl.when(b == 0)
    def _():
        dw_ref[...] = jnp.zeros_like(dw_ref)

    trunk = dtrunk_ref[...].astype(F32) + came_ref[...].astype(F32)
    dkv = (down_ref[...] + jnp.where(info_ref[1] == 0, trunk, 0.0)).astype(BF16)
    grads = jnp.concatenate([dq_ref[...], dkv], axis=1)
    dw_ref[...] += tn(low_ref[...], grads)
    put_slot(b ^ info_ref[2], nt(grads, w_ref[...]), part_refs)

    @pl.when(b == pl.num_programs(0) - 1)
    def _():
        halves, _, share, _ = near_ref.shape
        for other, ref in ((0, near_ref), (1, far_ref)):
            for i in range(halves):
                s = ((i ^ (info_ref[0] >> 1)) << 1) + ((info_ref[0] & 1) ^ other)
                for r in range(ctxs):
                    start = (s * ctxs + (info_ref[1] ^ r)) * share
                    ref[i, r] = dw_ref[pl.ds(pl.multiple_of(start, share), share), :].astype(BF16)


def input_grad(info, dq, down, dtrunk, came, low, w, sizes):
    shards, ctxs, tensors = sizes
    rows, columns = dq.shape
    width = low.shape[1]
    share = width // shards // ctxs
    side = (shards // 2, ctxs, share, 3 * columns)

    def tile(n):
        return pl.BlockSpec((TILE, n), lambda b, i: (b, 0))

    return pl.pallas_call(
        functools.partial(input_grad_kernel, ctxs=ctxs, tensors=tensors),
        grid_spec=pltpu.PrefetchScalarGridSpec(
            num_scalar_prefetch=1,
            grid=(rows // TILE,),
            in_specs=[
                tile(columns),
                tile(2 * columns),
                tile(2 * columns),
                tile(2 * columns),
                tile(width),
                whole(w.shape),
            ],
            out_specs=[whole((TILE, width))] * tensors
            + [whole(side), whole(side)],
            scratch_shapes=[pltpu.VMEM((width, 3 * columns), F32)],
        ),
        out_shape=[shape_of((TILE, width), F32)]
        + [shape_of((TILE, width), BF16)] * (tensors - 1)
        + [shape_of(side, BF16)] * 2,
        compiler_params=params(),
        cost_estimate=cost(rows * width * columns * 12, rows * width * 14),
        name="input_grad",
    )(info, dq, down, dtrunk, came, low, w)


def lay_rows_kernel(info_ref, *refs):
    in_refs, out_ref = refs[:-1], refs[-1]
    out_ref[...] = take_slot(pl.program_id(0) ^ info_ref[2], in_refs).astype(F32)


def lay_rows(info, parts):
    rows, width = parts[0].shape
    return pl.pallas_call(
        lay_rows_kernel,
        grid_spec=pltpu.PrefetchScalarGridSpec(
            num_scalar_prefetch=1,
            grid=(len(parts),),
            in_specs=[whole((rows, width))] * len(parts),
            out_specs=pl.BlockSpec((rows, width), lambda b, i: (b, 0)),
        ),
        out_shape=shape_of((rows * len(parts), width), F32),
        compiler_params=params(),
        cost_estimate=cost(0, rows * width * len(parts) * 6),
        name="lay_rows",
    )(info, *parts)


def local(sizes, *args):
    (
        layer_input,
        encoder_out,
        enc_length,
        parent_ids,
        token_segment,
        self_query,
        self_key,
        self_value,
        self_output,
        cross_query,
        cross_key,
        cross_value,
        cross_output,
        ffn_up,
        ffn_down,
        self_qbias,
        self_vbias,
        self_obias,
        cross_qbias,
        cross_vbias,
        cross_obias,
        ffn_upbias,
        ffn_downbias,
        norm1_gain,
        norm1_shift,
        norm2_gain,
        norm2_shift,
        norm3_gain,
        norm3_shift,
        out_grad,
    ) = args
    shards, ctxs, tensors = sizes["shard"], sizes["ctx"], sizes["tensor"]
    me_ctx = lax.axis_index("ctx")
    info = jnp.stack([lax.axis_index("shard"), me_ctx, lax.axis_index("tensor")]).astype(jnp.int32)
    scale = HEAD_DIM ** (-0.5)
    local_rows, width = layer_input.shape[1:]
    piece, columns = self_query.shape
    heads = columns // HEAD_DIM
    seg = token_segment.shape[1] // parent_ids.shape[1]
    assert local_rows == tensors * TILE and ctxs == 2

    def bits_of(axis):
        return [1 << k for k in range(sizes[axis].bit_length() - 1)]

    def swap(a, axis, bit):
        return lax.ppermute(a, axis, [(i, i ^ bit) for i in range(sizes[axis])])

    shard_bits = [("shard", 1 << k) for k in range(1, shards.bit_length() - 1)]

    def over_tensor(a):
        return [a] + [swap(a, "tensor", j) for j in range(1, tensors)]

    def grow(a, axis, bit, *others):
        return jnp.stack(tie([a, swap(a, axis, bit)], *others))

    def add(a, b):
        return (a.astype(F32) + b.astype(F32)).astype(BF16)

    def reduce_levels(near, far):
        came = swap(far, "shard", 1)
        lead = (2,) * len(shard_bits) + near.shape[1:]
        near, came = near.reshape(lead), came.reshape(lead)

        for axis, bit in list(reversed(shard_bits)) + [("ctx", 1)]:
            send = add(near[1], came[1])
            near, came = add(near[0], came[0]), swap(send, axis, bit)
        return add(near, came)

    def join_ctx(mine):
        other = swap(mine, "ctx", 1)
        first = me_ctx == 0
        return jnp.concatenate([jnp.where(first, mine, other), jnp.where(first, other, mine)])

    def row(vector):
        return vector.reshape(1, -1)

    def tie(a, *others):
        return lax.optimization_barrier((a,) + others)[0]

    vectors = jnp.stack(
        [
            self_obias,
            norm1_gain,
            norm1_shift,
            cross_obias,
            norm2_gain,
            norm2_shift,
            ffn_downbias,
            norm3_gain,
            norm3_shift,
        ]
    )

    pack = tensors if piece % (16 * tensors) == 0 else 1
    chunk = piece // pack
    packed_co = jnp.concatenate(
        [cross_output.T[i * chunk : (i + 1) * chunk] for i in range(pack)], axis=1
    )
    packed_co = jnp.pad(packed_co, ((0, 0), (0, width - packed_co.shape[1])))
    ffn_piece = jnp.concatenate([ffn_up, ffn_down.T, packed_co], axis=0)
    bias = jnp.concatenate([cross_qbias, cross_vbias, ffn_upbias])
    bias = jnp.pad(bias, (0, -bias.shape[0] % width)).reshape(-1, width)
    bias_high = lax.reduce_precision(bias, 8, 7)
    bias_rows = 16
    bias = jnp.concatenate([bias_high, bias - bias_high]).astype(BF16)
    bias = jnp.pad(bias, ((0, bias_rows - bias.shape[0]), (0, 0)))
    squares = over_tensor(
        jnp.concatenate(
            [
                jnp.concatenate([cross_key, cross_value, self_output.T, cross_query], axis=1),
                bias,
            ],
            axis=0,
        )
    )
    enc_sent = swap(encoder_out[0].astype(BF16), "ctx", 1)
    qkv_weights = lax.all_gather(
        jnp.concatenate([self_query, self_key, self_value], axis=1), "shard", axis=0, tiled=True
    )

    scalars = (info, parent_ids[0], token_segment[0])
    q, kv, input_low = project(layer_input, qkv_weights, row(self_qbias), row(self_vbias), scale)
    squares = jnp.stack(tie(squares, q))
    ffn_all = lax.all_gather(tie(ffn_piece, squares), ("tensor", "shard"), axis=0, tiled=True)
    kv_sent = lax.ppermute(tie(kv, squares), "ctx", [(0, 1)])
    for axis, bit in shard_bits[:-1]:
        squares = grow(squares, axis, bit, kv_sent)
    kv_sent = tie(kv_sent, squares)
    *mixes, self_logs = self_forward(scalars, q, kv, kv_sent, tensors, heads, seg)
    squares = grow(squares, *shard_bits[-1], self_logs)
    near = squares.reshape((shards // 2,) + squares.shape[-3:])
    far = swap(near, "shard", 1)
    all_heads = mixes[:1] + [swap(mixes[j], "tensor", j) for j in range(1, tensors)]
    weight_ckv, weight_o, weight_cq, bias = assemble(info, near, far, shards, columns, bias_rows)
    enc_low, ckv = encode(info, encoder_out, enc_sent, weight_ckv, bias, columns)
    all_heads = all_heads[:1] + list(tie(all_heads[1:], ckv))
    sum_one, one_low, cq, self_mix = after_self(
        info,
        layer_input,
        weight_o,
        weight_cq,
        vectors[0:1],
        vectors[1:2],
        vectors[2:3],
        bias,
        all_heads,
        scale,
    )

    cross_scalars = (info, enc_length)
    cross_mix, cross_logs = cross_forward(cross_scalars, cq, ckv)

    result, ffn_near, ffn_far, grad_two, two_grad_low, grad_cmix, feed_sums = feed(
        info,
        sum_one,
        vectors,
        cross_mix,
        columns,
        chunk,
        bias,
        out_grad,
        ffn_all.reshape(tensors, shards, -1, width),
        ctxs,
    )
    ffn_came = swap(ffn_far, "shard", 1)
    result_all = lax.all_gather(result, "tensor", axis=0, tiled=True)

    class Path:
        def __init__(self, near, came, order):
            lead = (2,) * len(shard_bits) + near.shape[1:]
            self.dims = list(reversed(shard_bits)) + [("ctx", 1)]
            self.order = list(order)
            self.keep, self.came = near.reshape(lead), came.reshape(lead)

        def fold(self):
            near, came = self.keep, self.came
            if not self.order:
                self.keep = add(near, came)
                return
            dim = self.dims.index(self.order[0])
            self.dims.pop(dim)
            index = (slice(None),) * dim
            self.send = add(near[index + (1,)], came[index + (1,)])
            self.keep = add(near[index + (0,)], came[index + (0,)])

        def go(self):
            axis, bit = self.order.pop(0)
            self.came = swap(self.send, axis, bit)

    high = list(reversed(shard_bits))
    orders = [[("ctx", 1)] + high, high + [("ctx", 1)]]

    dcq, dck, dcv = cross_backward(cross_scalars, cq, ckv, grad_cmix, cross_mix, cross_logs, scale)
    ffn_came = tie(ffn_came, dcq)
    ffn_paths = [Path(ffn_near[i], ffn_came[i], order) for i, order in enumerate(orders)]
    for p in ffn_paths:
        p.fold()
        grad_two = tie(grad_two, p.send, p.keep)
        p.go()
    grad_one, one_grad_low, self_sums, *grad_mixes = before_self(
        info, grad_two, dcq, weight_cq, sum_one, vectors[1:2], dcv, weight_o
    )
    head_grads = grad_mixes[:1] + [swap(grad_mixes[j], "tensor", j) for j in range(1, tensors)]
    mesh_sizes = (shards, ctxs, tensors)
    enc_keep, enc_send = encoder_grad(tie(dck, one_grad_low), dcv, weight_ckv)
    early_sums = jnp.concatenate([feed_sums, self_sums], axis=0)
    early_sums = early_sums + swap(early_sums, "tensor", 1)
    near_a, near_b, far_a, far_b = square_grads(
        info,
        [
            (tie(enc_low, enc_send, early_sums), dck),
            (enc_low, dcv),
            (one_grad_low, self_mix),
            (one_low, dcq),
            (two_grad_low, cross_mix),
        ],
        (2, 3),
        mesh_sizes,
    )
    enc_send, head_grads, far_a, far_b = tie((enc_send, head_grads, far_a, far_b), far_b)
    for _ in range(len(high)):
        for p in ffn_paths:
            p.came = tie(p.came, far_b)
            p.fold()
            head_grads = tie(head_grads, p.send, p.keep)
            p.go()
    enc_came = tie(swap(enc_send, "ctx", 1), *(p.keep for p in ffn_paths))
    enc_mine = (enc_keep + enc_came.astype(F32)).astype(BF16)
    grad_encoder = lax.psum(enc_mine, "tensor")
    for bit in bits_of("tensor")[1:]:
        early_sums = early_sums + tie(swap(early_sums, "tensor", bit), far_b)
    head_grads = tie(head_grads, enc_mine, result_all, early_sums)

    dq, down, dtrunk, late_sums = self_backward(
        scalars, q, kv, kv_sent, head_grads, mixes, self_logs, heads, seg, scale, width
    )
    trunk_came = lax.ppermute(dtrunk, "ctx", [(1, 0)])
    for p in ffn_paths:
        p.came = tie(p.came, dtrunk, grad_encoder)
        p.fold()
    ffn_blocks = jnp.concatenate([p.keep for p in ffn_paths], axis=1)
    ffn_came = [swap(ffn_blocks[j], "tensor", j) for j in range(1, tensors)]
    sums = jnp.concatenate([early_sums, late_sums], axis=0)
    for axis, bit in [("shard", 1)] + shard_bits:
        sums = sums + swap(sums, axis, bit)
    paths = [
        Path(near, tie(swap(far, "shard", 1), ffn_blocks), order)
        for near, far, order in zip((near_a, near_b), (far_a, far_b), orders)
    ]
    for p in paths:
        p.fold()
        trunk_came = tie(trunk_came, p.send, p.keep)
        p.go()
    trunk_came = tie(trunk_came, ffn_blocks, sums)
    *parts, near, far = input_grad(
        info, dq, down, dtrunk, trunk_came, input_low, qkv_weights, mesh_sizes
    )
    part_came = [swap(parts[j], "tensor", j) for j in range(1, tensors)]
    for _ in range(len(high)):
        for p in paths:
            p.came = tie(p.came, parts[0])
            p.fold()
            p.go()
    lead = (2,) * len(shard_bits) + near.shape[1:]
    near, far = near.reshape(lead), swap(far, "shard", 1).reshape(lead)
    send, keep = add(near[1], far[1]), add(near[0], far[0])
    for axis, bit in list(reversed(shard_bits))[:-1]:
        came = swap(send, axis, bit)
        send, keep = add(keep[1], came[1]), add(keep[0], came[0])
    came = swap(send, *shard_bits[0])
    keep = add(keep, came)
    ffn_total = ffn_blocks[0].astype(F32)
    for part in tie(ffn_came, parts[0]):
        ffn_total = ffn_total + part.astype(F32)
    ffn_total = ffn_total.astype(BF16)
    sums_came = swap(tie(sums, parts[0]), "ctx", 1)
    for p in paths:
        p.fold()
    squares = jnp.concatenate([p.keep for p in paths], axis=2)
    square_came = [swap(squares[j], "tensor", j) for j in range(1, tensors)]
    part_came, square_came = tie((part_came, square_came), keep, ffn_total)
    square_total = squares[0].astype(F32)
    for part in square_came:
        square_total = square_total + part.astype(F32)
    square_total = square_total.astype(BF16)
    part_came = tie(part_came, square_total)
    input_mine = grad_one + parts[0]
    for part in part_came:
        input_mine = input_mine + part.astype(F32)
    input_mine = input_mine.astype(BF16)
    input_all = over_tensor(input_mine)
    ctx_came = [swap(a, "ctx", 1) for a in (keep, ffn_total, square_total)]
    ctx_came, sums_came = tie((ctx_came, sums_came), input_mine)
    qkv_came, ffn_came, square_came = ctx_came
    sums = sums + sums_came
    qkv_grads = [add(keep[r], qkv_came[r ^ 1]) for r in range(ctxs)]
    first = me_ctx == 0
    qkv_grads = jnp.concatenate(
        [jnp.where(first, qkv_grads[r], qkv_grads[r ^ 1]) for r in range(ctxs)]
    ).astype(F32)
    grad_q, grad_k, grad_v = (qkv_grads[:, i * columns : (i + 1) * columns] for i in range(3))

    def in_order(mine, other):
        return [
            jnp.where(first, mine, other).astype(F32),
            jnp.where(first, other, mine).astype(F32),
        ]

    share = piece // ctxs
    halves = in_order(ffn_total, ffn_came)
    grad_up = jnp.concatenate([half[:share] for half in halves])
    grad_down = jnp.concatenate([half[share:] for half in halves])
    squares = jnp.concatenate(in_order(square_total, square_came))
    grad_ck, grad_cv, grad_o, grad_cq, grad_co = (
        squares[:, i * columns : (i + 1) * columns] for i in range(5)
    )
    grad_encoder = tie(grad_encoder, input_mine).astype(F32)
    result_all = tie(result_all, input_mine).astype(F32)
    input_all = input_all[:1] + list(tie(input_all[1:], sums, qkv_grads, grad_up, squares))
    grad_input = lay_rows(info, input_all)
    me_tensor = info[2]

    def mine(start, size):
        return lax.dynamic_slice(sums, (start + me_tensor, 0), (1, size)).reshape(-1)

    base = 16 + 8
    later = base + 2 * tensors

    return (
        result_all[None],
        grad_input[None],
        grad_encoder[None],
        grad_q,
        grad_k,
        grad_v,
        grad_o.T,
        grad_cq,
        grad_ck,
        grad_cv,
        grad_co.T,
        grad_up,
        grad_down.T,
        mine(later, columns),
        mine(later + tensors, columns),
        sums[18],
        mine(base, columns),
        mine(base + tensors, columns),
        sums[5],
        mine(8, ffn_upbias.shape[0]),
        sums[2],
        sums[16],
        sums[17],
        sums[3],
        sums[4],
        sums[0],
        sums[1],
    )


def solution(mesh):
    sizes = {axis: mesh.shape[axis] for axis in ("shard", "ctx", "tensor")}
    rows = P("shard", "ctx", None)
    tall, wide = P("shard", "tensor"), P("tensor", "shard")
    mats = (tall, tall, tall, wide, tall, tall, tall, wide, tall, wide)
    part = P("tensor")
    vectors = (part, part, P(), part, part, P(), part) + (P(),) * 7
    tree = P("shard", None)
    return jax.shard_map(
        functools.partial(local, sizes),
        mesh=mesh,
        in_specs=(rows, rows, P("shard"), tree, tree) + mats + vectors + (rows,),
        out_specs=(rows, rows, rows) + mats + vectors,
        check_vma=False,
    )
```

```python
import functools

import jax
import jax.numpy as jnp
from jax import lax
from jax.experimental import pallas as pl
from jax.experimental.pallas import tpu as pltpu
from jax.sharding import PartitionSpec as P

HEAD_DIM = 64
LANES = 128
TILE = 256
NEG = -1e30
EPS = 1e-05
F32 = jnp.float32
BF16 = jnp.bfloat16
VMEM_LIMIT = 56 * 1024 * 1024
WEIGHT = 0.01


def dot_of(a, b, a_dim, b_dim):
    return lax.dot_general(a, b, (((a_dim,), (b_dim,)), ((), ())), preferred_element_type=F32)


def nn(a, b):
    return dot_of(a, b, 1, 0)


def nt(a, b):
    return dot_of(a, b, 1, 1)


def tn(a, b):
    return dot_of(a, b, 0, 0)


def head_lanes(rows, half):
    lane = lax.broadcasted_iota(jnp.int32, (rows, LANES), 1)
    return (lane < HEAD_DIM) if half == 0 else (lane >= HEAD_DIM)


def flags_of(rows, seg):
    lane = lax.broadcasted_iota(jnp.int32, (rows, LANES), 1) % HEAD_DIM
    row = lax.broadcasted_iota(jnp.int32, (rows, LANES), 0)
    return jnp.where(lane == row // seg, 1.0, 0.0).astype(BF16)


def causal_keep(size, seg):
    key = lax.broadcasted_iota(jnp.int32, (size, size), 0)
    query = lax.broadcasted_iota(jnp.int32, (size, size), 1)
    return (key // seg != query // seg) | (key <= query)


def flip(a):
    return a.astype(F32).T.astype(a.dtype)


def lane_pad(a):
    gap = -a.shape[1] % LANES
    return jnp.concatenate([a, jnp.zeros((a.shape[0], gap), a.dtype)], axis=1) if gap else a


def fold_forward(state, queries, key_tile, value_tile, bias_tile, heads, keep):
    out = []
    for h in range(heads):
        g, half = divmod(h, 2)
        lanes = slice(g * LANES, (g + 1) * LANES)
        if half == 0:
            value_rows = flip(value_tile[:, lanes])
        keys = jnp.where(head_lanes(TILE, half), key_tile[:, lanes], bias_tile)
        scores = nt(keys, queries[h])
        if keep is not None:
            scores = jnp.where(keep, scores, NEG)
        peak, total, mix = state[3 * h : 3 * h + 3]
        new_peak = jnp.maximum(peak, jnp.max(scores, axis=0, keepdims=True))
        weights = jnp.exp(scores - new_peak)
        shrink = jnp.exp(peak - new_peak)
        total = total * shrink + jnp.sum(weights, axis=0, keepdims=True)
        mix = mix * shrink + nn(
            value_rows[half * HEAD_DIM : (half + 1) * HEAD_DIM], weights.astype(BF16)
        )
        out += [new_peak, total, mix]
    return tuple(out)


def fresh_state(heads, rows):
    state = []
    for _ in range(heads):
        state += [
            jnp.full((1, rows), NEG, F32),
            jnp.zeros((1, rows), F32),
            jnp.zeros((HEAD_DIM, rows), F32),
        ]
    return tuple(state)


def flagged_queries(q, heads, seg):
    rows = q.shape[0]
    flags = flags_of(rows, seg)
    return [
        jnp.where(head_lanes(rows, h % 2), q[:, (h // 2) * LANES : (h // 2 + 1) * LANES], flags)
        for h in range(heads)
    ]


def mixed(state, heads):
    parts = [state[3 * h + 2] / state[3 * h + 1] for h in range(heads)]
    if heads % 2:
        parts.append(jnp.zeros_like(parts[0]))
    return jnp.concatenate(
        [jnp.concatenate(parts[h : h + 2], axis=0).T for h in range(0, len(parts), 2)], axis=1
    ).astype(BF16)


def put_logs(state, heads, log_ref):
    log_ref[...] = jnp.zeros_like(log_ref)
    for h in range(heads):
        log_ref[h : h + 1, :] = state[3 * h] + jnp.log(state[3 * h + 1])


def ancestors(parent_ref, label, count):
    def step(_, carry):
        at, bits = carry
        found = at >= 0
        safe = jnp.maximum(at, 0)
        return jnp.where(found, parent_ref[safe], at), jnp.where(
            found, bits | (jnp.int32(1) << safe), bits
        )

    return lax.fori_loop(0, count, step, (parent_ref[label], jnp.int32(0)))[1]


def seg_terms(bits, labels, same, seg):
    lane = lax.broadcasted_iota(jnp.int32, (TILE, LANES), 1) % HEAD_DIM
    row = lax.broadcasted_iota(jnp.int32, (TILE, LANES), 0) // seg
    out = jnp.zeros((TILE, LANES), F32)
    for i, mask in enumerate(bits):
        for t, label in enumerate(labels):
            if same and i == t:
                continue
            term = jnp.where(((mask >> label) & 1) == 1, 0.0, NEG)
            out = jnp.where((lane == i) & (row == t), term, out)
    return out.astype(BF16)


def unpack_kv(tile):
    half = tile.shape[1] // 2
    return lane_pad(tile[:, :half]), lane_pad(tile[:, half:])


def fill_trunk(info_ref, own_ref, sent_ref, trunk_ref):
    def fill(ref):
        keys, values = unpack_kv(ref[...])
        trunk_ref[:, : keys.shape[1]] = keys
        trunk_ref[:, keys.shape[1] :] = values

    @pl.when((pl.program_id(0) == 0) & (info_ref[1] == 0))
    def _():
        fill(own_ref)

    @pl.when((pl.program_id(0) == 0) & (info_ref[1] != 0))
    def _():
        fill(sent_ref)


def tile_rows(c):
    return pl.ds(pl.multiple_of(c * TILE, TILE), TILE)


def block_masks(info_ref, parent_ref, label_ref, seg, rows):
    b = pl.program_id(0)
    per = TILE // seg
    first = info_ref[1] * rows + b * TILE
    own = [label_ref[first + i * seg] for i in range(per)]
    bits = [ancestors(parent_ref, label, parent_ref.shape[0]) for label in own]

    def terms(c):
        return seg_terms(bits, [label_ref[c * TILE + t * seg] for t in range(per)], False, seg)

    count = jnp.where(info_ref[1] == 0, b, rows // TILE)
    return seg_terms(bits, own, True, seg), terms, count


def put_slot(slot, value, refs):
    for j, ref in enumerate(refs):

        @pl.when(slot == j)
        def _(ref=ref):
            ref[...] = value.astype(ref.dtype)


def take_slot(slot, refs):
    value = refs[0][...]
    for j, ref in enumerate(refs[1:], 1):
        value = jnp.where(slot == j, ref[...], value)
    return value


def self_forward_kernel(
    info_ref, parent_ref, label_ref, q_ref, own_ref, sent_ref, *rest, heads, seg
):
    mix_refs, (log_ref, trunk_ref) = rest[:-2], rest[-2:]
    b = pl.program_id(0)
    fill_trunk(info_ref, own_ref, sent_ref, trunk_ref)
    width = trunk_ref.shape[1] // 2
    queries = flagged_queries(lane_pad(q_ref[...]), heads, seg)
    own_terms, terms, count = block_masks(
        info_ref, parent_ref, label_ref, seg, own_ref.shape[0]
    )
    keys, values = unpack_kv(own_ref[tile_rows(b), :])
    state = fold_forward(
        fresh_state(heads, TILE), queries, keys, values, own_terms, heads, causal_keep(TILE, seg)
    )

    def body(c, state):
        rows = tile_rows(c)
        return fold_forward(
            state,
            queries,
            trunk_ref[rows, :width],
            trunk_ref[rows, width:],
            terms(c),
            heads,
            None,
        )

    state = lax.fori_loop(0, count, body, state)
    put_logs(state, heads, log_ref)
    put_slot(b ^ info_ref[2], mixed(state, heads)[:, : mix_refs[0].shape[1]], mix_refs)


def params():
    return pltpu.CompilerParams(vmem_limit_bytes=VMEM_LIMIT)


def cost(flops, bytes_accessed, transcendentals=0):
    return pl.CostEstimate(
        flops=int(flops * WEIGHT),
        bytes_accessed=int(bytes_accessed * WEIGHT),
        transcendentals=int(transcendentals * WEIGHT),
    )


def whole(shape):
    return pl.BlockSpec(shape, lambda *_: (0,) * len(shape))


def shape_of(shape, dtype):
    return jax.ShapeDtypeStruct(shape, dtype)


def self_forward(scalars, q, own, sent, tensors, heads, seg):
    rows, columns = q.shape
    blocks = rows // TILE
    width = -(-columns // LANES) * LANES
    return pl.pallas_call(
        functools.partial(self_forward_kernel, heads=heads, seg=seg),
        grid_spec=pltpu.PrefetchScalarGridSpec(
            num_scalar_prefetch=3,
            grid=(blocks,),
            in_specs=[
                pl.BlockSpec((TILE, columns), lambda b, *_: (b, 0)),
                whole(own.shape),
                whole(own.shape),
            ],
            out_specs=[whole((TILE, columns))] * tensors
            + [pl.BlockSpec((8, TILE), lambda b, *_: (0, b))],
            scratch_shapes=[pltpu.VMEM((rows, 2 * width), BF16)],
        ),
        out_shape=[shape_of((TILE, columns), BF16)] * tensors + [shape_of((8, rows), F32)],
        compiler_params=params(),
        cost_estimate=cost(rows * rows * columns * 8, rows * columns * 16, rows * rows * heads),
        name="self_forward",
    )(*scalars, q, own, sent)


def fold_backward(
    queries, plain, grads, logs, deltas, key_tile, value_tile, bias_tile, heads, keep
):
    grad_keys, grad_values, grad_queries = [], [], []
    for h in range(heads):
        g, half = divmod(h, 2)
        lanes = slice(g * LANES, (g + 1) * LANES)
        if half == 0:
            key_rows = flip(key_tile[:, lanes])
        keys = jnp.where(head_lanes(TILE, half), key_tile[:, lanes], bias_tile)
        scores = nt(keys, queries[h])
        if keep is not None:
            scores = jnp.where(keep, scores, NEG)
        probs = jnp.exp(scores - logs[h])
        grad_probs = nt(value_tile[:, lanes], grads[h])
        grad_scores = (probs * (grad_probs - deltas[h])).astype(BF16)
        part_values = nn(probs.astype(BF16), grads[h])
        part_keys = nn(grad_scores, plain[h])
        if half == 0:
            grad_values.append(part_values)
            grad_keys.append(part_keys)
        else:
            grad_values[g] = grad_values[g] + part_values
            grad_keys[g] = grad_keys[g] + part_keys
        grad_queries.append(nn(key_rows[half * HEAD_DIM : (half + 1) * HEAD_DIM], grad_scores))
    return grad_keys, grad_values, tuple(grad_queries)


def backward_sides(q, grad, mix, heads, seg):
    rows = q.shape[0]
    queries = flagged_queries(q, heads, seg)
    plain, grads, deltas = [], [], []
    for h in range(heads):
        g, half = divmod(h, 2)
        lanes = slice(g * LANES, (g + 1) * LANES)
        mask = head_lanes(rows, half)
        plain.append(jnp.where(mask, q[:, lanes], jnp.zeros((), BF16)))
        grads.append(jnp.where(mask, grad[:, lanes], jnp.zeros((), BF16)))
        if half == 0:
            product = (grad[:, lanes].astype(F32) * mix[:, lanes].astype(F32)).T
        deltas.append(
            jnp.sum(product[half * HEAD_DIM : (half + 1) * HEAD_DIM], axis=0, keepdims=True)
        )
    return queries, plain, grads, deltas


def query_grads(grad_queries, scale):
    parts = list(grad_queries)
    if len(parts) % 2:
        parts.append(jnp.zeros_like(parts[0]))
    return (
        jnp.concatenate(
            [jnp.concatenate(parts[h : h + 2], axis=0).T for h in range(0, len(parts), 2)], axis=1
        )
        * scale
    ).astype(BF16)


def self_backward_kernel(
    info_ref, parent_ref, label_ref, q_ref, own_ref, sent_ref, *rest, heads, seg, scale, tensors
):
    grad_refs, mix_refs, rest = rest[:tensors], rest[tensors : 2 * tensors], rest[2 * tensors :]
    log_ref, dq_ref, down_ref, dtrunk_ref, sums_ref, trunk_ref, sum_ref, vector_ref = rest
    b = pl.program_id(0)
    slot = b ^ info_ref[2]
    fill_trunk(info_ref, own_ref, sent_ref, trunk_ref)
    width = trunk_ref.shape[1] // 2
    half_columns = own_ref.shape[1] // 2
    queries, plain, grads, deltas = backward_sides(
        lane_pad(q_ref[...]),
        lane_pad(take_slot(slot, grad_refs)),
        lane_pad(take_slot(slot, mix_refs)),
        heads,
        seg,
    )
    logs = [log_ref[h : h + 1, :] for h in range(heads)]
    own_terms, terms, count = block_masks(
        info_ref, parent_ref, label_ref, seg, own_ref.shape[0]
    )

    @pl.when(b == 0)
    def _():
        sum_ref[...] = jnp.zeros_like(sum_ref)
        vector_ref[...] = jnp.zeros_like(vector_ref)

    keys, values = unpack_kv(own_ref[tile_rows(b), :])
    grad_keys, grad_values, grad_queries = fold_backward(
        queries, plain, grads, logs, deltas, keys, values, own_terms, heads, causal_keep(TILE, seg)
    )
    down_ref[:, :half_columns] = jnp.concatenate(grad_keys, axis=1)[:, :half_columns]
    down_ref[:, half_columns:] = jnp.concatenate(grad_values, axis=1)[:, :half_columns]

    def body(c, grad_queries):
        rows = tile_rows(c)
        grad_keys, grad_values, more = fold_backward(
            queries,
            plain,
            grads,
            logs,
            deltas,
            trunk_ref[rows, :width],
            trunk_ref[rows, width:],
            terms(c),
            heads,
            None,
        )
        for g in range(len(grad_keys)):
            sum_ref[rows, g * LANES : (g + 1) * LANES] += grad_keys[g]
            sum_ref[rows, width + g * LANES : width + (g + 1) * LANES] += grad_values[g]
        return tuple(x + y for x, y in zip(grad_queries, more))

    grad_queries = lax.fori_loop(0, count, body, grad_queries)
    dq = query_grads(grad_queries, scale)[:, :half_columns]
    dq_ref[...] = dq
    vector_ref[0:1, :] += jnp.sum(dq.astype(F32), axis=0, keepdims=True)
    vector_ref[1:2, :] += jnp.sum(down_ref[:, half_columns:], axis=0, keepdims=True)

    @pl.when(b == pl.num_programs(0) - 1)
    def _():
        trunk_sum = jnp.sum(sum_ref[:, width : width + half_columns], axis=0, keepdims=True)
        sums_ref[...] = jnp.zeros_like(sums_ref)
        sums_ref[pl.ds(info_ref[2], 1), :half_columns] = vector_ref[0:1, :]
        sums_ref[pl.ds(tensors + info_ref[2], 1), :half_columns] = (
            vector_ref[1:2, :] + trunk_sum
        )
        dtrunk_ref[:, :half_columns] = sum_ref[:, :half_columns].astype(BF16)
        dtrunk_ref[:, half_columns:] = sum_ref[:, width : width + half_columns].astype(BF16)


def self_backward(scalars, q, own, sent, grads, mixes, logs, heads, seg, scale, model_width):
    rows, columns = q.shape
    blocks = rows // TILE
    width = -(-columns // LANES) * LANES
    tensors = len(grads)
    tile = pl.BlockSpec((TILE, columns), lambda b, *_: (b, 0))
    return pl.pallas_call(
        functools.partial(
            self_backward_kernel, heads=heads, seg=seg, scale=scale, tensors=tensors
        ),
        grid_spec=pltpu.PrefetchScalarGridSpec(
            num_scalar_prefetch=3,
            grid=(blocks,),
            in_specs=[tile, whole(own.shape), whole(own.shape)]
            + [whole((TILE, columns))] * (2 * tensors)
            + [pl.BlockSpec((8, TILE), lambda b, *_: (0, b))],
            out_specs=[
                tile,
                pl.BlockSpec((TILE, 2 * columns), lambda b, *_: (b, 0)),
                whole((rows, 2 * columns)),
                whole((2 * tensors, model_width)),
            ],
            scratch_shapes=[
                pltpu.VMEM((rows, 2 * width), BF16),
                pltpu.VMEM((rows, 2 * width), F32),
                pltpu.VMEM((8, columns), F32),
            ],
        ),
        out_shape=[
            shape_of((rows, columns), BF16),
            shape_of((rows, 2 * columns), F32),
            shape_of((rows, 2 * columns), BF16),
            shape_of((2 * tensors, model_width), F32),
        ],
        compiler_params=params(),
        cost_estimate=cost(rows * rows * columns * 20, rows * columns * 40, rows * rows * heads),
        name="self_backward",
    )(*scalars, q, own, sent, *grads, *mixes, logs)


def length_terms(info_ref, length_ref, c, half_rows):
    row = lax.broadcasted_iota(jnp.int32, (TILE, LANES), 0)
    lane = lax.broadcasted_iota(jnp.int32, (TILE, LANES), 1) % HEAD_DIM
    half, start = divmod(c * TILE, half_rows)
    place = row + ((half ^ info_ref[1]) * half_rows + start)
    return jnp.where((place >= length_ref[0]) & (lane == 0), NEG, 0.0).astype(BF16)


def cross_forward_kernel(info_ref, length_ref, q_ref, k_ref, v_ref, mix_ref, log_ref):
    rows, keys = q_ref.shape[0], k_ref.shape[0]
    queries = flagged_queries(q_ref[...], 2, rows)
    state = fresh_state(2, rows)
    for c in range(keys // TILE):
        part = slice(c * TILE, (c + 1) * TILE)
        terms = length_terms(info_ref, length_ref, c, keys // 2)
        state = fold_forward(state, queries, k_ref[part, :], v_ref[part, :], terms, 2, None)
    put_logs(state, 2, log_ref)
    mix_ref[...] = mixed(state, 2)


def cross_specs(rows, keys, groups):
    part = pl.BlockSpec((rows, LANES), lambda g, *_: (0, g))
    return (
        part,
        pl.BlockSpec((keys, LANES), lambda g, *_: (0, g)),
        pl.BlockSpec((keys, LANES), lambda g, *_: (0, groups + g)),
        pl.BlockSpec((8, rows), lambda g, *_: (g, 0)),
    )


def cross_forward(scalars, q, kv):
    rows, width = q.shape
    keys = kv.shape[0]
    groups = width // LANES
    part, key_side, value_side, log_side = cross_specs(rows, keys, groups)
    return pl.pallas_call(
        cross_forward_kernel,
        grid_spec=pltpu.PrefetchScalarGridSpec(
            num_scalar_prefetch=2,
            grid=(groups,),
            in_specs=[part, key_side, value_side],
            out_specs=[part, log_side],
        ),
        out_shape=[shape_of((rows, width), BF16), shape_of((8 * groups, rows), F32)],
        compiler_params=params(),
        cost_estimate=cost(
            rows * keys * width * 8, (rows + keys) * width * 4, rows * keys * groups * 2
        ),
        name="cross_forward",
    )(*scalars, q, kv, kv)


def cross_backward_kernel(
    info_ref,
    length_ref,
    q_ref,
    k_ref,
    v_ref,
    grad_ref,
    mix_ref,
    log_ref,
    dq_ref,
    dk_ref,
    dv_ref,
    *,
    scale,
):
    rows, keys = q_ref.shape[0], k_ref.shape[0]
    queries, plain, grads, deltas = backward_sides(
        q_ref[...], grad_ref[...], mix_ref[...], 2, rows
    )
    logs = [log_ref[h : h + 1, :] for h in range(2)]
    total = (jnp.zeros((HEAD_DIM, rows), F32),) * 2
    for c in range(keys // TILE):
        part = slice(c * TILE, (c + 1) * TILE)
        terms = length_terms(info_ref, length_ref, c, keys // 2)
        grad_keys, grad_values, more = fold_backward(
            queries, plain, grads, logs, deltas, k_ref[part, :], v_ref[part, :], terms, 2, None
        )
        dk_ref[part, :] = grad_keys[0].astype(BF16)
        dv_ref[part, :] = grad_values[0].astype(BF16)
        total = tuple(x + y for x, y in zip(total, more))
    dq_ref[...] = query_grads(total, scale)


def cross_backward(scalars, q, kv, grad, mix, logs, scale):
    rows, width = q.shape
    keys = kv.shape[0]
    groups = width // LANES
    part, key_side, value_side, log_side = cross_specs(rows, keys, groups)
    return pl.pallas_call(
        functools.partial(cross_backward_kernel, scale=scale),
        grid_spec=pltpu.PrefetchScalarGridSpec(
            num_scalar_prefetch=2,
            grid=(groups,),
            in_specs=[part, key_side, value_side, part, part, log_side],
            out_specs=[part, key_side, key_side],
        ),
        out_shape=[
            shape_of((rows, width), BF16),
            shape_of((keys, width), BF16),
            shape_of((keys, width), BF16),
        ],
        compiler_params=params(),
        cost_estimate=cost(
            rows * keys * width * 20, (rows * 4 + keys * 4) * width * 2, rows * keys * groups * 2
        ),
        name="cross_backward",
    )(*scalars, q, kv, kv, grad, mix, logs)


def norm_parts(values):
    center = values - jnp.mean(values, axis=-1, keepdims=True)
    inverse = lax.rsqrt(jnp.mean(center * center, axis=-1, keepdims=True) + EPS)
    return center * inverse, inverse


def norm_back(pre_sum, gain, grad_out):
    normed, inverse = norm_parts(pre_sum)
    grad_normed = grad_out * gain
    grad_pre = inverse * (
        grad_normed
        - jnp.mean(grad_normed, axis=-1, keepdims=True)
        - normed * jnp.mean(grad_normed * normed, axis=-1, keepdims=True)
    )
    return (
        grad_pre,
        jnp.sum(grad_out * normed, axis=0, keepdims=True),
        jnp.sum(grad_out, axis=0, keepdims=True),
    )


def project_kernel(x_ref, w_ref, qb_ref, vb_ref, q_ref, kv_ref, low_ref, *, scale):
    columns = q_ref.shape[1]
    low = x_ref[0].astype(BF16)
    low_ref[...] = low
    out = nn(low, w_ref[...])
    q_ref[...] = ((out[:, :columns] + qb_ref[...]) * scale).astype(BF16)
    kv_ref[:, :columns] = out[:, columns : 2 * columns].astype(BF16)
    kv_ref[:, columns:] = (out[:, 2 * columns :] + vb_ref[...]).astype(BF16)


def project(x, w, qb, vb, scale):
    _, rows, width = x.shape
    columns = qb.shape[1]
    return pl.pallas_call(
        functools.partial(project_kernel, scale=scale),
        grid=(rows // TILE,),
        in_specs=[
            pl.BlockSpec((1, TILE, width), lambda b: (0, b, 0)),
            whole(w.shape),
            whole(qb.shape),
            whole(vb.shape),
        ],
        out_specs=[
            pl.BlockSpec((TILE, columns), lambda b: (b, 0)),
            pl.BlockSpec((TILE, 2 * columns), lambda b: (b, 0)),
            pl.BlockSpec((TILE, width), lambda b: (b, 0)),
        ],
        out_shape=[
            shape_of((rows, columns), BF16),
            shape_of((rows, 2 * columns), BF16),
            shape_of((rows, width), BF16),
        ],
        compiler_params=params(),
        cost_estimate=cost(rows * width * columns * 6, rows * width * 8),
        name="project",
    )(x, w, qb, vb)


def assemble_kernel(info_ref, near_ref, far_ref, ckv_ref, o_ref, cq_ref, bias_ref):
    tensors, _, columns = o_ref.shape
    width = tensors * columns
    rows = near_ref.shape[2] - bias_ref.shape[1]

    def put(ref):
        for z in range(tensors):
            part = slice(z * columns, (z + 1) * columns)
            late = slice(width + z * columns, width + (z + 1) * columns)
            ckv_ref[:, part] = ref[0, z, :rows, :columns]
            ckv_ref[:, late] = ref[0, z, :rows, columns : 2 * columns]
            o_ref[z] = ref[0, z, :rows, 2 * columns : 3 * columns]
            cq_ref[:, part] = ref[0, z, :rows, 3 * columns :]
        bias_ref[...] = ref[0, :, rows:, :]

    other = (pl.program_id(0) & 1) ^ (info_ref[0] & 1)

    @pl.when(other == 0)
    def _():
        put(near_ref)

    @pl.when(other != 0)
    def _():
        put(far_ref)


def assemble(info, near, far, shards, columns, bias_rows):
    _, tensors, rows, packed = near.shape
    rows -= bias_rows
    width = tensors * columns
    height = shards * rows
    side = pl.BlockSpec((1,) + near.shape[1:], lambda s, i: ((s >> 1) ^ (i[0] >> 1), 0, 0, 0))
    bias = (tensors, bias_rows, packed)
    return pl.pallas_call(
        assemble_kernel,
        grid_spec=pltpu.PrefetchScalarGridSpec(
            num_scalar_prefetch=1,
            grid=(shards,),
            in_specs=[side, side],
            out_specs=[
                pl.BlockSpec((rows, 2 * width), lambda s, i: (s, 0)),
                pl.BlockSpec((tensors, rows, columns), lambda s, i: (0, s, 0)),
                pl.BlockSpec((rows, width), lambda s, i: (s, 0)),
                whole(bias),
            ],
        ),
        out_shape=[
            shape_of((height, 2 * width), BF16),
            shape_of((tensors, height, columns), BF16),
            shape_of((height, width), BF16),
            shape_of(bias, BF16),
        ],
        compiler_params=params(),
        cost_estimate=cost(0, near.size * 8),
        name="assemble",
    )(info, near, far)


def bias_part(bias_ref, j, start, columns):
    width = bias_ref.shape[2]
    row, lane = divmod(start, width)
    tall = bias_ref[j].astype(F32)
    full = tall[:2] + tall[2:4]
    if lane + columns <= width:
        return full[row : row + 1, lane : lane + columns]
    return jnp.concatenate(
        [full[row : row + 1, lane:], full[row + 1 : row + 2, : lane + columns - width]], axis=1
    )


def tensor_row(bias_ref, start, columns):
    return jnp.concatenate(
        [bias_part(bias_ref, j, start, columns) for j in range(bias_ref.shape[0])], axis=1
    )


def after_self_kernel(
    info_ref, x_ref, o_ref, cq_ref, ob_ref, gain_ref, shift_ref, bias_ref, *rest, scale
):
    mix_refs, (sum_ref, low_ref, q_ref, joined_ref) = rest[:-4], rest[-4:]
    joined_ref[...] = jnp.concatenate([mix_ref[...] for mix_ref in mix_refs], axis=1)
    total = x_ref[0] + ob_ref[...]
    for j, mix_ref in enumerate(mix_refs):
        total = total + nt(mix_ref[...], o_ref[j])
    sum_ref[...] = total
    hidden = norm_parts(total)[0] * gain_ref[...] + shift_ref[...]
    low = hidden.astype(BF16)
    low_ref[...] = low
    bias = tensor_row(bias_ref, 0, mix_refs[0].shape[1])
    q_ref[...] = ((nn(low, cq_ref[...]) + bias) * scale).astype(BF16)


def after_self(info, x, o, cq, ob, gain, shift, bias, mixes, scale):
    width = x.shape[2]
    rows = mixes[0].shape[0]
    return pl.pallas_call(
        functools.partial(after_self_kernel, scale=scale),
        grid_spec=pltpu.PrefetchScalarGridSpec(
            num_scalar_prefetch=1,
            grid=(1,),
            in_specs=[pl.BlockSpec((1, rows, width), lambda s, i: (0, i[2], 0))]
            + [whole(a.shape) for a in (o, cq, ob, gain, shift, bias) + tuple(mixes)],
            out_specs=[whole((rows, width))] * 4,
        ),
        out_shape=[shape_of((rows, width), F32)] + [shape_of((rows, width), BF16)] * 3,
        compiler_params=params(),
        cost_estimate=cost(rows * width * width * 4, width * width * 4 + rows * width * 12),
        name="after_self",
    )(info, x, o, cq, ob, gain, shift, bias, *mixes)


def encode_kernel(info_ref, own_ref, sent_ref, w_ref, bias_ref, low_ref, kv_ref, *, columns):
    width = low_ref.shape[1]
    half = pl.num_programs(0) // 2

    @pl.when(pl.program_id(0) < half)
    def _():
        low_ref[...] = own_ref[0].astype(BF16)

    @pl.when(pl.program_id(0) >= half)
    def _():
        low_ref[...] = sent_ref[...]

    out = nn(low_ref[...], w_ref[...])
    kv_ref[:, :width] = out[:, :width].astype(BF16)
    kv_ref[:, width:] = (
        out[:, width:] + tensor_row(bias_ref, columns, columns)
    ).astype(BF16)


def encode(info, own, sent, w, bias, columns):
    _, rows, width = own.shape
    half = rows // TILE
    return pl.pallas_call(
        functools.partial(encode_kernel, columns=columns),
        grid_spec=pltpu.PrefetchScalarGridSpec(
            num_scalar_prefetch=1,
            grid=(2 * half,),
            in_specs=[
                pl.BlockSpec((1, TILE, width), lambda b, i: (0, jnp.minimum(b, half - 1), 0)),
                pl.BlockSpec((TILE, width), lambda b, i: (jnp.maximum(b - half, 0), 0)),
                whole(w.shape),
                whole(bias.shape),
            ],
            out_specs=[
                pl.BlockSpec((TILE, width), lambda b, i: (b, 0)),
                pl.BlockSpec((TILE, 2 * width), lambda b, i: (b, 0)),
            ],
        ),
        out_shape=[shape_of((2 * rows, width), BF16), shape_of((2 * rows, 2 * width), BF16)],
        compiler_params=params(),
        cost_estimate=cost(rows * width * width * 8, rows * width * 14),
        name="encode",
    )(info, own, sent, w, bias)


def gelu_parts(values):
    half = 0.5 * (1.0 + lax.erf(values * (0.5**0.5)))
    slope = half + values * (jnp.exp(-0.5 * values * values) * (0.5 / jnp.pi) ** 0.5)
    return values * half, slope


def feed_kernel(
    info_ref,
    sum_ref,
    vectors_ref,
    mix_ref,
    packed_ref,
    bias_ref,
    goal_ref,
    w_ref,
    result_ref,
    near_ref,
    far_ref,
    grad_ref,
    grad_low_ref,
    grad_mix_ref,
    sums_ref,
    two_ref,
    low_ref,
    low_t_ref,
    act_ref,
    slope_ref,
    acc_ref,
    three_low_ref,
    three_t_ref,
    co_ref,
):
    phase, z = pl.program_id(0), pl.program_id(1)
    tensors = pl.num_programs(1)
    rows, width = sum_ref.shape
    hidden_units = w_ref.shape[3]
    piece = width // w_ref.shape[1]
    up = w_ref[0, :, :piece].reshape(width, hidden_units)
    down = w_ref[0, :, piece : 2 * piece].reshape(width, hidden_units)
    gain1, shift1, cob, gain2, shift2, downb, gain3, shift3 = (
        vectors_ref[i : i + 1, :] for i in range(1, 9)
    )

    @pl.when((phase == 0) & (z == 0))
    def _():
        _, shards, chunk, _ = packed_ref.shape
        columns = co_ref.shape[2]
        for t in range(co_ref.shape[0]):
            for s in range(shards):
                for i in range(piece // chunk):
                    start = s * piece + i * chunk
                    co_ref[t, start : start + chunk, :] = packed_ref[
                        t, s, :, i * columns : (i + 1) * columns
                    ]
        hidden_one = norm_parts(sum_ref[...])[0] * gain1 + shift1
        sum_two = hidden_one + cob
        for j in range(co_ref.shape[0]):
            part = mix_ref[:, j * columns : (j + 1) * columns]
            sum_two = sum_two + nt(part, co_ref[info_ref[2] ^ j])
        two_ref[...] = sum_two
        hidden_two = norm_parts(sum_two)[0] * gain2 + shift2
        low_ref[...] = hidden_two.astype(BF16)
        low_t_ref[...] = hidden_two.T.astype(BF16)
        acc_ref[...] = hidden_two + downb
        sums_ref[...] = jnp.zeros_like(sums_ref)

    @pl.when(phase == 0)
    def _():
        bias = bias_part(bias_ref, z ^ info_ref[2], 2 * co_ref.shape[2], hidden_units)
        pre = nn(low_ref[...], up) + bias
        value, slope = gelu_parts(pre)
        act = value.astype(BF16)
        act_ref[z] = act
        slope_ref[z] = slope
        acc_ref[...] += nt(act, down)

    @pl.when((phase == 0) & (z == tensors - 1))
    def _():
        sum_three = acc_ref[...]
        result = norm_parts(sum_three)[0] * gain3 + shift3
        result_ref[...] = result.astype(BF16)
        grad_three, *both = norm_back(sum_three, gain3, goal_ref[0])
        sums_ref[0:1, :] = both[0]
        sums_ref[1:2, :] = both[1]
        sums_ref[2:3, :] = jnp.sum(grad_three, axis=0, keepdims=True)
        acc_ref[...] = grad_three
        three_low_ref[...] = grad_three.astype(BF16)
        three_t_ref[...] = grad_three.T.astype(BF16)

    @pl.when(phase == 1)
    def _():
        grad_pre = nn(three_low_ref[...], down) * slope_ref[z]
        sums_ref[pl.ds(8 + z, 1), :hidden_units] = jnp.sum(grad_pre, axis=0, keepdims=True)
        pre_low = grad_pre.astype(BF16)
        acc_ref[...] += nt(pre_low, up)
        products = (
            nn(low_t_ref[...], pre_low).astype(BF16),
            nn(three_t_ref[...], act_ref[z]).astype(BF16),
        )
        _, _, ctxs, _, share, _ = near_ref.shape

        def put(core):
            for mat, product in enumerate(products):
                for s in range(w_ref.shape[1]):
                    ref = near_ref if (s & 1) == core else far_ref
                    for c in range(ctxs):
                        start = s * piece + c * share
                        ref[mat, (s >> 1) ^ (info_ref[0] >> 1), c ^ info_ref[1], 0] = product[
                            start : start + share
                        ]

        @pl.when((info_ref[0] & 1) == 0)
        def _():
            put(0)

        @pl.when((info_ref[0] & 1) != 0)
        def _():
            put(1)

    @pl.when((phase == 1) & (z == tensors - 1))
    def _():
        grad_two, *both = norm_back(two_ref[...], gain2, acc_ref[...])
        sums_ref[3:4, :] = both[0]
        sums_ref[4:5, :] = both[1]
        sums_ref[5:6, :] = jnp.sum(grad_two, axis=0, keepdims=True)
        grad_ref[...] = grad_two
        low = grad_two.astype(BF16)
        grad_low_ref[...] = low
        columns = co_ref.shape[2]
        for j in range(co_ref.shape[0]):
            part = nn(low, co_ref[info_ref[2] ^ j]).astype(BF16)
            grad_mix_ref[:, j * columns : (j + 1) * columns] = part


def feed(info, sum_one, vectors, mix, columns, chunk, bias, goal, w, ctxs):
    rows, width = sum_one.shape
    tensors, shards, taller, hidden_units = w.shape
    piece = width // shards
    assert hidden_units == width
    grads = (2, shards // 2, ctxs, tensors, piece // ctxs, hidden_units)
    grads_spec = pl.BlockSpec(
        grads[:3] + (1,) + grads[4:], lambda p, z, i: (0, 0, 0, (p * z) ^ i[2], 0, 0)
    )
    head = (sum_one, vectors, mix)
    last = 2 * piece // chunk
    return pl.pallas_call(
        feed_kernel,
        grid_spec=pltpu.PrefetchScalarGridSpec(
            num_scalar_prefetch=1,
            grid=(2, tensors),
            in_specs=[whole(a.shape) for a in head]
            + [
                pl.BlockSpec(
                    (tensors, shards, chunk, hidden_units), lambda p, z, i: (0, 0, last, 0)
                ),
                whole(bias.shape),
                pl.BlockSpec((1, rows, width), lambda p, z, i: (0, i[2], 0)),
                pl.BlockSpec((1, shards, taller, hidden_units), lambda p, z, i: (z, 0, 0, 0)),
            ],
            out_specs=[
                whole((rows, width)),
                grads_spec,
                grads_spec,
                whole((rows, width)),
                whole((rows, width)),
                whole((rows, width)),
                whole((16, width)),
            ],
            scratch_shapes=[
                pltpu.VMEM((rows, width), F32),
                pltpu.VMEM((rows, width), BF16),
                pltpu.VMEM((width, rows), BF16),
                pltpu.VMEM((tensors, rows, hidden_units), BF16),
                pltpu.VMEM((tensors, rows, hidden_units), F32),
                pltpu.VMEM((rows, width), F32),
                pltpu.VMEM((rows, width), BF16),
                pltpu.VMEM((width, rows), BF16),
                pltpu.VMEM((tensors, width, columns), BF16),
            ],
        ),
        out_shape=[
            shape_of((rows, width), BF16),
            shape_of(grads, BF16),
            shape_of(grads, BF16),
            shape_of((rows, width), F32),
            shape_of((rows, width), BF16),
            shape_of((rows, width), BF16),
            shape_of((16, width), F32),
        ],
        compiler_params=params(),
        cost_estimate=cost(rows * w.size * 6, w.size * 6, rows * width * tensors * 2),
        name="feed",
    )(info, *head, w, bias, goal, w)


def before_self_kernel(
    info_ref, grad_ref, dq_ref, cq_ref, sum_ref, gain_ref, dv_ref, o_ref, *out_refs
):
    grad_one_ref, low_ref, sums_ref = out_refs[:3]
    mix_refs = out_refs[3:]
    tensors, _, columns = o_ref.shape
    grad_hidden = grad_ref[...] + nt(dq_ref[...], cq_ref[...])
    grad_one, gain, shift = norm_back(sum_ref[...], gain_ref[...], grad_hidden)
    grad_one_ref[...] = grad_one
    low = grad_one.astype(BF16)
    low_ref[...] = low
    for j, mix_ref in enumerate(mix_refs):
        mix_ref[...] = nn(low, o_ref[j]).astype(BF16)
    sums_ref[...] = jnp.zeros_like(sums_ref)
    sums_ref[0:1, :] = gain
    sums_ref[1:2, :] = shift
    sums_ref[2:3, :] = jnp.sum(grad_one, axis=0, keepdims=True)
    queries = jnp.sum(dq_ref[...].astype(F32), axis=0, keepdims=True)
    values = jnp.sum(dv_ref[...].astype(F32), axis=0, keepdims=True)
    for j in range(tensors):
        part = slice(j * columns, (j + 1) * columns)
        at = info_ref[2] ^ j
        sums_ref[pl.ds(8 + at, 1), :columns] = queries[:, part]
        sums_ref[pl.ds(8 + tensors + at, 1), :columns] = values[:, part]


def before_self(info, grad, dq, cq, sum_one, gain, dv, o):
    rows, width = grad.shape
    tensors, _, columns = o.shape
    args = (grad, dq, cq, sum_one, gain, dv, o)
    return pl.pallas_call(
        before_self_kernel,
        grid_spec=pltpu.PrefetchScalarGridSpec(
            num_scalar_prefetch=1,
            grid=(1,),
            in_specs=[whole(a.shape) for a in args],
            out_specs=[whole((rows, width))] * 2
            + [whole((8 + 2 * tensors, width))]
            + [whole((rows, columns))] * tensors,
        ),
        out_shape=[
            shape_of((rows, width), F32),
            shape_of((rows, width), BF16),
            shape_of((8 + 2 * tensors, width), F32),
        ]
        + [shape_of((rows, columns), BF16)] * tensors,
        compiler_params=params(),
        cost_estimate=cost(rows * width * width * 4, width * width * 6 + rows * width * 14),
        name="before_self",
    )(info, *args)


def encoder_grad_kernel(dk_ref, dv_ref, w_ref, keep_ref, send_ref):
    width = dk_ref.shape[1]
    part = nt(dk_ref[...], w_ref[:, :width]) + nt(dv_ref[...], w_ref[:, width:])
    half = pl.num_programs(0) // 2

    @pl.when(pl.program_id(0) < half)
    def _():
        send_ref[...] = part.astype(BF16)

    @pl.when(pl.program_id(0) >= half)
    def _():
        keep_ref[...] = part


def encoder_grad(dk, dv, w):
    keys, width = dk.shape
    half = keys // TILE // 2
    side = pl.BlockSpec((TILE, width), lambda b: (jnp.where(b < half, b + half, b - half), 0))
    return pl.pallas_call(
        encoder_grad_kernel,
        grid=(2 * half,),
        in_specs=[side, side, whole(w.shape)],
        out_specs=[
            pl.BlockSpec((TILE, width), lambda b: (jnp.maximum(b - half, 0), 0)),
            pl.BlockSpec((TILE, width), lambda b: (jnp.minimum(b, half - 1), 0)),
        ],
        out_shape=[shape_of((keys // 2, width), F32), shape_of((keys // 2, width), BF16)],
        compiler_params=params(),
        cost_estimate=cost(keys * width * width * 4, keys * width * 10),
        name="encoder_grad",
    )(dk, dv, w)


def square_grads_kernel(info_ref, *refs, ctxs, groups):
    count = sum(groups)
    left_refs, right_refs = refs[:count], refs[count : 2 * count]
    flipped = refs[-count:]
    outs = refs[2 * count : -count]
    i, other = pl.program_id(0), pl.program_id(1)
    _, _, tensors, share, packed = outs[0].shape
    piece = share * ctxs
    columns = packed // groups[0]

    @pl.when((i == 0) & (other == 0))
    def _():
        for left_ref, flipped_ref in zip(left_refs, flipped):
            flipped_ref[...] = flip(left_ref[...])

    s = ((i ^ (info_ref[0] >> 1)) << 1) + ((info_ref[0] & 1) ^ other)
    rows = pl.ds(pl.multiple_of(s * piece, piece), piece)
    grads = [
        nn(flipped_ref[rows, :], right_ref[...]).astype(BF16)
        for flipped_ref, right_ref in zip(flipped, right_refs)
    ]

    def put(refs):
        for z in range(tensors):
            part = slice(z * columns, (z + 1) * columns)
            start = 0
            for ref, size in zip(refs, groups):
                tile = jnp.concatenate(
                    [grad[:, part] for grad in grads[start : start + size]], axis=1
                )
                start += size
                for r in range(ctxs):
                    chosen = tile[:share]
                    for c in range(1, ctxs):
                        chosen = jnp.where(
                            (info_ref[1] ^ r) == c, tile[c * share : (c + 1) * share], chosen
                        )
                    ref[0, r, z] = chosen

    @pl.when(other == 0)
    def _():
        put(outs[: len(groups)])

    @pl.when(other != 0)
    def _():
        put(outs[len(groups) :])


def square_grads(info, pairs, groups, sizes):
    shards, ctxs, tensors = sizes
    width = pairs[0][0].shape[1]
    share = width // shards // ctxs
    args = [left for left, _ in pairs] + [right for _, right in pairs]
    sides = [
        (shards // 2, ctxs, tensors, share, size * width // tensors) for size in groups
    ] * 2
    return pl.pallas_call(
        functools.partial(square_grads_kernel, ctxs=ctxs, groups=groups),
        grid_spec=pltpu.PrefetchScalarGridSpec(
            num_scalar_prefetch=1,
            grid=(shards // 2, 2),
            in_specs=[whole(a.shape) for a in args],
            out_specs=[
                pl.BlockSpec((1,) + side[1:], lambda i, c, n: (i, 0, 0, 0, 0)) for side in sides
            ],
            scratch_shapes=[pltpu.VMEM((width, left.shape[0]), BF16) for left, _ in pairs],
        ),
        out_shape=[shape_of(side, BF16) for side in sides],
        compiler_params=params(),
        cost_estimate=cost(2 * width * sum(a.size for a in args), width * width * 8),
        name="square_grads",
    )(info, *args)


def input_grad_kernel(
    info_ref, dq_ref, down_ref, dtrunk_ref, came_ref, low_ref, w_ref, *rest, ctxs, tensors
):
    part_refs = rest[:tensors]
    near_ref, far_ref, dw_ref = rest[tensors:]
    b = pl.program_id(0)

    @pl.when(b == 0)
    def _():
        dw_ref[...] = jnp.zeros_like(dw_ref)

    trunk = dtrunk_ref[...].astype(F32) + came_ref[...].astype(F32)
    dkv = (down_ref[...] + jnp.where(info_ref[1] == 0, trunk, 0.0)).astype(BF16)
    grads = jnp.concatenate([dq_ref[...], dkv], axis=1)
    dw_ref[...] += tn(low_ref[...], grads)
    put_slot(b ^ info_ref[2], nt(grads, w_ref[...]), part_refs)

    @pl.when(b == pl.num_programs(0) - 1)
    def _():
        halves, _, share, _ = near_ref.shape
        for other, ref in ((0, near_ref), (1, far_ref)):
            for i in range(halves):
                s = ((i ^ (info_ref[0] >> 1)) << 1) + ((info_ref[0] & 1) ^ other)
                for r in range(ctxs):
                    start = (s * ctxs + (info_ref[1] ^ r)) * share
                    ref[i, r] = dw_ref[pl.ds(pl.multiple_of(start, share), share), :].astype(BF16)


def input_grad(info, dq, down, dtrunk, came, low, w, sizes):
    shards, ctxs, tensors = sizes
    rows, columns = dq.shape
    width = low.shape[1]
    share = width // shards // ctxs
    side = (shards // 2, ctxs, share, 3 * columns)

    def tile(n):
        return pl.BlockSpec((TILE, n), lambda b, i: (b, 0))

    return pl.pallas_call(
        functools.partial(input_grad_kernel, ctxs=ctxs, tensors=tensors),
        grid_spec=pltpu.PrefetchScalarGridSpec(
            num_scalar_prefetch=1,
            grid=(rows // TILE,),
            in_specs=[
                tile(columns),
                tile(2 * columns),
                tile(2 * columns),
                tile(2 * columns),
                tile(width),
                whole(w.shape),
            ],
            out_specs=[whole((TILE, width))] * tensors
            + [whole(side), whole(side)],
            scratch_shapes=[pltpu.VMEM((width, 3 * columns), F32)],
        ),
        out_shape=[shape_of((TILE, width), F32)]
        + [shape_of((TILE, width), BF16)] * (tensors - 1)
        + [shape_of(side, BF16)] * 2,
        compiler_params=params(),
        cost_estimate=cost(rows * width * columns * 12, rows * width * 14),
        name="input_grad",
    )(info, dq, down, dtrunk, came, low, w)


def lay_rows_kernel(info_ref, *refs):
    in_refs, out_ref = refs[:-1], refs[-1]
    out_ref[...] = take_slot(pl.program_id(0) ^ info_ref[2], in_refs).astype(F32)


def lay_rows(info, parts):
    rows, width = parts[0].shape
    return pl.pallas_call(
        lay_rows_kernel,
        grid_spec=pltpu.PrefetchScalarGridSpec(
            num_scalar_prefetch=1,
            grid=(len(parts),),
            in_specs=[whole((rows, width))] * len(parts),
            out_specs=pl.BlockSpec((rows, width), lambda b, i: (b, 0)),
        ),
        out_shape=shape_of((rows * len(parts), width), F32),
        compiler_params=params(),
        cost_estimate=cost(0, rows * width * len(parts) * 6),
        name="lay_rows",
    )(info, *parts)


def local(sizes, *args):
    (
        layer_input,
        encoder_out,
        enc_length,
        parent_ids,
        token_segment,
        self_query,
        self_key,
        self_value,
        self_output,
        cross_query,
        cross_key,
        cross_value,
        cross_output,
        ffn_up,
        ffn_down,
        self_qbias,
        self_vbias,
        self_obias,
        cross_qbias,
        cross_vbias,
        cross_obias,
        ffn_upbias,
        ffn_downbias,
        norm1_gain,
        norm1_shift,
        norm2_gain,
        norm2_shift,
        norm3_gain,
        norm3_shift,
        out_grad,
    ) = args
    shards, ctxs, tensors = sizes["shard"], sizes["ctx"], sizes["tensor"]
    me_ctx = lax.axis_index("ctx")
    info = jnp.stack([lax.axis_index("shard"), me_ctx, lax.axis_index("tensor")]).astype(jnp.int32)
    scale = HEAD_DIM ** (-0.5)
    local_rows, width = layer_input.shape[1:]
    piece, columns = self_query.shape
    heads = columns // HEAD_DIM
    seg = token_segment.shape[1] // parent_ids.shape[1]
    assert local_rows == tensors * TILE and ctxs == 2

    def bits_of(axis):
        return [1 << k for k in range(sizes[axis].bit_length() - 1)]

    def swap(a, axis, bit):
        return lax.ppermute(a, axis, [(i, i ^ bit) for i in range(sizes[axis])])

    shard_bits = [("shard", 1 << k) for k in range(1, shards.bit_length() - 1)]

    def over_tensor(a):
        return [a] + [swap(a, "tensor", j) for j in range(1, tensors)]

    def grow(a, axis, bit, *others):
        return jnp.stack(tie([a, swap(a, axis, bit)], *others))

    def add(a, b):
        return (a.astype(F32) + b.astype(F32)).astype(BF16)

    def reduce_levels(near, far):
        came = swap(far, "shard", 1)
        lead = (2,) * len(shard_bits) + near.shape[1:]
        near, came = near.reshape(lead), came.reshape(lead)

        for axis, bit in list(reversed(shard_bits)) + [("ctx", 1)]:
            send = add(near[1], came[1])
            near, came = add(near[0], came[0]), swap(send, axis, bit)
        return add(near, came)

    def join_ctx(mine):
        other = swap(mine, "ctx", 1)
        first = me_ctx == 0
        return jnp.concatenate([jnp.where(first, mine, other), jnp.where(first, other, mine)])

    def row(vector):
        return vector.reshape(1, -1)

    def tie(a, *others):
        return lax.optimization_barrier((a,) + others)[0]

    vectors = jnp.stack(
        [
            self_obias,
            norm1_gain,
            norm1_shift,
            cross_obias,
            norm2_gain,
            norm2_shift,
            ffn_downbias,
            norm3_gain,
            norm3_shift,
        ]
    )

    pack = tensors if piece % (16 * tensors) == 0 else 1
    chunk = piece // pack
    packed_co = jnp.concatenate(
        [cross_output.T[i * chunk : (i + 1) * chunk] for i in range(pack)], axis=1
    )
    packed_co = jnp.pad(packed_co, ((0, 0), (0, width - packed_co.shape[1])))
    ffn_piece = jnp.concatenate([ffn_up, ffn_down.T, packed_co], axis=0)
    bias = jnp.concatenate([cross_qbias, cross_vbias, ffn_upbias])
    bias = jnp.pad(bias, (0, -bias.shape[0] % width)).reshape(-1, width)
    bias_high = lax.reduce_precision(bias, 8, 7)
    bias_rows = 16
    bias = jnp.concatenate([bias_high, bias - bias_high]).astype(BF16)
    bias = jnp.pad(bias, ((0, bias_rows - bias.shape[0]), (0, 0)))
    squares = over_tensor(
        jnp.concatenate(
            [
                jnp.concatenate([cross_key, cross_value, self_output.T, cross_query], axis=1),
                bias,
            ],
            axis=0,
        )
    )
    enc_sent = swap(encoder_out[0].astype(BF16), "ctx", 1)
    qkv_weights = lax.all_gather(
        jnp.concatenate([self_query, self_key, self_value], axis=1), "shard", axis=0, tiled=True
    )

    scalars = (info, parent_ids[0], token_segment[0])
    q, kv, input_low = project(layer_input, qkv_weights, row(self_qbias), row(self_vbias), scale)
    squares = jnp.stack(tie(squares, q))
    ffn_all = lax.all_gather(tie(ffn_piece, squares), ("tensor", "shard"), axis=0, tiled=True)
    kv_sent = lax.ppermute(tie(kv, squares), "ctx", [(0, 1)])
    for axis, bit in shard_bits[:-1]:
        squares = grow(squares, axis, bit, kv_sent)
    kv_sent = tie(kv_sent, squares)
    *mixes, self_logs = self_forward(scalars, q, kv, kv_sent, tensors, heads, seg)
    squares = grow(squares, *shard_bits[-1], self_logs)
    near = squares.reshape((shards // 2,) + squares.shape[-3:])
    far = swap(near, "shard", 1)
    all_heads = mixes[:1] + [swap(mixes[j], "tensor", j) for j in range(1, tensors)]
    weight_ckv, weight_o, weight_cq, bias = assemble(info, near, far, shards, columns, bias_rows)
    enc_low, ckv = encode(info, encoder_out, enc_sent, weight_ckv, bias, columns)
    all_heads = all_heads[:1] + list(tie(all_heads[1:], ckv))
    sum_one, one_low, cq, self_mix = after_self(
        info,
        layer_input,
        weight_o,
        weight_cq,
        vectors[0:1],
        vectors[1:2],
        vectors[2:3],
        bias,
        all_heads,
        scale,
    )

    cross_scalars = (info, enc_length)
    cross_mix, cross_logs = cross_forward(cross_scalars, cq, ckv)

    result, ffn_near, ffn_far, grad_two, two_grad_low, grad_cmix, feed_sums = feed(
        info,
        sum_one,
        vectors,
        cross_mix,
        columns,
        chunk,
        bias,
        out_grad,
        ffn_all.reshape(tensors, shards, -1, width),
        ctxs,
    )
    ffn_came = swap(ffn_far, "shard", 1)
    result_all = lax.all_gather(result, "tensor", axis=0, tiled=True)

    class Path:
        def __init__(self, near, came, order):
            lead = (2,) * len(shard_bits) + near.shape[1:]
            self.dims = list(reversed(shard_bits)) + [("ctx", 1)]
            self.order = list(order)
            self.keep, self.came = near.reshape(lead), came.reshape(lead)

        def fold(self):
            near, came = self.keep, self.came
            if not self.order:
                self.keep = add(near, came)
                return
            dim = self.dims.index(self.order[0])
            self.dims.pop(dim)
            index = (slice(None),) * dim
            self.send = add(near[index + (1,)], came[index + (1,)])
            self.keep = add(near[index + (0,)], came[index + (0,)])

        def go(self):
            axis, bit = self.order.pop(0)
            self.came = swap(self.send, axis, bit)

    high = list(reversed(shard_bits))
    orders = [[("ctx", 1)] + high, high + [("ctx", 1)]]

    dcq, dck, dcv = cross_backward(cross_scalars, cq, ckv, grad_cmix, cross_mix, cross_logs, scale)
    enc_keep, enc_send = encoder_grad(dck, dcv, weight_ckv)
    enc_came = swap(enc_send, "ctx", 1)
    grad_two = tie(grad_two, enc_send)
    grad_one, one_grad_low, self_sums, *grad_mixes = before_self(
        info, grad_two, dcq, weight_cq, sum_one, vectors[1:2], dcv, weight_o
    )
    head_grads = grad_mixes[:1] + [swap(grad_mixes[j], "tensor", j) for j in range(1, tensors)]
    mesh_sizes = (shards, ctxs, tensors)
    early_sums = jnp.concatenate([feed_sums, self_sums], axis=0)
    early_sums = early_sums + swap(early_sums, "tensor", 1)
    ffn_came = tie(ffn_came, one_grad_low)
    ffn_paths = [Path(ffn_near[i], ffn_came[i], order) for i, order in enumerate(orders)]
    sends = []
    for p in ffn_paths:
        p.fold()
        sends += [p.send, p.keep]
        p.go()
    enc_mine = (enc_keep + tie(enc_came, *sends).astype(F32)).astype(BF16)
    grad_encoder = lax.psum(enc_mine, "tensor")
    near_a, near_b, far_a, far_b = square_grads(
        info,
        [
            (tie(enc_low, early_sums, enc_mine, result_all), dck),
            (enc_low, dcv),
            (one_grad_low, self_mix),
            (one_low, dcq),
            (two_grad_low, cross_mix),
        ],
        (2, 3),
        mesh_sizes,
    )
    head_grads, far_a, far_b = tie((head_grads, far_a, far_b), far_b)
    for _ in range(len(high)):
        for p in ffn_paths:
            p.came = tie(p.came, far_b)
            p.fold()
            head_grads = tie(head_grads, p.send, p.keep)
            p.go()
    sums_came = [swap(early_sums, "tensor", bit) for bit in bits_of("tensor")[1:2]]

    dq, down, dtrunk, late_sums = self_backward(
        scalars, q, kv, kv_sent, head_grads, mixes, self_logs, heads, seg, scale, width
    )
    trunk_came = lax.ppermute(dtrunk, "ctx", [(1, 0)])
    paths = [
        Path(near, tie(swap(far, "shard", 1), dtrunk), order)
        for near, far, order in zip((near_a, near_b), (far_a, far_b), orders)
    ]
    for p in paths:
        p.fold()
        trunk_came = tie(trunk_came, p.send, p.keep)
        p.go()
    for p in ffn_paths:
        p.came = tie(p.came, dtrunk, grad_encoder, *(q.keep for q in paths))
        p.fold()
    ffn_blocks = jnp.concatenate([p.keep for p in ffn_paths], axis=1)
    ffn_came = [swap(ffn_blocks[j], "tensor", j) for j in range(1, tensors)]
    for came in tie(sums_came, dtrunk):
        early_sums = early_sums + came
    for bit in bits_of("tensor")[2:]:
        early_sums = early_sums + swap(early_sums, "tensor", bit)
    sums = jnp.concatenate([early_sums, late_sums], axis=0)
    for axis, bit in [("shard", 1)] + shard_bits:
        sums = sums + swap(sums, axis, bit)
    trunk_came = tie(trunk_came, ffn_blocks, sums)
    *parts, near, far = input_grad(
        info, dq, down, dtrunk, trunk_came, input_low, qkv_weights, mesh_sizes
    )
    part_came = [swap(parts[j], "tensor", j) for j in range(1, tensors)]
    for _ in range(len(high)):
        for p in paths:
            p.came = tie(p.came, parts[0])
            p.fold()
            p.go()
    lead = (2,) * len(shard_bits) + near.shape[1:]
    near, far = near.reshape(lead), swap(far, "shard", 1).reshape(lead)
    send, keep = add(near[1], far[1]), add(near[0], far[0])
    for axis, bit in list(reversed(shard_bits))[:-1]:
        came = swap(send, axis, bit)
        send, keep = add(keep[1], came[1]), add(keep[0], came[0])
    came = swap(send, *shard_bits[0])
    keep = add(keep, came)
    ffn_total = ffn_blocks[0].astype(F32)
    for part in tie(ffn_came, parts[0]):
        ffn_total = ffn_total + part.astype(F32)
    ffn_total = ffn_total.astype(BF16)
    sums_came = swap(tie(sums, parts[0]), "ctx", 1)
    for p in paths:
        p.fold()
    squares = jnp.concatenate([p.keep for p in paths], axis=2)
    square_came = [swap(squares[j], "tensor", j) for j in range(1, tensors)]
    part_came, square_came = tie((part_came, square_came), keep, ffn_total)
    square_total = squares[0].astype(F32)
    for part in square_came:
        square_total = square_total + part.astype(F32)
    square_total = square_total.astype(BF16)
    part_came = tie(part_came, square_total)
    input_mine = grad_one + parts[0]
    for part in part_came:
        input_mine = input_mine + part.astype(F32)
    input_mine = input_mine.astype(BF16)
    input_all = over_tensor(input_mine)
    ctx_came = [swap(a, "ctx", 1) for a in (keep, ffn_total, square_total)]
    ctx_came, sums_came = tie((ctx_came, sums_came), input_mine)
    qkv_came, ffn_came, square_came = ctx_came
    sums = sums + sums_came
    qkv_grads = [add(keep[r], qkv_came[r ^ 1]) for r in range(ctxs)]
    first = me_ctx == 0
    qkv_grads = jnp.concatenate(
        [jnp.where(first, qkv_grads[r], qkv_grads[r ^ 1]) for r in range(ctxs)]
    ).astype(F32)
    grad_q, grad_k, grad_v = (qkv_grads[:, i * columns : (i + 1) * columns] for i in range(3))

    def in_order(mine, other):
        return [
            jnp.where(first, mine, other).astype(F32),
            jnp.where(first, other, mine).astype(F32),
        ]

    share = piece // ctxs
    halves = in_order(ffn_total, ffn_came)
    grad_up = jnp.concatenate([half[:share] for half in halves])
    grad_down = jnp.concatenate([half[share:] for half in halves])
    squares = jnp.concatenate(in_order(square_total, square_came))
    grad_ck, grad_cv, grad_o, grad_cq, grad_co = (
        squares[:, i * columns : (i + 1) * columns] for i in range(5)
    )
    grad_encoder = tie(grad_encoder, input_all[1]).astype(F32)
    result_all = tie(result_all, input_all[1]).astype(F32)
    input_all = input_all[:1] + list(tie(input_all[1:], sums, qkv_grads, grad_up, squares))
    grad_input = lay_rows(info, input_all)
    me_tensor = info[2]

    def mine(start, size):
        return lax.dynamic_slice(sums, (start + me_tensor, 0), (1, size)).reshape(-1)

    base = 16 + 8
    later = base + 2 * tensors

    return (
        result_all[None],
        grad_input[None],
        grad_encoder[None],
        grad_q,
        grad_k,
        grad_v,
        grad_o.T,
        grad_cq,
        grad_ck,
        grad_cv,
        grad_co.T,
        grad_up,
        grad_down.T,
        mine(later, columns),
        mine(later + tensors, columns),
        sums[18],
        mine(base, columns),
        mine(base + tensors, columns),
        sums[5],
        mine(8, ffn_upbias.shape[0]),
        sums[2],
        sums[16],
        sums[17],
        sums[3],
        sums[4],
        sums[0],
        sums[1],
    )


def solution(mesh):
    sizes = {axis: mesh.shape[axis] for axis in ("shard", "ctx", "tensor")}
    rows = P("shard", "ctx", None)
    tall, wide = P("shard", "tensor"), P("tensor", "shard")
    mats = (tall, tall, tall, wide, tall, tall, tall, wide, tall, wide)
    part = P("tensor")
    vectors = (part, part, P(), part, part, P(), part) + (P(),) * 7
    tree = P("shard", None)
    return jax.shard_map(
        functools.partial(local, sizes),
        mesh=mesh,
        in_specs=(rows, rows, P("shard"), tree, tree) + mats + vectors + (rows,),
        out_specs=(rows, rows, rows) + mats + vectors,
        check_vma=False,
    )
```

```python
import functools

import jax
import jax.numpy as jnp
from jax import lax
from jax.experimental import pallas as pl
from jax.experimental.pallas import tpu as pltpu
from jax.sharding import PartitionSpec as P

HEAD_DIM = 64
LANES = 128
TILE = 256
NEG = -1e30
EPS = 1e-05
F32 = jnp.float32
BF16 = jnp.bfloat16
VMEM_LIMIT = 56 * 1024 * 1024
WEIGHT = 0.01


def dot_of(a, b, a_dim, b_dim):
    return lax.dot_general(a, b, (((a_dim,), (b_dim,)), ((), ())), preferred_element_type=F32)


def nn(a, b):
    return dot_of(a, b, 1, 0)


def nt(a, b):
    return dot_of(a, b, 1, 1)


def tn(a, b):
    return dot_of(a, b, 0, 0)


def head_lanes(rows, half):
    lane = lax.broadcasted_iota(jnp.int32, (rows, LANES), 1)
    return (lane < HEAD_DIM) if half == 0 else (lane >= HEAD_DIM)


def flags_of(rows, seg):
    lane = lax.broadcasted_iota(jnp.int32, (rows, LANES), 1) % HEAD_DIM
    row = lax.broadcasted_iota(jnp.int32, (rows, LANES), 0)
    return jnp.where(lane == row // seg, 1.0, 0.0).astype(BF16)


def causal_keep(size, seg):
    key = lax.broadcasted_iota(jnp.int32, (size, size), 0)
    query = lax.broadcasted_iota(jnp.int32, (size, size), 1)
    return (key // seg != query // seg) | (key <= query)


def flip(a):
    return a.astype(F32).T.astype(a.dtype)


def lane_pad(a):
    gap = -a.shape[1] % LANES
    return jnp.concatenate([a, jnp.zeros((a.shape[0], gap), a.dtype)], axis=1) if gap else a


def fold_forward(state, queries, key_tile, value_tile, bias_tile, heads, keep):
    out = []
    for h in range(heads):
        g, half = divmod(h, 2)
        lanes = slice(g * LANES, (g + 1) * LANES)
        if half == 0:
            value_rows = flip(value_tile[:, lanes])
        keys = jnp.where(head_lanes(key_tile.shape[0], half), key_tile[:, lanes], bias_tile)
        scores = nt(keys, queries[h])
        if keep is not None:
            scores = jnp.where(keep, scores, NEG)
        peak, total, mix = state[3 * h : 3 * h + 3]
        new_peak = jnp.maximum(peak, jnp.max(scores, axis=0, keepdims=True))
        weights = jnp.exp(scores - new_peak)
        shrink = jnp.exp(peak - new_peak)
        total = total * shrink + jnp.sum(weights, axis=0, keepdims=True)
        mix = mix * shrink + nn(
            value_rows[half * HEAD_DIM : (half + 1) * HEAD_DIM], weights.astype(BF16)
        )
        out += [new_peak, total, mix]
    return tuple(out)


def fresh_state(heads, rows):
    state = []
    for _ in range(heads):
        state += [
            jnp.full((1, rows), NEG, F32),
            jnp.zeros((1, rows), F32),
            jnp.zeros((HEAD_DIM, rows), F32),
        ]
    return tuple(state)


def flagged_queries(q, heads, seg):
    rows = q.shape[0]
    flags = flags_of(rows, seg)
    return [
        jnp.where(head_lanes(rows, h % 2), q[:, (h // 2) * LANES : (h // 2 + 1) * LANES], flags)
        for h in range(heads)
    ]


def mixed(state, heads):
    parts = [state[3 * h + 2] / state[3 * h + 1] for h in range(heads)]
    if heads % 2:
        parts.append(jnp.zeros_like(parts[0]))
    return jnp.concatenate(
        [jnp.concatenate(parts[h : h + 2], axis=0).T for h in range(0, len(parts), 2)], axis=1
    ).astype(BF16)


def put_logs(state, heads, log_ref):
    log_ref[...] = jnp.zeros_like(log_ref)
    for h in range(heads):
        log_ref[h : h + 1, :] = state[3 * h] + jnp.log(state[3 * h + 1])


def ancestors(parent_ref, label, count):
    def step(_, carry):
        at, bits = carry
        found = at >= 0
        safe = jnp.maximum(at, 0)
        return jnp.where(found, parent_ref[safe], at), jnp.where(
            found, bits | (jnp.int32(1) << safe), bits
        )

    return lax.fori_loop(0, count, step, (parent_ref[label], jnp.int32(0)))[1]


def seg_terms(bits, labels, same, seg):
    lane = lax.broadcasted_iota(jnp.int32, (TILE, LANES), 1) % HEAD_DIM
    row = lax.broadcasted_iota(jnp.int32, (TILE, LANES), 0) // seg
    out = jnp.zeros((TILE, LANES), F32)
    for i, mask in enumerate(bits):
        for t, label in enumerate(labels):
            if same and i == t:
                continue
            term = jnp.where(((mask >> label) & 1) == 1, 0.0, NEG)
            out = jnp.where((lane == i) & (row == t), term, out)
    return out.astype(BF16)


def unpack_kv(tile):
    half = tile.shape[1] // 2
    return lane_pad(tile[:, :half]), lane_pad(tile[:, half:])


def fill_trunk(info_ref, own_ref, sent_ref, trunk_ref):
    def fill(ref):
        keys, values = unpack_kv(ref[...])
        trunk_ref[:, : keys.shape[1]] = keys
        trunk_ref[:, keys.shape[1] :] = values

    @pl.when((pl.program_id(0) == 0) & (info_ref[1] == 0))
    def _():
        fill(own_ref)

    @pl.when((pl.program_id(0) == 0) & (info_ref[1] != 0))
    def _():
        fill(sent_ref)


def tile_rows(c):
    return pl.ds(pl.multiple_of(c * TILE, TILE), TILE)


def block_masks(info_ref, parent_ref, label_ref, seg, rows):
    b = pl.program_id(0)
    per = TILE // seg
    first = info_ref[1] * rows + b * TILE
    own = [label_ref[first + i * seg] for i in range(per)]
    bits = [ancestors(parent_ref, label, parent_ref.shape[0]) for label in own]

    def terms(c):
        return seg_terms(bits, [label_ref[c * TILE + t * seg] for t in range(per)], False, seg)

    count = jnp.where(info_ref[1] == 0, b, rows // TILE)
    return seg_terms(bits, own, True, seg), terms, count


def put_slot(slot, value, refs):
    for j, ref in enumerate(refs):

        @pl.when(slot == j)
        def _(ref=ref):
            ref[...] = value.astype(ref.dtype)


def take_slot(slot, refs):
    value = refs[0][...]
    for j, ref in enumerate(refs[1:], 1):
        value = jnp.where(slot == j, ref[...], value)
    return value


def self_forward_kernel(
    info_ref, parent_ref, label_ref, q_ref, own_ref, sent_ref, *rest, heads, seg
):
    mix_refs, (log_ref, trunk_ref) = rest[:-2], rest[-2:]
    b = pl.program_id(0)
    fill_trunk(info_ref, own_ref, sent_ref, trunk_ref)
    width = trunk_ref.shape[1] // 2
    queries = flagged_queries(lane_pad(q_ref[...]), heads, seg)
    own_terms, terms, count = block_masks(
        info_ref, parent_ref, label_ref, seg, own_ref.shape[0]
    )
    keys, values = unpack_kv(own_ref[tile_rows(b), :])
    state = fold_forward(
        fresh_state(heads, TILE), queries, keys, values, own_terms, heads, causal_keep(TILE, seg)
    )

    def body(c, state):
        rows = tile_rows(c)
        return fold_forward(
            state,
            queries,
            trunk_ref[rows, :width],
            trunk_ref[rows, width:],
            terms(c),
            heads,
            None,
        )

    def all_at_once(state):
        every = jnp.concatenate([terms(c) for c in range(trunk_ref.shape[0] // TILE)], axis=0)
        return fold_forward(
            state, queries, trunk_ref[:, :width], trunk_ref[:, width:], every, heads, None
        )

    state = lax.cond(
        count == trunk_ref.shape[0] // TILE,
        all_at_once,
        lambda state: lax.fori_loop(0, count, body, state),
        state,
    )
    put_logs(state, heads, log_ref)
    put_slot(b ^ info_ref[2], mixed(state, heads)[:, : mix_refs[0].shape[1]], mix_refs)


def params():
    return pltpu.CompilerParams(vmem_limit_bytes=VMEM_LIMIT)


def cost(flops, bytes_accessed, transcendentals=0):
    return pl.CostEstimate(
        flops=int(flops * WEIGHT),
        bytes_accessed=int(bytes_accessed * WEIGHT),
        transcendentals=int(transcendentals * WEIGHT),
    )


def whole(shape):
    return pl.BlockSpec(shape, lambda *_: (0,) * len(shape))


def shape_of(shape, dtype):
    return jax.ShapeDtypeStruct(shape, dtype)


def self_forward(scalars, q, own, sent, tensors, heads, seg):
    rows, columns = q.shape
    blocks = rows // TILE
    width = -(-columns // LANES) * LANES
    return pl.pallas_call(
        functools.partial(self_forward_kernel, heads=heads, seg=seg),
        grid_spec=pltpu.PrefetchScalarGridSpec(
            num_scalar_prefetch=3,
            grid=(blocks,),
            in_specs=[
                pl.BlockSpec((TILE, columns), lambda b, *_: (b, 0)),
                whole(own.shape),
                whole(own.shape),
            ],
            out_specs=[whole((TILE, columns))] * tensors
            + [pl.BlockSpec((8, TILE), lambda b, *_: (0, b))],
            scratch_shapes=[pltpu.VMEM((rows, 2 * width), BF16)],
        ),
        out_shape=[shape_of((TILE, columns), BF16)] * tensors + [shape_of((8, rows), F32)],
        compiler_params=params(),
        cost_estimate=cost(rows * rows * columns * 8, rows * columns * 16, rows * rows * heads),
        name="self_forward",
    )(*scalars, q, own, sent)


def fold_backward(
    queries, plain, grads, logs, deltas, key_tile, value_tile, bias_tile, heads, keep
):
    grad_keys, grad_values, grad_queries = [], [], []
    for h in range(heads):
        g, half = divmod(h, 2)
        lanes = slice(g * LANES, (g + 1) * LANES)
        if half == 0:
            key_rows = flip(key_tile[:, lanes])
        keys = jnp.where(head_lanes(key_tile.shape[0], half), key_tile[:, lanes], bias_tile)
        scores = nt(keys, queries[h])
        if keep is not None:
            scores = jnp.where(keep, scores, NEG)
        probs = jnp.exp(scores - logs[h])
        grad_probs = nt(value_tile[:, lanes], grads[h])
        grad_scores = (probs * (grad_probs - deltas[h])).astype(BF16)
        part_values = nn(probs.astype(BF16), grads[h])
        part_keys = nn(grad_scores, plain[h])
        if half == 0:
            grad_values.append(part_values)
            grad_keys.append(part_keys)
        else:
            grad_values[g] = grad_values[g] + part_values
            grad_keys[g] = grad_keys[g] + part_keys
        grad_queries.append(nn(key_rows[half * HEAD_DIM : (half + 1) * HEAD_DIM], grad_scores))
    return grad_keys, grad_values, tuple(grad_queries)


def backward_sides(q, grad, mix, heads, seg):
    rows = q.shape[0]
    queries = flagged_queries(q, heads, seg)
    plain, grads, deltas = [], [], []
    for h in range(heads):
        g, half = divmod(h, 2)
        lanes = slice(g * LANES, (g + 1) * LANES)
        mask = head_lanes(rows, half)
        plain.append(jnp.where(mask, q[:, lanes], jnp.zeros((), BF16)))
        grads.append(jnp.where(mask, grad[:, lanes], jnp.zeros((), BF16)))
        if half == 0:
            product = (grad[:, lanes].astype(F32) * mix[:, lanes].astype(F32)).T
        deltas.append(
            jnp.sum(product[half * HEAD_DIM : (half + 1) * HEAD_DIM], axis=0, keepdims=True)
        )
    return queries, plain, grads, deltas


def query_grads(grad_queries, scale):
    parts = list(grad_queries)
    if len(parts) % 2:
        parts.append(jnp.zeros_like(parts[0]))
    return (
        jnp.concatenate(
            [jnp.concatenate(parts[h : h + 2], axis=0).T for h in range(0, len(parts), 2)], axis=1
        )
        * scale
    ).astype(BF16)


def self_backward_kernel(
    info_ref, parent_ref, label_ref, q_ref, own_ref, sent_ref, *rest, heads, seg, scale, tensors
):
    grad_refs, mix_refs, rest = rest[:tensors], rest[tensors : 2 * tensors], rest[2 * tensors :]
    log_ref, dq_ref, down_ref, dtrunk_ref, sums_ref, trunk_ref, sum_ref, vector_ref = rest
    b = pl.program_id(0)
    slot = b ^ info_ref[2]
    fill_trunk(info_ref, own_ref, sent_ref, trunk_ref)
    width = trunk_ref.shape[1] // 2
    half_columns = own_ref.shape[1] // 2
    queries, plain, grads, deltas = backward_sides(
        lane_pad(q_ref[...]),
        lane_pad(take_slot(slot, grad_refs)),
        lane_pad(take_slot(slot, mix_refs)),
        heads,
        seg,
    )
    logs = [log_ref[h : h + 1, :] for h in range(heads)]
    own_terms, terms, count = block_masks(
        info_ref, parent_ref, label_ref, seg, own_ref.shape[0]
    )

    @pl.when(b == 0)
    def _():
        sum_ref[...] = jnp.zeros_like(sum_ref)
        vector_ref[...] = jnp.zeros_like(vector_ref)

    keys, values = unpack_kv(own_ref[tile_rows(b), :])
    grad_keys, grad_values, grad_queries = fold_backward(
        queries, plain, grads, logs, deltas, keys, values, own_terms, heads, causal_keep(TILE, seg)
    )
    down_ref[:, :half_columns] = jnp.concatenate(grad_keys, axis=1)[:, :half_columns]
    down_ref[:, half_columns:] = jnp.concatenate(grad_values, axis=1)[:, :half_columns]

    def body(c, grad_queries):
        rows = tile_rows(c)
        grad_keys, grad_values, more = fold_backward(
            queries,
            plain,
            grads,
            logs,
            deltas,
            trunk_ref[rows, :width],
            trunk_ref[rows, width:],
            terms(c),
            heads,
            None,
        )
        for g in range(len(grad_keys)):
            sum_ref[rows, g * LANES : (g + 1) * LANES] += grad_keys[g]
            sum_ref[rows, width + g * LANES : width + (g + 1) * LANES] += grad_values[g]
        return tuple(x + y for x, y in zip(grad_queries, more))

    def all_at_once(grad_queries):
        every = jnp.concatenate([terms(c) for c in range(trunk_ref.shape[0] // TILE)], axis=0)
        grad_keys, grad_values, more = fold_backward(
            queries,
            plain,
            grads,
            logs,
            deltas,
            trunk_ref[:, :width],
            trunk_ref[:, width:],
            every,
            heads,
            None,
        )
        for g in range(len(grad_keys)):
            sum_ref[:, g * LANES : (g + 1) * LANES] += grad_keys[g]
            sum_ref[:, width + g * LANES : width + (g + 1) * LANES] += grad_values[g]
        return tuple(x + y for x, y in zip(grad_queries, more))

    grad_queries = lax.cond(
        count == trunk_ref.shape[0] // TILE,
        all_at_once,
        lambda grad_queries: lax.fori_loop(0, count, body, grad_queries),
        grad_queries,
    )
    dq = query_grads(grad_queries, scale)[:, :half_columns]
    dq_ref[...] = dq
    vector_ref[0:1, :] += jnp.sum(dq.astype(F32), axis=0, keepdims=True)
    vector_ref[1:2, :] += jnp.sum(down_ref[:, half_columns:], axis=0, keepdims=True)

    @pl.when(b == pl.num_programs(0) - 1)
    def _():
        trunk_sum = jnp.sum(sum_ref[:, width : width + half_columns], axis=0, keepdims=True)
        sums_ref[...] = jnp.zeros_like(sums_ref)
        sums_ref[pl.ds(info_ref[2], 1), :half_columns] = vector_ref[0:1, :]
        sums_ref[pl.ds(tensors + info_ref[2], 1), :half_columns] = (
            vector_ref[1:2, :] + trunk_sum
        )
        dtrunk_ref[:, :half_columns] = sum_ref[:, :half_columns].astype(BF16)
        dtrunk_ref[:, half_columns:] = sum_ref[:, width : width + half_columns].astype(BF16)


def self_backward(scalars, q, own, sent, grads, mixes, logs, heads, seg, scale, model_width):
    rows, columns = q.shape
    blocks = rows // TILE
    width = -(-columns // LANES) * LANES
    tensors = len(grads)
    tile = pl.BlockSpec((TILE, columns), lambda b, *_: (b, 0))
    return pl.pallas_call(
        functools.partial(
            self_backward_kernel, heads=heads, seg=seg, scale=scale, tensors=tensors
        ),
        grid_spec=pltpu.PrefetchScalarGridSpec(
            num_scalar_prefetch=3,
            grid=(blocks,),
            in_specs=[tile, whole(own.shape), whole(own.shape)]
            + [whole((TILE, columns))] * (2 * tensors)
            + [pl.BlockSpec((8, TILE), lambda b, *_: (0, b))],
            out_specs=[
                tile,
                pl.BlockSpec((TILE, 2 * columns), lambda b, *_: (b, 0)),
                whole((rows, 2 * columns)),
                whole((2 * tensors, model_width)),
            ],
            scratch_shapes=[
                pltpu.VMEM((rows, 2 * width), BF16),
                pltpu.VMEM((rows, 2 * width), F32),
                pltpu.VMEM((8, columns), F32),
            ],
        ),
        out_shape=[
            shape_of((rows, columns), BF16),
            shape_of((rows, 2 * columns), F32),
            shape_of((rows, 2 * columns), BF16),
            shape_of((2 * tensors, model_width), F32),
        ],
        compiler_params=params(),
        cost_estimate=cost(rows * rows * columns * 20, rows * columns * 40, rows * rows * heads),
        name="self_backward",
    )(*scalars, q, own, sent, *grads, *mixes, logs)


def length_terms(info_ref, length_ref, keys):
    row = lax.broadcasted_iota(jnp.int32, (keys, LANES), 0)
    lane = lax.broadcasted_iota(jnp.int32, (keys, LANES), 1) % HEAD_DIM
    half = keys // 2
    place = jnp.where(row < half, row + info_ref[1] * half, row - info_ref[1] * half)
    return jnp.where((place >= length_ref[0]) & (lane == 0), NEG, 0.0).astype(BF16)


def cross_forward_kernel(info_ref, length_ref, q_ref, k_ref, v_ref, mix_ref, log_ref):
    rows, keys = q_ref.shape[0], k_ref.shape[0]
    queries = flagged_queries(q_ref[...], 2, rows)
    terms = length_terms(info_ref, length_ref, keys)
    state = fold_forward(
        fresh_state(2, rows), queries, k_ref[...], v_ref[...], terms, 2, None
    )
    put_logs(state, 2, log_ref)
    mix_ref[...] = mixed(state, 2)


def cross_specs(rows, keys, groups):
    part = pl.BlockSpec((rows, LANES), lambda g, *_: (0, g))
    return (
        part,
        pl.BlockSpec((keys, LANES), lambda g, *_: (0, g)),
        pl.BlockSpec((keys, LANES), lambda g, *_: (0, groups + g)),
        pl.BlockSpec((8, rows), lambda g, *_: (g, 0)),
    )


def cross_forward(scalars, q, kv):
    rows, width = q.shape
    keys = kv.shape[0]
    groups = width // LANES
    part, key_side, value_side, log_side = cross_specs(rows, keys, groups)
    return pl.pallas_call(
        cross_forward_kernel,
        grid_spec=pltpu.PrefetchScalarGridSpec(
            num_scalar_prefetch=2,
            grid=(groups,),
            in_specs=[part, key_side, value_side],
            out_specs=[part, log_side],
        ),
        out_shape=[shape_of((rows, width), BF16), shape_of((8 * groups, rows), F32)],
        compiler_params=params(),
        cost_estimate=cost(
            rows * keys * width * 8, (rows + keys) * width * 4, rows * keys * groups * 2
        ),
        name="cross_forward",
    )(*scalars, q, kv, kv)


def cross_backward_kernel(
    info_ref,
    length_ref,
    q_ref,
    k_ref,
    v_ref,
    grad_ref,
    mix_ref,
    log_ref,
    dq_ref,
    dk_ref,
    dv_ref,
    *,
    scale,
):
    rows, keys = q_ref.shape[0], k_ref.shape[0]
    queries, plain, grads, deltas = backward_sides(
        q_ref[...], grad_ref[...], mix_ref[...], 2, rows
    )
    logs = [log_ref[h : h + 1, :] for h in range(2)]
    terms = length_terms(info_ref, length_ref, keys)
    grad_keys, grad_values, total = fold_backward(
        queries, plain, grads, logs, deltas, k_ref[...], v_ref[...], terms, 2, None
    )
    dk_ref[...] = grad_keys[0].astype(BF16)
    dv_ref[...] = grad_values[0].astype(BF16)
    dq_ref[...] = query_grads(total, scale)


def cross_backward(scalars, q, kv, grad, mix, logs, scale):
    rows, width = q.shape
    keys = kv.shape[0]
    groups = width // LANES
    part, key_side, value_side, log_side = cross_specs(rows, keys, groups)
    return pl.pallas_call(
        functools.partial(cross_backward_kernel, scale=scale),
        grid_spec=pltpu.PrefetchScalarGridSpec(
            num_scalar_prefetch=2,
            grid=(groups,),
            in_specs=[part, key_side, value_side, part, part, log_side],
            out_specs=[part, key_side, key_side],
        ),
        out_shape=[
            shape_of((rows, width), BF16),
            shape_of((keys, width), BF16),
            shape_of((keys, width), BF16),
        ],
        compiler_params=params(),
        cost_estimate=cost(
            rows * keys * width * 20, (rows * 4 + keys * 4) * width * 2, rows * keys * groups * 2
        ),
        name="cross_backward",
    )(*scalars, q, kv, kv, grad, mix, logs)


def norm_parts(values):
    center = values - jnp.mean(values, axis=-1, keepdims=True)
    inverse = lax.rsqrt(jnp.mean(center * center, axis=-1, keepdims=True) + EPS)
    return center * inverse, inverse


def norm_back(pre_sum, gain, grad_out):
    normed, inverse = norm_parts(pre_sum)
    grad_normed = grad_out * gain
    grad_pre = inverse * (
        grad_normed
        - jnp.mean(grad_normed, axis=-1, keepdims=True)
        - normed * jnp.mean(grad_normed * normed, axis=-1, keepdims=True)
    )
    return (
        grad_pre,
        jnp.sum(grad_out * normed, axis=0, keepdims=True),
        jnp.sum(grad_out, axis=0, keepdims=True),
    )


def project_kernel(x_ref, w_ref, qb_ref, vb_ref, q_ref, kv_ref, low_ref, *, scale):
    columns = q_ref.shape[1]
    low = x_ref[0].astype(BF16)
    low_ref[...] = low
    out = nn(low, w_ref[...])
    q_ref[...] = ((out[:, :columns] + qb_ref[...]) * scale).astype(BF16)
    kv_ref[:, :columns] = out[:, columns : 2 * columns].astype(BF16)
    kv_ref[:, columns:] = (out[:, 2 * columns :] + vb_ref[...]).astype(BF16)


def project(x, w, qb, vb, scale):
    _, rows, width = x.shape
    columns = qb.shape[1]
    return pl.pallas_call(
        functools.partial(project_kernel, scale=scale),
        grid=(rows // TILE,),
        in_specs=[
            pl.BlockSpec((1, TILE, width), lambda b: (0, b, 0)),
            whole(w.shape),
            whole(qb.shape),
            whole(vb.shape),
        ],
        out_specs=[
            pl.BlockSpec((TILE, columns), lambda b: (b, 0)),
            pl.BlockSpec((TILE, 2 * columns), lambda b: (b, 0)),
            pl.BlockSpec((TILE, width), lambda b: (b, 0)),
        ],
        out_shape=[
            shape_of((rows, columns), BF16),
            shape_of((rows, 2 * columns), BF16),
            shape_of((rows, width), BF16),
        ],
        compiler_params=params(),
        cost_estimate=cost(rows * width * columns * 6, rows * width * 8),
        name="project",
    )(x, w, qb, vb)


def assemble_kernel(info_ref, near_ref, far_ref, ckv_ref, o_ref, cq_ref, bias_ref):
    tensors, _, columns = o_ref.shape
    width = tensors * columns
    rows = near_ref.shape[2] - bias_ref.shape[1]

    def put(ref):
        for z in range(tensors):
            part = slice(z * columns, (z + 1) * columns)
            late = slice(width + z * columns, width + (z + 1) * columns)
            ckv_ref[:, part] = ref[0, z, :rows, :columns]
            ckv_ref[:, late] = ref[0, z, :rows, columns : 2 * columns]
            o_ref[z] = ref[0, z, :rows, 2 * columns : 3 * columns]
            cq_ref[:, part] = ref[0, z, :rows, 3 * columns :]
        bias_ref[...] = ref[0, :, rows:, :]

    other = (pl.program_id(0) & 1) ^ (info_ref[0] & 1)

    @pl.when(other == 0)
    def _():
        put(near_ref)

    @pl.when(other != 0)
    def _():
        put(far_ref)


def assemble(info, near, far, shards, columns, bias_rows):
    _, tensors, rows, packed = near.shape
    rows -= bias_rows
    width = tensors * columns
    height = shards * rows
    side = pl.BlockSpec((1,) + near.shape[1:], lambda s, i: ((s >> 1) ^ (i[0] >> 1), 0, 0, 0))
    bias = (tensors, bias_rows, packed)
    return pl.pallas_call(
        assemble_kernel,
        grid_spec=pltpu.PrefetchScalarGridSpec(
            num_scalar_prefetch=1,
            grid=(shards,),
            in_specs=[side, side],
            out_specs=[
                pl.BlockSpec((rows, 2 * width), lambda s, i: (s, 0)),
                pl.BlockSpec((tensors, rows, columns), lambda s, i: (0, s, 0)),
                pl.BlockSpec((rows, width), lambda s, i: (s, 0)),
                whole(bias),
            ],
        ),
        out_shape=[
            shape_of((height, 2 * width), BF16),
            shape_of((tensors, height, columns), BF16),
            shape_of((height, width), BF16),
            shape_of(bias, BF16),
        ],
        compiler_params=params(),
        cost_estimate=cost(0, near.size * 8),
        name="assemble",
    )(info, near, far)


def bias_part(bias_ref, j, start, columns):
    width = bias_ref.shape[2]
    row, lane = divmod(start, width)
    tall = bias_ref[j].astype(F32)
    full = tall[:2] + tall[2:4]
    if lane + columns <= width:
        return full[row : row + 1, lane : lane + columns]
    return jnp.concatenate(
        [full[row : row + 1, lane:], full[row + 1 : row + 2, : lane + columns - width]], axis=1
    )


def tensor_row(bias_ref, start, columns):
    return jnp.concatenate(
        [bias_part(bias_ref, j, start, columns) for j in range(bias_ref.shape[0])], axis=1
    )


def after_self_kernel(
    info_ref, x_ref, o_ref, cq_ref, ob_ref, gain_ref, shift_ref, bias_ref, *rest, scale
):
    mix_refs, (sum_ref, low_ref, q_ref, joined_ref) = rest[:-4], rest[-4:]
    joined_ref[...] = jnp.concatenate([mix_ref[...] for mix_ref in mix_refs], axis=1)
    total = x_ref[0] + ob_ref[...]
    for j, mix_ref in enumerate(mix_refs):
        total = total + nt(mix_ref[...], o_ref[j])
    sum_ref[...] = total
    hidden = norm_parts(total)[0] * gain_ref[...] + shift_ref[...]
    low = hidden.astype(BF16)
    low_ref[...] = low
    bias = tensor_row(bias_ref, 0, mix_refs[0].shape[1])
    q_ref[...] = ((nn(low, cq_ref[...]) + bias) * scale).astype(BF16)


def after_self(info, x, o, cq, ob, gain, shift, bias, mixes, scale):
    width = x.shape[2]
    rows = mixes[0].shape[0]
    return pl.pallas_call(
        functools.partial(after_self_kernel, scale=scale),
        grid_spec=pltpu.PrefetchScalarGridSpec(
            num_scalar_prefetch=1,
            grid=(1,),
            in_specs=[pl.BlockSpec((1, rows, width), lambda s, i: (0, i[2], 0))]
            + [whole(a.shape) for a in (o, cq, ob, gain, shift, bias) + tuple(mixes)],
            out_specs=[whole((rows, width))] * 4,
        ),
        out_shape=[shape_of((rows, width), F32)] + [shape_of((rows, width), BF16)] * 3,
        compiler_params=params(),
        cost_estimate=cost(rows * width * width * 4, width * width * 4 + rows * width * 12),
        name="after_self",
    )(info, x, o, cq, ob, gain, shift, bias, *mixes)


def encode_kernel(info_ref, own_ref, sent_ref, w_ref, bias_ref, low_ref, kv_ref, *, columns):
    width = low_ref.shape[1]
    half = pl.num_programs(0) // 2

    @pl.when(pl.program_id(0) < half)
    def _():
        low_ref[...] = own_ref[0].astype(BF16)

    @pl.when(pl.program_id(0) >= half)
    def _():
        low_ref[...] = sent_ref[...]

    out = nn(low_ref[...], w_ref[...])
    kv_ref[:, :width] = out[:, :width].astype(BF16)
    kv_ref[:, width:] = (
        out[:, width:] + tensor_row(bias_ref, columns, columns)
    ).astype(BF16)


def encode(info, own, sent, w, bias, columns):
    _, rows, width = own.shape
    half = rows // TILE
    return pl.pallas_call(
        functools.partial(encode_kernel, columns=columns),
        grid_spec=pltpu.PrefetchScalarGridSpec(
            num_scalar_prefetch=1,
            grid=(2 * half,),
            in_specs=[
                pl.BlockSpec((1, TILE, width), lambda b, i: (0, jnp.minimum(b, half - 1), 0)),
                pl.BlockSpec((TILE, width), lambda b, i: (jnp.maximum(b - half, 0), 0)),
                whole(w.shape),
                whole(bias.shape),
            ],
            out_specs=[
                pl.BlockSpec((TILE, width), lambda b, i: (b, 0)),
                pl.BlockSpec((TILE, 2 * width), lambda b, i: (b, 0)),
            ],
        ),
        out_shape=[shape_of((2 * rows, width), BF16), shape_of((2 * rows, 2 * width), BF16)],
        compiler_params=params(),
        cost_estimate=cost(rows * width * width * 8, rows * width * 14),
        name="encode",
    )(info, own, sent, w, bias)


def gelu_parts(values):
    half = 0.5 * (1.0 + lax.erf(values * (0.5**0.5)))
    slope = half + values * (jnp.exp(-0.5 * values * values) * (0.5 / jnp.pi) ** 0.5)
    return values * half, slope


def feed_kernel(
    info_ref,
    sum_ref,
    vectors_ref,
    mix_ref,
    packed_ref,
    bias_ref,
    goal_ref,
    w_ref,
    result_ref,
    near_ref,
    far_ref,
    grad_ref,
    grad_low_ref,
    grad_mix_ref,
    sums_ref,
    two_ref,
    low_ref,
    low_t_ref,
    act_ref,
    slope_ref,
    acc_ref,
    three_low_ref,
    three_t_ref,
    co_ref,
):
    phase, z = pl.program_id(0), pl.program_id(1)
    tensors = pl.num_programs(1)
    rows, width = sum_ref.shape
    hidden_units = w_ref.shape[3]
    piece = width // w_ref.shape[1]
    up = w_ref[0, :, :piece].reshape(width, hidden_units)
    down = w_ref[0, :, piece : 2 * piece].reshape(width, hidden_units)
    gain1, shift1, cob, gain2, shift2, downb, gain3, shift3 = (
        vectors_ref[i : i + 1, :] for i in range(1, 9)
    )

    @pl.when((phase == 0) & (z == 0))
    def _():
        _, shards, chunk, _ = packed_ref.shape
        columns = co_ref.shape[2]
        for t in range(co_ref.shape[0]):
            for s in range(shards):
                for i in range(piece // chunk):
                    start = s * piece + i * chunk
                    co_ref[t, start : start + chunk, :] = packed_ref[
                        t, s, :, i * columns : (i + 1) * columns
                    ]
        hidden_one = norm_parts(sum_ref[...])[0] * gain1 + shift1
        sum_two = hidden_one + cob
        for j in range(co_ref.shape[0]):
            part = mix_ref[:, j * columns : (j + 1) * columns]
            sum_two = sum_two + nt(part, co_ref[info_ref[2] ^ j])
        two_ref[...] = sum_two
        hidden_two = norm_parts(sum_two)[0] * gain2 + shift2
        low_ref[...] = hidden_two.astype(BF16)
        low_t_ref[...] = hidden_two.T.astype(BF16)
        acc_ref[...] = hidden_two + downb
        sums_ref[...] = jnp.zeros_like(sums_ref)

    @pl.when(phase == 0)
    def _():
        bias = bias_part(bias_ref, z ^ info_ref[2], 2 * co_ref.shape[2], hidden_units)
        pre = nn(low_ref[...], up) + bias
        value, slope = gelu_parts(pre)
        act = value.astype(BF16)
        act_ref[z] = act
        slope_ref[z] = slope
        acc_ref[...] += nt(act, down)

    @pl.when((phase == 0) & (z == tensors - 1))
    def _():
        sum_three = acc_ref[...]
        result = norm_parts(sum_three)[0] * gain3 + shift3
        result_ref[...] = result.astype(BF16)
        grad_three, *both = norm_back(sum_three, gain3, goal_ref[0])
        sums_ref[0:1, :] = both[0]
        sums_ref[1:2, :] = both[1]
        sums_ref[2:3, :] = jnp.sum(grad_three, axis=0, keepdims=True)
        acc_ref[...] = grad_three
        three_low_ref[...] = grad_three.astype(BF16)
        three_t_ref[...] = grad_three.T.astype(BF16)

    @pl.when(phase == 1)
    def _():
        grad_pre = nn(three_low_ref[...], down) * slope_ref[z]
        sums_ref[pl.ds(8 + z, 1), :hidden_units] = jnp.sum(grad_pre, axis=0, keepdims=True)
        pre_low = grad_pre.astype(BF16)
        acc_ref[...] += nt(pre_low, up)
        products = (
            nn(low_t_ref[...], pre_low).astype(BF16),
            nn(three_t_ref[...], act_ref[z]).astype(BF16),
        )
        _, _, ctxs, _, share, _ = near_ref.shape

        def put(core):
            for mat, product in enumerate(products):
                for s in range(w_ref.shape[1]):
                    ref = near_ref if (s & 1) == core else far_ref
                    for c in range(ctxs):
                        start = s * piece + c * share
                        ref[mat, (s >> 1) ^ (info_ref[0] >> 1), c ^ info_ref[1], 0] = product[
                            start : start + share
                        ]

        @pl.when((info_ref[0] & 1) == 0)
        def _():
            put(0)

        @pl.when((info_ref[0] & 1) != 0)
        def _():
            put(1)

    @pl.when((phase == 1) & (z == tensors - 1))
    def _():
        grad_two, *both = norm_back(two_ref[...], gain2, acc_ref[...])
        sums_ref[3:4, :] = both[0]
        sums_ref[4:5, :] = both[1]
        sums_ref[5:6, :] = jnp.sum(grad_two, axis=0, keepdims=True)
        grad_ref[...] = grad_two
        low = grad_two.astype(BF16)
        grad_low_ref[...] = low
        columns = co_ref.shape[2]
        for j in range(co_ref.shape[0]):
            part = nn(low, co_ref[info_ref[2] ^ j]).astype(BF16)
            grad_mix_ref[:, j * columns : (j + 1) * columns] = part


def feed(info, sum_one, vectors, mix, columns, chunk, bias, goal, w, ctxs):
    rows, width = sum_one.shape
    tensors, shards, taller, hidden_units = w.shape
    piece = width // shards
    assert hidden_units == width
    grads = (2, shards // 2, ctxs, tensors, piece // ctxs, hidden_units)
    grads_spec = pl.BlockSpec(
        grads[:3] + (1,) + grads[4:], lambda p, z, i: (0, 0, 0, (p * z) ^ i[2], 0, 0)
    )
    head = (sum_one, vectors, mix)
    last = 2 * piece // chunk
    return pl.pallas_call(
        feed_kernel,
        grid_spec=pltpu.PrefetchScalarGridSpec(
            num_scalar_prefetch=1,
            grid=(2, tensors),
            in_specs=[whole(a.shape) for a in head]
            + [
                pl.BlockSpec(
                    (tensors, shards, chunk, hidden_units), lambda p, z, i: (0, 0, last, 0)
                ),
                whole(bias.shape),
                pl.BlockSpec((1, rows, width), lambda p, z, i: (0, i[2], 0)),
                pl.BlockSpec((1, shards, taller, hidden_units), lambda p, z, i: (z, 0, 0, 0)),
            ],
            out_specs=[
                whole((rows, width)),
                grads_spec,
                grads_spec,
                whole((rows, width)),
                whole((rows, width)),
                whole((rows, width)),
                whole((16, width)),
            ],
            scratch_shapes=[
                pltpu.VMEM((rows, width), F32),
                pltpu.VMEM((rows, width), BF16),
                pltpu.VMEM((width, rows), BF16),
                pltpu.VMEM((tensors, rows, hidden_units), BF16),
                pltpu.VMEM((tensors, rows, hidden_units), F32),
                pltpu.VMEM((rows, width), F32),
                pltpu.VMEM((rows, width), BF16),
                pltpu.VMEM((width, rows), BF16),
                pltpu.VMEM((tensors, width, columns), BF16),
            ],
        ),
        out_shape=[
            shape_of((rows, width), BF16),
            shape_of(grads, BF16),
            shape_of(grads, BF16),
            shape_of((rows, width), F32),
            shape_of((rows, width), BF16),
            shape_of((rows, width), BF16),
            shape_of((16, width), F32),
        ],
        compiler_params=params(),
        cost_estimate=cost(rows * w.size * 6, w.size * 6, rows * width * tensors * 2),
        name="feed",
    )(info, *head, w, bias, goal, w)


def before_self_kernel(
    info_ref, grad_ref, dq_ref, cq_ref, sum_ref, gain_ref, dv_ref, o_ref, *out_refs
):
    grad_one_ref, low_ref, sums_ref = out_refs[:3]
    mix_refs = out_refs[3:]
    tensors, _, columns = o_ref.shape
    grad_hidden = grad_ref[...] + nt(dq_ref[...], cq_ref[...])
    grad_one, gain, shift = norm_back(sum_ref[...], gain_ref[...], grad_hidden)
    grad_one_ref[...] = grad_one
    low = grad_one.astype(BF16)
    low_ref[...] = low
    for j, mix_ref in enumerate(mix_refs):
        mix_ref[...] = nn(low, o_ref[j]).astype(BF16)
    sums_ref[...] = jnp.zeros_like(sums_ref)
    sums_ref[0:1, :] = gain
    sums_ref[1:2, :] = shift
    sums_ref[2:3, :] = jnp.sum(grad_one, axis=0, keepdims=True)
    queries = jnp.sum(dq_ref[...].astype(F32), axis=0, keepdims=True)
    values = jnp.sum(dv_ref[...].astype(F32), axis=0, keepdims=True)
    for j in range(tensors):
        part = slice(j * columns, (j + 1) * columns)
        at = info_ref[2] ^ j
        sums_ref[pl.ds(8 + at, 1), :columns] = queries[:, part]
        sums_ref[pl.ds(8 + tensors + at, 1), :columns] = values[:, part]


def before_self(info, grad, dq, cq, sum_one, gain, dv, o):
    rows, width = grad.shape
    tensors, _, columns = o.shape
    args = (grad, dq, cq, sum_one, gain, dv, o)
    return pl.pallas_call(
        before_self_kernel,
        grid_spec=pltpu.PrefetchScalarGridSpec(
            num_scalar_prefetch=1,
            grid=(1,),
            in_specs=[whole(a.shape) for a in args],
            out_specs=[whole((rows, width))] * 2
            + [whole((8 + 2 * tensors, width))]
            + [whole((rows, columns))] * tensors,
        ),
        out_shape=[
            shape_of((rows, width), F32),
            shape_of((rows, width), BF16),
            shape_of((8 + 2 * tensors, width), F32),
        ]
        + [shape_of((rows, columns), BF16)] * tensors,
        compiler_params=params(),
        cost_estimate=cost(rows * width * width * 4, width * width * 6 + rows * width * 14),
        name="before_self",
    )(info, *args)


def encoder_grad_kernel(dk_ref, dv_ref, w_ref, keep_ref, send_ref):
    width = dk_ref.shape[1]
    part = nt(dk_ref[...], w_ref[:, :width]) + nt(dv_ref[...], w_ref[:, width:])
    half = pl.num_programs(0) // 2

    @pl.when(pl.program_id(0) < half)
    def _():
        send_ref[...] = part.astype(BF16)

    @pl.when(pl.program_id(0) >= half)
    def _():
        keep_ref[...] = part


def encoder_grad(dk, dv, w):
    keys, width = dk.shape
    half = keys // TILE // 2
    side = pl.BlockSpec((TILE, width), lambda b: (jnp.where(b < half, b + half, b - half), 0))
    return pl.pallas_call(
        encoder_grad_kernel,
        grid=(2 * half,),
        in_specs=[side, side, whole(w.shape)],
        out_specs=[
            pl.BlockSpec((TILE, width), lambda b: (jnp.maximum(b - half, 0), 0)),
            pl.BlockSpec((TILE, width), lambda b: (jnp.minimum(b, half - 1), 0)),
        ],
        out_shape=[shape_of((keys // 2, width), F32), shape_of((keys // 2, width), BF16)],
        compiler_params=params(),
        cost_estimate=cost(keys * width * width * 4, keys * width * 10),
        name="encoder_grad",
    )(dk, dv, w)


def square_grads_kernel(info_ref, *refs, ctxs, groups):
    count = sum(groups)
    left_refs, right_refs = refs[:count], refs[count : 2 * count]
    flipped = refs[-count:]
    outs = refs[2 * count : -count]
    i, other = pl.program_id(0), pl.program_id(1)
    _, _, tensors, share, packed = outs[0].shape
    piece = share * ctxs
    columns = packed // groups[0]

    @pl.when((i == 0) & (other == 0))
    def _():
        for left_ref, flipped_ref in zip(left_refs, flipped):
            flipped_ref[...] = flip(left_ref[...])

    s = ((i ^ (info_ref[0] >> 1)) << 1) + ((info_ref[0] & 1) ^ other)
    rows = pl.ds(pl.multiple_of(s * piece, piece), piece)
    grads = [
        nn(flipped_ref[rows, :], right_ref[...]).astype(BF16)
        for flipped_ref, right_ref in zip(flipped, right_refs)
    ]

    def put(refs):
        for z in range(tensors):
            part = slice(z * columns, (z + 1) * columns)
            start = 0
            for ref, size in zip(refs, groups):
                tile = jnp.concatenate(
                    [grad[:, part] for grad in grads[start : start + size]], axis=1
                )
                start += size
                for r in range(ctxs):
                    chosen = tile[:share]
                    for c in range(1, ctxs):
                        chosen = jnp.where(
                            (info_ref[1] ^ r) == c, tile[c * share : (c + 1) * share], chosen
                        )
                    ref[0, r, z] = chosen

    @pl.when(other == 0)
    def _():
        put(outs[: len(groups)])

    @pl.when(other != 0)
    def _():
        put(outs[len(groups) :])


def square_grads(info, pairs, groups, sizes):
    shards, ctxs, tensors = sizes
    width = pairs[0][0].shape[1]
    share = width // shards // ctxs
    args = [left for left, _ in pairs] + [right for _, right in pairs]
    sides = [
        (shards // 2, ctxs, tensors, share, size * width // tensors) for size in groups
    ] * 2
    return pl.pallas_call(
        functools.partial(square_grads_kernel, ctxs=ctxs, groups=groups),
        grid_spec=pltpu.PrefetchScalarGridSpec(
            num_scalar_prefetch=1,
            grid=(shards // 2, 2),
            in_specs=[whole(a.shape) for a in args],
            out_specs=[
                pl.BlockSpec((1,) + side[1:], lambda i, c, n: (i, 0, 0, 0, 0)) for side in sides
            ],
            scratch_shapes=[pltpu.VMEM((width, left.shape[0]), BF16) for left, _ in pairs],
        ),
        out_shape=[shape_of(side, BF16) for side in sides],
        compiler_params=params(),
        cost_estimate=cost(2 * width * sum(a.size for a in args), width * width * 8),
        name="square_grads",
    )(info, *args)


def input_grad_kernel(
    info_ref, dq_ref, down_ref, dtrunk_ref, came_ref, low_ref, w_ref, *rest, ctxs, tensors
):
    part_refs = rest[:tensors]
    near_ref, far_ref, dw_ref = rest[tensors:]
    b = pl.program_id(0)

    @pl.when(b == 0)
    def _():
        dw_ref[...] = jnp.zeros_like(dw_ref)

    trunk = dtrunk_ref[...].astype(F32) + came_ref[...].astype(F32)
    dkv = (down_ref[...] + jnp.where(info_ref[1] == 0, trunk, 0.0)).astype(BF16)
    grads = jnp.concatenate([dq_ref[...], dkv], axis=1)
    dw_ref[...] += tn(low_ref[...], grads)
    put_slot(b ^ info_ref[2], nt(grads, w_ref[...]), part_refs)

    @pl.when(b == pl.num_programs(0) - 1)
    def _():
        halves, _, share, _ = near_ref.shape
        for other, ref in ((0, near_ref), (1, far_ref)):
            for i in range(halves):
                s = ((i ^ (info_ref[0] >> 1)) << 1) + ((info_ref[0] & 1) ^ other)
                for r in range(ctxs):
                    start = (s * ctxs + (info_ref[1] ^ r)) * share
                    ref[i, r] = dw_ref[pl.ds(pl.multiple_of(start, share), share), :].astype(BF16)


def input_grad(info, dq, down, dtrunk, came, low, w, sizes):
    shards, ctxs, tensors = sizes
    rows, columns = dq.shape
    width = low.shape[1]
    share = width // shards // ctxs
    side = (shards // 2, ctxs, share, 3 * columns)

    def tile(n):
        return pl.BlockSpec((TILE, n), lambda b, i: (b, 0))

    return pl.pallas_call(
        functools.partial(input_grad_kernel, ctxs=ctxs, tensors=tensors),
        grid_spec=pltpu.PrefetchScalarGridSpec(
            num_scalar_prefetch=1,
            grid=(rows // TILE,),
            in_specs=[
                tile(columns),
                tile(2 * columns),
                tile(2 * columns),
                tile(2 * columns),
                tile(width),
                whole(w.shape),
            ],
            out_specs=[whole((TILE, width))] * tensors
            + [whole(side), whole(side)],
            scratch_shapes=[pltpu.VMEM((width, 3 * columns), F32)],
        ),
        out_shape=[shape_of((TILE, width), F32)]
        + [shape_of((TILE, width), BF16)] * (tensors - 1)
        + [shape_of(side, BF16)] * 2,
        compiler_params=params(),
        cost_estimate=cost(rows * width * columns * 12, rows * width * 14),
        name="input_grad",
    )(info, dq, down, dtrunk, came, low, w)


def lay_rows_kernel(info_ref, *refs):
    in_refs, out_ref = refs[:-1], refs[-1]
    out_ref[...] = take_slot(pl.program_id(0) ^ info_ref[2], in_refs).astype(F32)


def lay_rows(info, parts):
    rows, width = parts[0].shape
    return pl.pallas_call(
        lay_rows_kernel,
        grid_spec=pltpu.PrefetchScalarGridSpec(
            num_scalar_prefetch=1,
            grid=(len(parts),),
            in_specs=[whole((rows, width))] * len(parts),
            out_specs=pl.BlockSpec((rows, width), lambda b, i: (b, 0)),
        ),
        out_shape=shape_of((rows * len(parts), width), F32),
        compiler_params=params(),
        cost_estimate=cost(0, rows * width * len(parts) * 6),
        name="lay_rows",
    )(info, *parts)


def local(sizes, *args):
    (
        layer_input,
        encoder_out,
        enc_length,
        parent_ids,
        token_segment,
        self_query,
        self_key,
        self_value,
        self_output,
        cross_query,
        cross_key,
        cross_value,
        cross_output,
        ffn_up,
        ffn_down,
        self_qbias,
        self_vbias,
        self_obias,
        cross_qbias,
        cross_vbias,
        cross_obias,
        ffn_upbias,
        ffn_downbias,
        norm1_gain,
        norm1_shift,
        norm2_gain,
        norm2_shift,
        norm3_gain,
        norm3_shift,
        out_grad,
    ) = args
    shards, ctxs, tensors = sizes["shard"], sizes["ctx"], sizes["tensor"]
    me_ctx = lax.axis_index("ctx")
    info = jnp.stack([lax.axis_index("shard"), me_ctx, lax.axis_index("tensor")]).astype(jnp.int32)
    scale = HEAD_DIM ** (-0.5)
    local_rows, width = layer_input.shape[1:]
    piece, columns = self_query.shape
    heads = columns // HEAD_DIM
    seg = token_segment.shape[1] // parent_ids.shape[1]
    assert local_rows == tensors * TILE and ctxs == 2

    def bits_of(axis):
        return [1 << k for k in range(sizes[axis].bit_length() - 1)]

    def swap(a, axis, bit):
        return lax.ppermute(a, axis, [(i, i ^ bit) for i in range(sizes[axis])])

    shard_bits = [("shard", 1 << k) for k in range(1, shards.bit_length() - 1)]

    def over_tensor(a):
        return [a] + [swap(a, "tensor", j) for j in range(1, tensors)]

    def grow(a, axis, bit, *others):
        return jnp.stack(tie([a, swap(a, axis, bit)], *others))

    def add(a, b):
        return (a.astype(F32) + b.astype(F32)).astype(BF16)

    def reduce_levels(near, far):
        came = swap(far, "shard", 1)
        lead = (2,) * len(shard_bits) + near.shape[1:]
        near, came = near.reshape(lead), came.reshape(lead)

        for axis, bit in list(reversed(shard_bits)) + [("ctx", 1)]:
            send = add(near[1], came[1])
            near, came = add(near[0], came[0]), swap(send, axis, bit)
        return add(near, came)

    def join_ctx(mine):
        other = swap(mine, "ctx", 1)
        first = me_ctx == 0
        return jnp.concatenate([jnp.where(first, mine, other), jnp.where(first, other, mine)])

    def row(vector):
        return vector.reshape(1, -1)

    def tie(a, *others):
        return lax.optimization_barrier((a,) + others)[0]

    vectors = jnp.stack(
        [
            self_obias,
            norm1_gain,
            norm1_shift,
            cross_obias,
            norm2_gain,
            norm2_shift,
            ffn_downbias,
            norm3_gain,
            norm3_shift,
        ]
    )

    pack = tensors if piece % (16 * tensors) == 0 else 1
    chunk = piece // pack
    packed_co = jnp.concatenate(
        [cross_output.T[i * chunk : (i + 1) * chunk] for i in range(pack)], axis=1
    )
    packed_co = jnp.pad(packed_co, ((0, 0), (0, width - packed_co.shape[1])))
    ffn_piece = jnp.concatenate([ffn_up, ffn_down.T, packed_co], axis=0)
    bias = jnp.concatenate([cross_qbias, cross_vbias, ffn_upbias])
    bias = jnp.pad(bias, (0, -bias.shape[0] % width)).reshape(-1, width)
    bias_high = lax.reduce_precision(bias, 8, 7)
    bias_rows = 16
    bias = jnp.concatenate([bias_high, bias - bias_high]).astype(BF16)
    bias = jnp.pad(bias, ((0, bias_rows - bias.shape[0]), (0, 0)))
    squares = over_tensor(
        jnp.concatenate(
            [
                jnp.concatenate([cross_key, cross_value, self_output.T, cross_query], axis=1),
                bias,
            ],
            axis=0,
        )
    )
    enc_sent = swap(encoder_out[0].astype(BF16), "ctx", 1)
    qkv_weights = lax.all_gather(
        jnp.concatenate([self_query, self_key, self_value], axis=1), "shard", axis=0, tiled=True
    )

    scalars = (info, parent_ids[0], token_segment[0])
    q, kv, input_low = project(layer_input, qkv_weights, row(self_qbias), row(self_vbias), scale)
    squares = jnp.stack(tie(squares, q))
    ffn_all = lax.all_gather(tie(ffn_piece, squares), ("tensor", "shard"), axis=0, tiled=True)
    kv_sent = lax.ppermute(tie(kv, squares), "ctx", [(0, 1)])
    for axis, bit in shard_bits[:-1]:
        squares = grow(squares, axis, bit, kv_sent)
    kv_sent = tie(kv_sent, squares)
    *mixes, self_logs = self_forward(scalars, q, kv, kv_sent, tensors, heads, seg)
    squares = grow(squares, *shard_bits[-1], self_logs)
    near = squares.reshape((shards // 2,) + squares.shape[-3:])
    far = swap(near, "shard", 1)
    all_heads = mixes[:1] + [swap(mixes[j], "tensor", j) for j in range(1, tensors)]
    weight_ckv, weight_o, weight_cq, bias = assemble(info, near, far, shards, columns, bias_rows)
    enc_low, ckv = encode(info, encoder_out, enc_sent, weight_ckv, bias, columns)
    all_heads = all_heads[:1] + list(tie(all_heads[1:], ckv))
    sum_one, one_low, cq, self_mix = after_self(
        info,
        layer_input,
        weight_o,
        weight_cq,
        vectors[0:1],
        vectors[1:2],
        vectors[2:3],
        bias,
        all_heads,
        scale,
    )

    cross_scalars = (info, enc_length)
    cross_mix, cross_logs = cross_forward(cross_scalars, cq, ckv)

    result, ffn_near, ffn_far, grad_two, two_grad_low, grad_cmix, feed_sums = feed(
        info,
        sum_one,
        vectors,
        cross_mix,
        columns,
        chunk,
        bias,
        out_grad,
        ffn_all.reshape(tensors, shards, -1, width),
        ctxs,
    )
    ffn_came = swap(ffn_far, "shard", 1)
    result_all = lax.all_gather(result, "tensor", axis=0, tiled=True)

    class Path:
        def __init__(self, near, came, order):
            lead = (2,) * len(shard_bits) + near.shape[1:]
            self.dims = list(reversed(shard_bits)) + [("ctx", 1)]
            self.order = list(order)
            self.keep, self.came = near.reshape(lead), came.reshape(lead)

        def fold(self):
            near, came = self.keep, self.came
            if not self.order:
                self.keep = add(near, came)
                return
            dim = self.dims.index(self.order[0])
            self.dims.pop(dim)
            index = (slice(None),) * dim
            self.send = add(near[index + (1,)], came[index + (1,)])
            self.keep = add(near[index + (0,)], came[index + (0,)])

        def go(self):
            axis, bit = self.order.pop(0)
            self.came = swap(self.send, axis, bit)

    high = list(reversed(shard_bits))
    orders = [[("ctx", 1)] + high, high + [("ctx", 1)]]

    dcq, dck, dcv = cross_backward(cross_scalars, cq, ckv, grad_cmix, cross_mix, cross_logs, scale)
    enc_keep, enc_send = encoder_grad(dck, dcv, weight_ckv)
    enc_came = swap(enc_send, "ctx", 1)
    grad_two = tie(grad_two, enc_send)
    grad_one, one_grad_low, self_sums, *grad_mixes = before_self(
        info, grad_two, dcq, weight_cq, sum_one, vectors[1:2], dcv, weight_o
    )
    head_grads = grad_mixes[:1] + [swap(grad_mixes[j], "tensor", j) for j in range(1, tensors)]
    mesh_sizes = (shards, ctxs, tensors)
    early_sums = jnp.concatenate([feed_sums, self_sums], axis=0)
    early_sums = early_sums + swap(early_sums, "tensor", 1)
    ffn_came = tie(ffn_came, one_grad_low)
    ffn_paths = [Path(ffn_near[i], ffn_came[i], order) for i, order in enumerate(orders)]
    sends = []
    for p in ffn_paths:
        p.fold()
        sends += [p.send, p.keep]
        p.go()
    enc_mine = (enc_keep + tie(enc_came, *sends).astype(F32)).astype(BF16)
    grad_encoder = lax.psum(enc_mine, "tensor")
    near_a, near_b, far_a, far_b = square_grads(
        info,
        [
            (tie(enc_low, early_sums, enc_mine, result_all), dck),
            (enc_low, dcv),
            (one_grad_low, self_mix),
            (one_low, dcq),
            (two_grad_low, cross_mix),
        ],
        (2, 3),
        mesh_sizes,
    )
    head_grads, far_a, far_b = tie((head_grads, far_a, far_b), far_b)
    for _ in range(len(high)):
        for p in ffn_paths:
            p.came = tie(p.came, far_b)
            p.fold()
            head_grads = tie(head_grads, p.send, p.keep)
            p.go()
    sums_came = [swap(early_sums, "tensor", bit) for bit in bits_of("tensor")[1:2]]

    dq, down, dtrunk, late_sums = self_backward(
        scalars, q, kv, kv_sent, head_grads, mixes, self_logs, heads, seg, scale, width
    )
    trunk_came = lax.ppermute(dtrunk, "ctx", [(1, 0)])
    paths = [
        Path(near, tie(swap(far, "shard", 1), dtrunk), order)
        for near, far, order in zip((near_a, near_b), (far_a, far_b), orders)
    ]
    for p in paths:
        p.fold()
        trunk_came = tie(trunk_came, p.send, p.keep)
        p.go()
    for p in ffn_paths:
        p.came = tie(p.came, dtrunk, grad_encoder, *(q.keep for q in paths))
        p.fold()
    ffn_blocks = jnp.concatenate([p.keep for p in ffn_paths], axis=1)
    ffn_came = [swap(ffn_blocks[j], "tensor", j) for j in range(1, tensors)]
    for came in tie(sums_came, dtrunk):
        early_sums = early_sums + came
    for bit in bits_of("tensor")[2:]:
        early_sums = early_sums + swap(early_sums, "tensor", bit)
    sums = jnp.concatenate([early_sums, late_sums], axis=0)
    for axis, bit in [("shard", 1)] + shard_bits:
        sums = sums + swap(sums, axis, bit)
    trunk_came = tie(trunk_came, ffn_blocks, sums)
    *parts, near, far = input_grad(
        info, dq, down, dtrunk, trunk_came, input_low, qkv_weights, mesh_sizes
    )
    part_came = [swap(parts[j], "tensor", j) for j in range(1, tensors)]
    for _ in range(len(high)):
        for p in paths:
            p.came = tie(p.came, parts[0])
            p.fold()
            p.go()
    lead = (2,) * len(shard_bits) + near.shape[1:]
    near, far = near.reshape(lead), swap(far, "shard", 1).reshape(lead)
    send, keep = add(near[1], far[1]), add(near[0], far[0])
    for axis, bit in list(reversed(shard_bits))[:-1]:
        came = swap(send, axis, bit)
        send, keep = add(keep[1], came[1]), add(keep[0], came[0])
    came = swap(send, *shard_bits[0])
    keep = add(keep, came)
    ffn_total = ffn_blocks[0].astype(F32)
    for part in tie(ffn_came, parts[0]):
        ffn_total = ffn_total + part.astype(F32)
    ffn_total = ffn_total.astype(BF16)
    sums_came = swap(tie(sums, parts[0]), "ctx", 1)
    for p in paths:
        p.fold()
    squares = jnp.concatenate([p.keep for p in paths], axis=2)
    square_came = [swap(squares[j], "tensor", j) for j in range(1, tensors)]
    part_came, square_came = tie((part_came, square_came), keep, ffn_total)
    square_total = squares[0].astype(F32)
    for part in square_came:
        square_total = square_total + part.astype(F32)
    square_total = square_total.astype(BF16)
    part_came = tie(part_came, square_total)
    input_mine = grad_one + parts[0]
    for part in part_came:
        input_mine = input_mine + part.astype(F32)
    input_mine = input_mine.astype(BF16)
    input_all = over_tensor(input_mine)
    ctx_came = [swap(a, "ctx", 1) for a in (keep, ffn_total, square_total)]
    ctx_came, sums_came = tie((ctx_came, sums_came), input_mine)
    qkv_came, ffn_came, square_came = ctx_came
    sums = sums + sums_came
    qkv_grads = [add(keep[r], qkv_came[r ^ 1]) for r in range(ctxs)]
    first = me_ctx == 0
    qkv_grads = jnp.concatenate(
        [jnp.where(first, qkv_grads[r], qkv_grads[r ^ 1]) for r in range(ctxs)]
    ).astype(F32)
    grad_q, grad_k, grad_v = (qkv_grads[:, i * columns : (i + 1) * columns] for i in range(3))

    def in_order(mine, other):
        return [
            jnp.where(first, mine, other).astype(F32),
            jnp.where(first, other, mine).astype(F32),
        ]

    share = piece // ctxs
    halves = in_order(ffn_total, ffn_came)
    grad_up = jnp.concatenate([half[:share] for half in halves])
    grad_down = jnp.concatenate([half[share:] for half in halves])
    squares = jnp.concatenate(in_order(square_total, square_came))
    grad_ck, grad_cv, grad_o, grad_cq, grad_co = (
        squares[:, i * columns : (i + 1) * columns] for i in range(5)
    )
    grad_encoder = tie(grad_encoder, input_all[1]).astype(F32)
    result_all = tie(result_all, input_all[1]).astype(F32)
    input_all = input_all[:1] + list(tie(input_all[1:], sums, qkv_grads, grad_up, squares))
    grad_input = lay_rows(info, input_all)
    me_tensor = info[2]

    def mine(start, size):
        return lax.dynamic_slice(sums, (start + me_tensor, 0), (1, size)).reshape(-1)

    base = 16 + 8
    later = base + 2 * tensors

    return (
        result_all[None],
        grad_input[None],
        grad_encoder[None],
        grad_q,
        grad_k,
        grad_v,
        grad_o.T,
        grad_cq,
        grad_ck,
        grad_cv,
        grad_co.T,
        grad_up,
        grad_down.T,
        mine(later, columns),
        mine(later + tensors, columns),
        sums[18],
        mine(base, columns),
        mine(base + tensors, columns),
        sums[5],
        mine(8, ffn_upbias.shape[0]),
        sums[2],
        sums[16],
        sums[17],
        sums[3],
        sums[4],
        sums[0],
        sums[1],
    )


def solution(mesh):
    sizes = {axis: mesh.shape[axis] for axis in ("shard", "ctx", "tensor")}
    rows = P("shard", "ctx", None)
    tall, wide = P("shard", "tensor"), P("tensor", "shard")
    mats = (tall, tall, tall, wide, tall, tall, tall, wide, tall, wide)
    part = P("tensor")
    vectors = (part, part, P(), part, part, P(), part) + (P(),) * 7
    tree = P("shard", None)
    return jax.shard_map(
        functools.partial(local, sizes),
        mesh=mesh,
        in_specs=(rows, rows, P("shard"), tree, tree) + mats + vectors + (rows,),
        out_specs=(rows, rows, rows) + mats + vectors,
        check_vma=False,
    )
```

```python
import functools

import jax
import jax.numpy as jnp
from jax import lax
from jax.experimental import pallas as pl
from jax.experimental.pallas import tpu as pltpu
from jax.sharding import PartitionSpec as P

HEAD_DIM = 64
LANES = 128
TILE = 256
NEG = -1e30
EPS = 1e-05
F32 = jnp.float32
BF16 = jnp.bfloat16
VMEM_LIMIT = 56 * 1024 * 1024
WEIGHT = 0.01


def dot_of(a, b, a_dim, b_dim):
    return lax.dot_general(a, b, (((a_dim,), (b_dim,)), ((), ())), preferred_element_type=F32)


def nn(a, b):
    return dot_of(a, b, 1, 0)


def nt(a, b):
    return dot_of(a, b, 1, 1)


def tn(a, b):
    return dot_of(a, b, 0, 0)


def head_lanes(rows, half):
    lane = lax.broadcasted_iota(jnp.int32, (rows, LANES), 1)
    return (lane < HEAD_DIM) if half == 0 else (lane >= HEAD_DIM)


def flags_of(rows, seg):
    lane = lax.broadcasted_iota(jnp.int32, (rows, LANES), 1) % HEAD_DIM
    row = lax.broadcasted_iota(jnp.int32, (rows, LANES), 0)
    return jnp.where(lane == row // seg, 1.0, 0.0).astype(BF16)


def causal_keep(size, seg):
    key = lax.broadcasted_iota(jnp.int32, (size, size), 0)
    query = lax.broadcasted_iota(jnp.int32, (size, size), 1)
    return (key // seg != query // seg) | (key <= query)


def flip(a):
    return a.astype(F32).T.astype(a.dtype)


def lane_pad(a):
    gap = -a.shape[1] % LANES
    return jnp.concatenate([a, jnp.zeros((a.shape[0], gap), a.dtype)], axis=1) if gap else a


def fold_forward(state, queries, key_tile, value_tile, bias_tile, heads, keep):
    out = []
    for h in range(heads):
        g, half = divmod(h, 2)
        lanes = slice(g * LANES, (g + 1) * LANES)
        if half == 0:
            value_rows = flip(value_tile[:, lanes])
        keys = jnp.where(head_lanes(key_tile.shape[0], half), key_tile[:, lanes], bias_tile)
        scores = nt(keys, queries[h])
        if keep is not None:
            scores = jnp.where(keep, scores, NEG)
        peak, total, mix = state[3 * h : 3 * h + 3]
        new_peak = jnp.maximum(peak, jnp.max(scores, axis=0, keepdims=True))
        weights = jnp.exp(scores - new_peak)
        shrink = jnp.exp(peak - new_peak)
        total = total * shrink + jnp.sum(weights, axis=0, keepdims=True)
        mix = mix * shrink + nn(
            value_rows[half * HEAD_DIM : (half + 1) * HEAD_DIM], weights.astype(BF16)
        )
        out += [new_peak, total, mix]
    return tuple(out)


def fresh_state(heads, rows):
    state = []
    for _ in range(heads):
        state += [
            jnp.full((1, rows), NEG, F32),
            jnp.zeros((1, rows), F32),
            jnp.zeros((HEAD_DIM, rows), F32),
        ]
    return tuple(state)


def flagged_queries(q, heads, seg):
    rows = q.shape[0]
    flags = flags_of(rows, seg)
    return [
        jnp.where(head_lanes(rows, h % 2), q[:, (h // 2) * LANES : (h // 2 + 1) * LANES], flags)
        for h in range(heads)
    ]


def mixed(state, heads):
    parts = [state[3 * h + 2] / state[3 * h + 1] for h in range(heads)]
    if heads % 2:
        parts.append(jnp.zeros_like(parts[0]))
    return jnp.concatenate(
        [jnp.concatenate(parts[h : h + 2], axis=0).T for h in range(0, len(parts), 2)], axis=1
    ).astype(BF16)


def put_logs(state, heads, log_ref):
    log_ref[...] = jnp.zeros_like(log_ref)
    for h in range(heads):
        log_ref[h : h + 1, :] = state[3 * h] + jnp.log(state[3 * h + 1])


def ancestors(parent_ref, label, count):
    def step(_, carry):
        at, bits = carry
        found = at >= 0
        safe = jnp.maximum(at, 0)
        return jnp.where(found, parent_ref[safe], at), jnp.where(
            found, bits | (jnp.int32(1) << safe), bits
        )

    return lax.fori_loop(0, count, step, (parent_ref[label], jnp.int32(0)))[1]


def seg_terms(bits, labels, same, seg):
    lane = lax.broadcasted_iota(jnp.int32, (TILE, LANES), 1) % HEAD_DIM
    row = lax.broadcasted_iota(jnp.int32, (TILE, LANES), 0) // seg
    out = jnp.zeros((TILE, LANES), F32)
    for i, mask in enumerate(bits):
        for t, label in enumerate(labels):
            if same and i == t:
                continue
            term = jnp.where(((mask >> label) & 1) == 1, 0.0, NEG)
            out = jnp.where((lane == i) & (row == t), term, out)
    return out.astype(BF16)


def unpack_kv(tile):
    half = tile.shape[1] // 2
    return lane_pad(tile[:, :half]), lane_pad(tile[:, half:])


def fill_trunk(info_ref, own_ref, sent_ref, trunk_ref):
    def fill(ref):
        keys, values = unpack_kv(ref[...])
        trunk_ref[:, : keys.shape[1]] = keys
        trunk_ref[:, keys.shape[1] :] = values

    @pl.when((pl.program_id(0) == 0) & (info_ref[1] == 0))
    def _():
        fill(own_ref)

    @pl.when((pl.program_id(0) == 0) & (info_ref[1] != 0))
    def _():
        fill(sent_ref)


def tile_rows(c):
    return pl.ds(pl.multiple_of(c * TILE, TILE), TILE)


def block_masks(info_ref, parent_ref, label_ref, seg, rows):
    b = pl.program_id(0)
    per = TILE // seg
    first = info_ref[1] * rows + b * TILE
    own = [label_ref[first + i * seg] for i in range(per)]
    bits = [ancestors(parent_ref, label, parent_ref.shape[0]) for label in own]

    def terms(c):
        return seg_terms(bits, [label_ref[c * TILE + t * seg] for t in range(per)], False, seg)

    count = jnp.where(info_ref[1] == 0, b, rows // TILE)
    return seg_terms(bits, own, True, seg), terms, count


def put_slot(slot, value, refs):
    for j, ref in enumerate(refs):

        @pl.when(slot == j)
        def _(ref=ref):
            ref[...] = value.astype(ref.dtype)


def take_slot(slot, refs):
    value = refs[0][...]
    for j, ref in enumerate(refs[1:], 1):
        value = jnp.where(slot == j, ref[...], value)
    return value


def self_forward_kernel(
    info_ref, parent_ref, label_ref, q_ref, own_ref, sent_ref, *rest, heads, seg
):
    mix_refs, (log_ref, trunk_ref) = rest[:-2], rest[-2:]
    b = pl.program_id(0)
    fill_trunk(info_ref, own_ref, sent_ref, trunk_ref)
    width = trunk_ref.shape[1] // 2
    queries = flagged_queries(lane_pad(q_ref[...]), heads, seg)
    own_terms, terms, count = block_masks(
        info_ref, parent_ref, label_ref, seg, own_ref.shape[0]
    )
    keys, values = unpack_kv(own_ref[tile_rows(b), :])
    state = fold_forward(
        fresh_state(heads, TILE), queries, keys, values, own_terms, heads, causal_keep(TILE, seg)
    )

    def body(c, state):
        rows = tile_rows(c)
        return fold_forward(
            state,
            queries,
            trunk_ref[rows, :width],
            trunk_ref[rows, width:],
            terms(c),
            heads,
            None,
        )

    def all_at_once(state):
        every = jnp.concatenate([terms(c) for c in range(trunk_ref.shape[0] // TILE)], axis=0)
        return fold_forward(
            state, queries, trunk_ref[:, :width], trunk_ref[:, width:], every, heads, None
        )

    state = lax.cond(
        count == trunk_ref.shape[0] // TILE,
        all_at_once,
        lambda state: lax.fori_loop(0, count, body, state),
        state,
    )
    put_logs(state, heads, log_ref)
    put_slot(b ^ info_ref[2], mixed(state, heads)[:, : mix_refs[0].shape[1]], mix_refs)


def params():
    return pltpu.CompilerParams(vmem_limit_bytes=VMEM_LIMIT)


def cost(flops, bytes_accessed, transcendentals=0):
    return pl.CostEstimate(
        flops=int(flops * WEIGHT),
        bytes_accessed=int(bytes_accessed * WEIGHT),
        transcendentals=int(transcendentals * WEIGHT),
    )


def whole(shape):
    return pl.BlockSpec(shape, lambda *_: (0,) * len(shape))


def shape_of(shape, dtype):
    return jax.ShapeDtypeStruct(shape, dtype)


def self_forward(scalars, q, own, sent, tensors, heads, seg):
    rows, columns = q.shape
    blocks = rows // TILE
    width = -(-columns // LANES) * LANES
    return pl.pallas_call(
        functools.partial(self_forward_kernel, heads=heads, seg=seg),
        grid_spec=pltpu.PrefetchScalarGridSpec(
            num_scalar_prefetch=3,
            grid=(blocks,),
            in_specs=[
                pl.BlockSpec((TILE, columns), lambda b, *_: (b, 0)),
                whole(own.shape),
                whole(own.shape),
            ],
            out_specs=[whole((TILE, columns))] * tensors
            + [pl.BlockSpec((8, TILE), lambda b, *_: (0, b))],
            scratch_shapes=[pltpu.VMEM((rows, 2 * width), BF16)],
        ),
        out_shape=[shape_of((TILE, columns), BF16)] * tensors + [shape_of((8, rows), F32)],
        compiler_params=params(),
        cost_estimate=cost(rows * rows * columns * 8, rows * columns * 16, rows * rows * heads),
        name="self_forward",
    )(*scalars, q, own, sent)


def fold_backward(
    queries, plain, grads, logs, deltas, key_tile, value_tile, bias_tile, heads, keep
):
    grad_keys, grad_values, grad_queries = [], [], []
    for h in range(heads):
        g, half = divmod(h, 2)
        lanes = slice(g * LANES, (g + 1) * LANES)
        if half == 0:
            key_rows = flip(key_tile[:, lanes])
        keys = jnp.where(head_lanes(key_tile.shape[0], half), key_tile[:, lanes], bias_tile)
        scores = nt(keys, queries[h])
        if keep is not None:
            scores = jnp.where(keep, scores, NEG)
        probs = jnp.exp(scores - logs[h])
        grad_probs = nt(value_tile[:, lanes], grads[h])
        grad_scores = (probs * (grad_probs - deltas[h])).astype(BF16)
        part_values = nn(probs.astype(BF16), grads[h])
        part_keys = nn(grad_scores, plain[h])
        if half == 0:
            grad_values.append(part_values)
            grad_keys.append(part_keys)
        else:
            grad_values[g] = grad_values[g] + part_values
            grad_keys[g] = grad_keys[g] + part_keys
        grad_queries.append(nn(key_rows[half * HEAD_DIM : (half + 1) * HEAD_DIM], grad_scores))
    return grad_keys, grad_values, tuple(grad_queries)


def backward_sides(q, grad, mix, heads, seg):
    rows = q.shape[0]
    queries = flagged_queries(q, heads, seg)
    plain, grads, deltas = [], [], []
    for h in range(heads):
        g, half = divmod(h, 2)
        lanes = slice(g * LANES, (g + 1) * LANES)
        mask = head_lanes(rows, half)
        plain.append(jnp.where(mask, q[:, lanes], jnp.zeros((), BF16)))
        grads.append(jnp.where(mask, grad[:, lanes], jnp.zeros((), BF16)))
        if half == 0:
            product = (grad[:, lanes].astype(F32) * mix[:, lanes].astype(F32)).T
        deltas.append(
            jnp.sum(product[half * HEAD_DIM : (half + 1) * HEAD_DIM], axis=0, keepdims=True)
        )
    return queries, plain, grads, deltas


def query_grads(grad_queries, scale):
    parts = list(grad_queries)
    if len(parts) % 2:
        parts.append(jnp.zeros_like(parts[0]))
    return (
        jnp.concatenate(
            [jnp.concatenate(parts[h : h + 2], axis=0).T for h in range(0, len(parts), 2)], axis=1
        )
        * scale
    ).astype(BF16)


def self_backward_kernel(
    info_ref, parent_ref, label_ref, q_ref, own_ref, sent_ref, *rest, heads, seg, scale, tensors
):
    grad_refs, mix_refs, rest = rest[:tensors], rest[tensors : 2 * tensors], rest[2 * tensors :]
    log_ref, dq_ref, down_ref, dtrunk_ref, sums_ref, trunk_ref, sum_ref, vector_ref = rest
    b = pl.program_id(0)
    slot = b ^ info_ref[2]
    fill_trunk(info_ref, own_ref, sent_ref, trunk_ref)
    width = trunk_ref.shape[1] // 2
    half_columns = own_ref.shape[1] // 2
    queries, plain, grads, deltas = backward_sides(
        lane_pad(q_ref[...]),
        lane_pad(take_slot(slot, grad_refs)),
        lane_pad(take_slot(slot, mix_refs)),
        heads,
        seg,
    )
    logs = [log_ref[h : h + 1, :] for h in range(heads)]
    own_terms, terms, count = block_masks(
        info_ref, parent_ref, label_ref, seg, own_ref.shape[0]
    )

    @pl.when(b == 0)
    def _():
        sum_ref[...] = jnp.zeros_like(sum_ref)
        vector_ref[...] = jnp.zeros_like(vector_ref)

    keys, values = unpack_kv(own_ref[tile_rows(b), :])
    grad_keys, grad_values, grad_queries = fold_backward(
        queries, plain, grads, logs, deltas, keys, values, own_terms, heads, causal_keep(TILE, seg)
    )
    down_ref[:, :half_columns] = jnp.concatenate(grad_keys, axis=1)[:, :half_columns]
    down_ref[:, half_columns:] = jnp.concatenate(grad_values, axis=1)[:, :half_columns]

    def body(c, grad_queries):
        rows = tile_rows(c)
        grad_keys, grad_values, more = fold_backward(
            queries,
            plain,
            grads,
            logs,
            deltas,
            trunk_ref[rows, :width],
            trunk_ref[rows, width:],
            terms(c),
            heads,
            None,
        )
        for g in range(len(grad_keys)):
            sum_ref[rows, g * LANES : (g + 1) * LANES] += grad_keys[g]
            sum_ref[rows, width + g * LANES : width + (g + 1) * LANES] += grad_values[g]
        return tuple(x + y for x, y in zip(grad_queries, more))

    def all_at_once(grad_queries):
        every = jnp.concatenate([terms(c) for c in range(trunk_ref.shape[0] // TILE)], axis=0)
        grad_keys, grad_values, more = fold_backward(
            queries,
            plain,
            grads,
            logs,
            deltas,
            trunk_ref[:, :width],
            trunk_ref[:, width:],
            every,
            heads,
            None,
        )
        for g in range(len(grad_keys)):
            sum_ref[:, g * LANES : (g + 1) * LANES] += grad_keys[g]
            sum_ref[:, width + g * LANES : width + (g + 1) * LANES] += grad_values[g]
        return tuple(x + y for x, y in zip(grad_queries, more))

    grad_queries = lax.cond(
        count == trunk_ref.shape[0] // TILE,
        all_at_once,
        lambda grad_queries: lax.fori_loop(0, count, body, grad_queries),
        grad_queries,
    )
    dq = query_grads(grad_queries, scale)[:, :half_columns]
    dq_ref[...] = dq
    vector_ref[0:1, :] += jnp.sum(dq.astype(F32), axis=0, keepdims=True)
    vector_ref[1:2, :] += jnp.sum(down_ref[:, half_columns:], axis=0, keepdims=True)

    @pl.when(b == pl.num_programs(0) - 1)
    def _():
        trunk_sum = jnp.sum(sum_ref[:, width : width + half_columns], axis=0, keepdims=True)
        sums_ref[...] = jnp.zeros_like(sums_ref)
        sums_ref[pl.ds(info_ref[2], 1), :half_columns] = vector_ref[0:1, :]
        sums_ref[pl.ds(tensors + info_ref[2], 1), :half_columns] = (
            vector_ref[1:2, :] + trunk_sum
        )
        dtrunk_ref[:, :half_columns] = sum_ref[:, :half_columns].astype(BF16)
        dtrunk_ref[:, half_columns:] = sum_ref[:, width : width + half_columns].astype(BF16)


def self_backward(scalars, q, own, sent, grads, mixes, logs, heads, seg, scale, model_width):
    rows, columns = q.shape
    blocks = rows // TILE
    width = -(-columns // LANES) * LANES
    tensors = len(grads)
    tile = pl.BlockSpec((TILE, columns), lambda b, *_: (b, 0))
    return pl.pallas_call(
        functools.partial(
            self_backward_kernel, heads=heads, seg=seg, scale=scale, tensors=tensors
        ),
        grid_spec=pltpu.PrefetchScalarGridSpec(
            num_scalar_prefetch=3,
            grid=(blocks,),
            in_specs=[tile, whole(own.shape), whole(own.shape)]
            + [whole((TILE, columns))] * (2 * tensors)
            + [pl.BlockSpec((8, TILE), lambda b, *_: (0, b))],
            out_specs=[
                tile,
                pl.BlockSpec((TILE, 2 * columns), lambda b, *_: (b, 0)),
                whole((rows, 2 * columns)),
                whole((2 * tensors, model_width)),
            ],
            scratch_shapes=[
                pltpu.VMEM((rows, 2 * width), BF16),
                pltpu.VMEM((rows, 2 * width), F32),
                pltpu.VMEM((8, columns), F32),
            ],
        ),
        out_shape=[
            shape_of((rows, columns), BF16),
            shape_of((rows, 2 * columns), F32),
            shape_of((rows, 2 * columns), BF16),
            shape_of((2 * tensors, model_width), F32),
        ],
        compiler_params=params(),
        cost_estimate=cost(rows * rows * columns * 20, rows * columns * 40, rows * rows * heads),
        name="self_backward",
    )(*scalars, q, own, sent, *grads, *mixes, logs)


def length_terms(info_ref, length_ref, keys):
    row = lax.broadcasted_iota(jnp.int32, (keys, LANES), 0)
    lane = lax.broadcasted_iota(jnp.int32, (keys, LANES), 1) % HEAD_DIM
    half = keys // 2
    place = jnp.where(row < half, row + info_ref[1] * half, row - info_ref[1] * half)
    return jnp.where((place >= length_ref[0]) & (lane == 0), NEG, 0.0).astype(BF16)


def cross_forward_kernel(info_ref, length_ref, q_ref, k_ref, v_ref, mix_ref, log_ref):
    rows, keys = q_ref.shape[0], k_ref.shape[0]
    queries = flagged_queries(q_ref[...], 2, rows)
    terms = length_terms(info_ref, length_ref, keys)
    state = fold_forward(
        fresh_state(2, rows), queries, k_ref[...], v_ref[...], terms, 2, None
    )
    put_logs(state, 2, log_ref)
    mix_ref[...] = mixed(state, 2)


def cross_specs(rows, keys, groups):
    part = pl.BlockSpec((rows, LANES), lambda g, *_: (0, g))
    return (
        part,
        pl.BlockSpec((keys, LANES), lambda g, *_: (0, g)),
        pl.BlockSpec((keys, LANES), lambda g, *_: (0, groups + g)),
        pl.BlockSpec((8, rows), lambda g, *_: (g, 0)),
    )


def cross_forward(scalars, q, kv):
    rows, width = q.shape
    keys = kv.shape[0]
    groups = width // LANES
    part, key_side, value_side, log_side = cross_specs(rows, keys, groups)
    return pl.pallas_call(
        cross_forward_kernel,
        grid_spec=pltpu.PrefetchScalarGridSpec(
            num_scalar_prefetch=2,
            grid=(groups,),
            in_specs=[part, key_side, value_side],
            out_specs=[part, log_side],
        ),
        out_shape=[shape_of((rows, width), BF16), shape_of((8 * groups, rows), F32)],
        compiler_params=params(),
        cost_estimate=cost(
            rows * keys * width * 8, (rows + keys) * width * 4, rows * keys * groups * 2
        ),
        name="cross_forward",
    )(*scalars, q, kv, kv)


def cross_backward_kernel(
    info_ref,
    length_ref,
    q_ref,
    k_ref,
    v_ref,
    grad_ref,
    mix_ref,
    log_ref,
    dq_ref,
    dk_ref,
    dv_ref,
    *,
    scale,
):
    rows, keys = q_ref.shape[0], k_ref.shape[0]
    queries, plain, grads, deltas = backward_sides(
        q_ref[...], grad_ref[...], mix_ref[...], 2, rows
    )
    logs = [log_ref[h : h + 1, :] for h in range(2)]
    terms = length_terms(info_ref, length_ref, keys)
    grad_keys, grad_values, total = fold_backward(
        queries, plain, grads, logs, deltas, k_ref[...], v_ref[...], terms, 2, None
    )
    dk_ref[...] = grad_keys[0].astype(BF16)
    dv_ref[...] = grad_values[0].astype(BF16)
    dq_ref[...] = query_grads(total, scale)


def cross_backward(scalars, q, kv, grad, mix, logs, scale):
    rows, width = q.shape
    keys = kv.shape[0]
    groups = width // LANES
    part, key_side, value_side, log_side = cross_specs(rows, keys, groups)
    return pl.pallas_call(
        functools.partial(cross_backward_kernel, scale=scale),
        grid_spec=pltpu.PrefetchScalarGridSpec(
            num_scalar_prefetch=2,
            grid=(groups,),
            in_specs=[part, key_side, value_side, part, part, log_side],
            out_specs=[part, key_side, key_side],
        ),
        out_shape=[
            shape_of((rows, width), BF16),
            shape_of((keys, width), BF16),
            shape_of((keys, width), BF16),
        ],
        compiler_params=params(),
        cost_estimate=cost(
            rows * keys * width * 20, (rows * 4 + keys * 4) * width * 2, rows * keys * groups * 2
        ),
        name="cross_backward",
    )(*scalars, q, kv, kv, grad, mix, logs)


def norm_parts(values):
    center = values - jnp.mean(values, axis=-1, keepdims=True)
    inverse = lax.rsqrt(jnp.mean(center * center, axis=-1, keepdims=True) + EPS)
    return center * inverse, inverse


def norm_back(pre_sum, gain, grad_out):
    normed, inverse = norm_parts(pre_sum)
    grad_normed = grad_out * gain
    grad_pre = inverse * (
        grad_normed
        - jnp.mean(grad_normed, axis=-1, keepdims=True)
        - normed * jnp.mean(grad_normed * normed, axis=-1, keepdims=True)
    )
    return (
        grad_pre,
        jnp.sum(grad_out * normed, axis=0, keepdims=True),
        jnp.sum(grad_out, axis=0, keepdims=True),
    )


def project_kernel(x_ref, w_ref, qb_ref, vb_ref, q_ref, kv_ref, low_ref, *, scale):
    columns = q_ref.shape[1]
    low = x_ref[0].astype(BF16)
    low_ref[...] = low
    out = nn(low, w_ref[...])
    q_ref[...] = ((out[:, :columns] + qb_ref[...]) * scale).astype(BF16)
    kv_ref[:, :columns] = out[:, columns : 2 * columns].astype(BF16)
    kv_ref[:, columns:] = (out[:, 2 * columns :] + vb_ref[...]).astype(BF16)


def project(x, w, qb, vb, scale):
    _, rows, width = x.shape
    columns = qb.shape[1]
    return pl.pallas_call(
        functools.partial(project_kernel, scale=scale),
        grid=(rows // TILE,),
        in_specs=[
            pl.BlockSpec((1, TILE, width), lambda b: (0, b, 0)),
            whole(w.shape),
            whole(qb.shape),
            whole(vb.shape),
        ],
        out_specs=[
            pl.BlockSpec((TILE, columns), lambda b: (b, 0)),
            pl.BlockSpec((TILE, 2 * columns), lambda b: (b, 0)),
            pl.BlockSpec((TILE, width), lambda b: (b, 0)),
        ],
        out_shape=[
            shape_of((rows, columns), BF16),
            shape_of((rows, 2 * columns), BF16),
            shape_of((rows, width), BF16),
        ],
        compiler_params=params(),
        cost_estimate=cost(rows * width * columns * 6, rows * width * 8),
        name="project",
    )(x, w, qb, vb)


def assemble_kernel(info_ref, near_ref, far_ref, ckv_ref, o_ref, cq_ref, bias_ref):
    tensors, _, columns = o_ref.shape
    width = tensors * columns
    rows = near_ref.shape[2] - bias_ref.shape[1]

    def put(ref):
        for z in range(tensors):
            part = slice(z * columns, (z + 1) * columns)
            late = slice(width + z * columns, width + (z + 1) * columns)
            ckv_ref[:, part] = ref[0, z, :rows, :columns]
            ckv_ref[:, late] = ref[0, z, :rows, columns : 2 * columns]
            o_ref[z] = ref[0, z, :rows, 2 * columns : 3 * columns]
            cq_ref[:, part] = ref[0, z, :rows, 3 * columns :]
        bias_ref[...] = ref[0, :, rows:, :]

    other = (pl.program_id(0) & 1) ^ (info_ref[0] & 1)

    @pl.when(other == 0)
    def _():
        put(near_ref)

    @pl.when(other != 0)
    def _():
        put(far_ref)


def assemble(info, near, far, shards, columns, bias_rows):
    _, tensors, rows, packed = near.shape
    rows -= bias_rows
    width = tensors * columns
    height = shards * rows
    side = pl.BlockSpec((1,) + near.shape[1:], lambda s, i: ((s >> 1) ^ (i[0] >> 1), 0, 0, 0))
    bias = (tensors, bias_rows, packed)
    return pl.pallas_call(
        assemble_kernel,
        grid_spec=pltpu.PrefetchScalarGridSpec(
            num_scalar_prefetch=1,
            grid=(shards,),
            in_specs=[side, side],
            out_specs=[
                pl.BlockSpec((rows, 2 * width), lambda s, i: (s, 0)),
                pl.BlockSpec((tensors, rows, columns), lambda s, i: (0, s, 0)),
                pl.BlockSpec((rows, width), lambda s, i: (s, 0)),
                whole(bias),
            ],
        ),
        out_shape=[
            shape_of((height, 2 * width), BF16),
            shape_of((tensors, height, columns), BF16),
            shape_of((height, width), BF16),
            shape_of(bias, BF16),
        ],
        compiler_params=params(),
        cost_estimate=cost(0, near.size * 8),
        name="assemble",
    )(info, near, far)


def bias_part(bias_ref, j, start, columns):
    width = bias_ref.shape[2]
    row, lane = divmod(start, width)
    tall = bias_ref[j].astype(F32)
    full = tall[:2] + tall[2:4]
    if lane + columns <= width:
        return full[row : row + 1, lane : lane + columns]
    return jnp.concatenate(
        [full[row : row + 1, lane:], full[row + 1 : row + 2, : lane + columns - width]], axis=1
    )


def tensor_row(bias_ref, start, columns):
    return jnp.concatenate(
        [bias_part(bias_ref, j, start, columns) for j in range(bias_ref.shape[0])], axis=1
    )


def after_self_kernel(
    info_ref, x_ref, o_ref, cq_ref, ob_ref, gain_ref, shift_ref, bias_ref, *rest, scale
):
    mix_refs, (sum_ref, low_ref, q_ref, joined_ref) = rest[:-4], rest[-4:]
    joined_ref[...] = jnp.concatenate([mix_ref[...] for mix_ref in mix_refs], axis=1)
    total = x_ref[0] + ob_ref[...]
    for j, mix_ref in enumerate(mix_refs):
        total = total + nt(mix_ref[...], o_ref[j])
    sum_ref[...] = total
    hidden = norm_parts(total)[0] * gain_ref[...] + shift_ref[...]
    low = hidden.astype(BF16)
    low_ref[...] = low
    bias = tensor_row(bias_ref, 0, mix_refs[0].shape[1])
    q_ref[...] = ((nn(low, cq_ref[...]) + bias) * scale).astype(BF16)


def after_self(info, x, o, cq, ob, gain, shift, bias, mixes, scale):
    width = x.shape[2]
    rows = mixes[0].shape[0]
    return pl.pallas_call(
        functools.partial(after_self_kernel, scale=scale),
        grid_spec=pltpu.PrefetchScalarGridSpec(
            num_scalar_prefetch=1,
            grid=(1,),
            in_specs=[pl.BlockSpec((1, rows, width), lambda s, i: (0, i[2], 0))]
            + [whole(a.shape) for a in (o, cq, ob, gain, shift, bias) + tuple(mixes)],
            out_specs=[whole((rows, width))] * 4,
        ),
        out_shape=[shape_of((rows, width), F32)] + [shape_of((rows, width), BF16)] * 3,
        compiler_params=params(),
        cost_estimate=cost(rows * width * width * 4, width * width * 4 + rows * width * 12),
        name="after_self",
    )(info, x, o, cq, ob, gain, shift, bias, *mixes)


def encode_kernel(info_ref, own_ref, sent_ref, w_ref, bias_ref, low_ref, kv_ref, *, columns):
    width = low_ref.shape[1]
    half = pl.num_programs(0) // 2

    @pl.when(pl.program_id(0) < half)
    def _():
        low_ref[...] = own_ref[0].astype(BF16)

    @pl.when(pl.program_id(0) >= half)
    def _():
        low_ref[...] = sent_ref[...]

    out = nn(low_ref[...], w_ref[...])
    kv_ref[:, :width] = out[:, :width].astype(BF16)
    kv_ref[:, width:] = (
        out[:, width:] + tensor_row(bias_ref, columns, columns)
    ).astype(BF16)


def encode(info, own, sent, w, bias, columns):
    _, rows, width = own.shape
    half = rows // TILE
    return pl.pallas_call(
        functools.partial(encode_kernel, columns=columns),
        grid_spec=pltpu.PrefetchScalarGridSpec(
            num_scalar_prefetch=1,
            grid=(2 * half,),
            in_specs=[
                pl.BlockSpec((1, TILE, width), lambda b, i: (0, jnp.minimum(b, half - 1), 0)),
                pl.BlockSpec((TILE, width), lambda b, i: (jnp.maximum(b - half, 0), 0)),
                whole(w.shape),
                whole(bias.shape),
            ],
            out_specs=[
                pl.BlockSpec((TILE, width), lambda b, i: (b, 0)),
                pl.BlockSpec((TILE, 2 * width), lambda b, i: (b, 0)),
            ],
        ),
        out_shape=[shape_of((2 * rows, width), BF16), shape_of((2 * rows, 2 * width), BF16)],
        compiler_params=params(),
        cost_estimate=cost(rows * width * width * 8, rows * width * 14),
        name="encode",
    )(info, own, sent, w, bias)


def gelu_parts(values):
    half = 0.5 * (1.0 + lax.erf(values * (0.5**0.5)))
    slope = half + values * (jnp.exp(-0.5 * values * values) * (0.5 / jnp.pi) ** 0.5)
    return values * half, slope


def feed_kernel(
    info_ref,
    sum_ref,
    vectors_ref,
    mix_ref,
    packed_ref,
    bias_ref,
    goal_ref,
    w_ref,
    result_ref,
    near_ref,
    far_ref,
    grad_ref,
    grad_low_ref,
    grad_mix_ref,
    sums_ref,
    two_ref,
    low_ref,
    low_t_ref,
    act_ref,
    slope_ref,
    acc_ref,
    three_low_ref,
    three_t_ref,
    co_ref,
):
    phase, z = pl.program_id(0), pl.program_id(1)
    tensors = pl.num_programs(1)
    rows, width = sum_ref.shape
    hidden_units = w_ref.shape[3]
    piece = width // w_ref.shape[1]
    up = w_ref[0, :, :piece].reshape(width, hidden_units)
    down = w_ref[0, :, piece : 2 * piece].reshape(width, hidden_units)
    gain1, shift1, cob, gain2, shift2, downb, gain3, shift3 = (
        vectors_ref[i : i + 1, :] for i in range(1, 9)
    )

    @pl.when((phase == 0) & (z == 0))
    def _():
        _, shards, chunk, _ = packed_ref.shape
        columns = co_ref.shape[2]
        for t in range(co_ref.shape[0]):
            for s in range(shards):
                for i in range(piece // chunk):
                    start = s * piece + i * chunk
                    co_ref[t, start : start + chunk, :] = packed_ref[
                        t, s, :, i * columns : (i + 1) * columns
                    ]
        hidden_one = norm_parts(sum_ref[...])[0] * gain1 + shift1
        sum_two = hidden_one + cob
        for j in range(co_ref.shape[0]):
            part = mix_ref[:, j * columns : (j + 1) * columns]
            sum_two = sum_two + nt(part, co_ref[info_ref[2] ^ j])
        two_ref[...] = sum_two
        hidden_two = norm_parts(sum_two)[0] * gain2 + shift2
        low_ref[...] = hidden_two.astype(BF16)
        low_t_ref[...] = hidden_two.T.astype(BF16)
        acc_ref[...] = hidden_two + downb
        sums_ref[...] = jnp.zeros_like(sums_ref)

    @pl.when(phase == 0)
    def _():
        bias = bias_part(bias_ref, z ^ info_ref[2], 2 * co_ref.shape[2], hidden_units)
        pre = nn(low_ref[...], up) + bias
        value, slope = gelu_parts(pre)
        act = value.astype(BF16)
        act_ref[z] = act
        slope_ref[z] = slope
        acc_ref[...] += nt(act, down)

    @pl.when((phase == 0) & (z == tensors - 1))
    def _():
        sum_three = acc_ref[...]
        result = norm_parts(sum_three)[0] * gain3 + shift3
        result_ref[...] = result.astype(BF16)
        grad_three, *both = norm_back(sum_three, gain3, goal_ref[0])
        sums_ref[0:1, :] = both[0]
        sums_ref[1:2, :] = both[1]
        sums_ref[2:3, :] = jnp.sum(grad_three, axis=0, keepdims=True)
        acc_ref[...] = grad_three
        three_low_ref[...] = grad_three.astype(BF16)
        three_t_ref[...] = grad_three.T.astype(BF16)

    @pl.when(phase == 1)
    def _():
        grad_pre = nn(three_low_ref[...], down) * slope_ref[z]
        sums_ref[pl.ds(8 + z, 1), :hidden_units] = jnp.sum(grad_pre, axis=0, keepdims=True)
        pre_low = grad_pre.astype(BF16)
        acc_ref[...] += nt(pre_low, up)
        products = (
            nn(low_t_ref[...], pre_low).astype(BF16),
            nn(three_t_ref[...], act_ref[z]).astype(BF16),
        )
        _, _, ctxs, _, share, _ = near_ref.shape

        def put(core):
            for mat, product in enumerate(products):
                for s in range(w_ref.shape[1]):
                    ref = near_ref if (s & 1) == core else far_ref
                    for c in range(ctxs):
                        start = s * piece + c * share
                        ref[mat, (s >> 1) ^ (info_ref[0] >> 1), c ^ info_ref[1], 0] = product[
                            start : start + share
                        ]

        @pl.when((info_ref[0] & 1) == 0)
        def _():
            put(0)

        @pl.when((info_ref[0] & 1) != 0)
        def _():
            put(1)

    @pl.when((phase == 1) & (z == tensors - 1))
    def _():
        grad_two, *both = norm_back(two_ref[...], gain2, acc_ref[...])
        sums_ref[3:4, :] = both[0]
        sums_ref[4:5, :] = both[1]
        sums_ref[5:6, :] = jnp.sum(grad_two, axis=0, keepdims=True)
        grad_ref[...] = grad_two
        low = grad_two.astype(BF16)
        grad_low_ref[...] = low
        columns = co_ref.shape[2]
        for j in range(co_ref.shape[0]):
            part = nn(low, co_ref[info_ref[2] ^ j]).astype(BF16)
            grad_mix_ref[:, j * columns : (j + 1) * columns] = part


def feed(info, sum_one, vectors, mix, columns, chunk, bias, goal, w, ctxs):
    rows, width = sum_one.shape
    tensors, shards, taller, hidden_units = w.shape
    piece = width // shards
    assert hidden_units == width
    grads = (2, shards // 2, ctxs, tensors, piece // ctxs, hidden_units)
    grads_spec = pl.BlockSpec(
        grads[:3] + (1,) + grads[4:], lambda p, z, i: (0, 0, 0, (p * z) ^ i[2], 0, 0)
    )
    head = (sum_one, vectors, mix)
    last = 2 * piece // chunk
    return pl.pallas_call(
        feed_kernel,
        grid_spec=pltpu.PrefetchScalarGridSpec(
            num_scalar_prefetch=1,
            grid=(2, tensors),
            in_specs=[whole(a.shape) for a in head]
            + [
                pl.BlockSpec(
                    (tensors, shards, chunk, hidden_units), lambda p, z, i: (0, 0, last, 0)
                ),
                whole(bias.shape),
                pl.BlockSpec((1, rows, width), lambda p, z, i: (0, i[2], 0)),
                pl.BlockSpec((1, shards, taller, hidden_units), lambda p, z, i: (z, 0, 0, 0)),
            ],
            out_specs=[
                whole((rows, width)),
                grads_spec,
                grads_spec,
                whole((rows, width)),
                whole((rows, width)),
                whole((rows, width)),
                whole((16, width)),
            ],
            scratch_shapes=[
                pltpu.VMEM((rows, width), F32),
                pltpu.VMEM((rows, width), BF16),
                pltpu.VMEM((width, rows), BF16),
                pltpu.VMEM((tensors, rows, hidden_units), BF16),
                pltpu.VMEM((tensors, rows, hidden_units), F32),
                pltpu.VMEM((rows, width), F32),
                pltpu.VMEM((rows, width), BF16),
                pltpu.VMEM((width, rows), BF16),
                pltpu.VMEM((tensors, width, columns), BF16),
            ],
        ),
        out_shape=[
            shape_of((rows, width), BF16),
            shape_of(grads, BF16),
            shape_of(grads, BF16),
            shape_of((rows, width), F32),
            shape_of((rows, width), BF16),
            shape_of((rows, width), BF16),
            shape_of((16, width), F32),
        ],
        compiler_params=params(),
        cost_estimate=cost(rows * w.size * 6, w.size * 6, rows * width * tensors * 2),
        name="feed",
    )(info, *head, w, bias, goal, w)


def before_self_kernel(
    info_ref, grad_ref, dq_ref, cq_ref, sum_ref, gain_ref, dv_ref, o_ref, *out_refs
):
    grad_one_ref, low_ref, sums_ref = out_refs[:3]
    mix_refs = out_refs[3:]
    tensors, _, columns = o_ref.shape
    grad_hidden = grad_ref[...] + nt(dq_ref[...], cq_ref[...])
    grad_one, gain, shift = norm_back(sum_ref[...], gain_ref[...], grad_hidden)
    grad_one_ref[...] = grad_one
    low = grad_one.astype(BF16)
    low_ref[...] = low
    for j, mix_ref in enumerate(mix_refs):
        mix_ref[...] = nn(low, o_ref[j]).astype(BF16)
    sums_ref[...] = jnp.zeros_like(sums_ref)
    sums_ref[0:1, :] = gain
    sums_ref[1:2, :] = shift
    sums_ref[2:3, :] = jnp.sum(grad_one, axis=0, keepdims=True)
    queries = jnp.sum(dq_ref[...].astype(F32), axis=0, keepdims=True)
    values = jnp.sum(dv_ref[...].astype(F32), axis=0, keepdims=True)
    for j in range(tensors):
        part = slice(j * columns, (j + 1) * columns)
        at = info_ref[2] ^ j
        sums_ref[pl.ds(8 + at, 1), :columns] = queries[:, part]
        sums_ref[pl.ds(8 + tensors + at, 1), :columns] = values[:, part]


def before_self(info, grad, dq, cq, sum_one, gain, dv, o):
    rows, width = grad.shape
    tensors, _, columns = o.shape
    args = (grad, dq, cq, sum_one, gain, dv, o)
    return pl.pallas_call(
        before_self_kernel,
        grid_spec=pltpu.PrefetchScalarGridSpec(
            num_scalar_prefetch=1,
            grid=(1,),
            in_specs=[whole(a.shape) for a in args],
            out_specs=[whole((rows, width))] * 2
            + [whole((8 + 2 * tensors, width))]
            + [whole((rows, columns))] * tensors,
        ),
        out_shape=[
            shape_of((rows, width), F32),
            shape_of((rows, width), BF16),
            shape_of((8 + 2 * tensors, width), F32),
        ]
        + [shape_of((rows, columns), BF16)] * tensors,
        compiler_params=params(),
        cost_estimate=cost(rows * width * width * 4, width * width * 6 + rows * width * 14),
        name="before_self",
    )(info, *args)


def encoder_grad_kernel(dk_ref, dv_ref, w_ref, keep_ref, send_ref):
    width = dk_ref.shape[1]
    part = nt(dk_ref[...], w_ref[:, :width]) + nt(dv_ref[...], w_ref[:, width:])
    half = pl.num_programs(0) // 2

    @pl.when(pl.program_id(0) < half)
    def _():
        send_ref[...] = part.astype(BF16)

    @pl.when(pl.program_id(0) >= half)
    def _():
        keep_ref[...] = part


def encoder_grad(dk, dv, w):
    keys, width = dk.shape
    half = keys // TILE // 2
    side = pl.BlockSpec((TILE, width), lambda b: (jnp.where(b < half, b + half, b - half), 0))
    return pl.pallas_call(
        encoder_grad_kernel,
        grid=(2 * half,),
        in_specs=[side, side, whole(w.shape)],
        out_specs=[
            pl.BlockSpec((TILE, width), lambda b: (jnp.maximum(b - half, 0), 0)),
            pl.BlockSpec((TILE, width), lambda b: (jnp.minimum(b, half - 1), 0)),
        ],
        out_shape=[shape_of((keys // 2, width), F32), shape_of((keys // 2, width), BF16)],
        compiler_params=params(),
        cost_estimate=cost(keys * width * width * 4, keys * width * 10),
        name="encoder_grad",
    )(dk, dv, w)


def square_grads_kernel(info_ref, *refs, ctxs, groups, places):
    count = sum(groups)
    lefts = max(places) + 1
    left_refs, right_refs = refs[:lefts], refs[lefts : lefts + count]
    flipped = refs[-lefts:]
    outs = refs[lefts + count : -lefts]
    i, other = pl.program_id(0), pl.program_id(1)
    _, _, tensors, share, packed = outs[0].shape
    piece = share * ctxs
    columns = packed // groups[0]

    @pl.when((i == 0) & (other == 0))
    def _():
        for left_ref, flipped_ref in zip(left_refs, flipped):
            flipped_ref[...] = flip(left_ref[...])

    s = ((i ^ (info_ref[0] >> 1)) << 1) + ((info_ref[0] & 1) ^ other)
    rows = pl.ds(pl.multiple_of(s * piece, piece), piece)
    grads = [
        nn(flipped[at][rows, :], right_ref[...]).astype(BF16)
        for at, right_ref in zip(places, right_refs)
    ]

    def put(refs):
        for z in range(tensors):
            part = slice(z * columns, (z + 1) * columns)
            start = 0
            for ref, size in zip(refs, groups):
                tile = jnp.concatenate(
                    [grad[:, part] for grad in grads[start : start + size]], axis=1
                )
                start += size
                for r in range(ctxs):
                    chosen = tile[:share]
                    for c in range(1, ctxs):
                        chosen = jnp.where(
                            (info_ref[1] ^ r) == c, tile[c * share : (c + 1) * share], chosen
                        )
                    ref[0, r, z] = chosen

    @pl.when(other == 0)
    def _():
        put(outs[: len(groups)])

    @pl.when(other != 0)
    def _():
        put(outs[len(groups) :])


def square_grads(info, pairs, groups, sizes):
    shards, ctxs, tensors = sizes
    width = pairs[0][0].shape[1]
    share = width // shards // ctxs
    lefts, places = [], []
    for left, _ in pairs:
        same = [at for at, other in enumerate(lefts) if other is left]
        places.append(same[0] if same else len(lefts))
        if not same:
            lefts.append(left)
    args = lefts + [right for _, right in pairs]
    sides = [
        (shards // 2, ctxs, tensors, share, size * width // tensors) for size in groups
    ] * 2
    return pl.pallas_call(
        functools.partial(
            square_grads_kernel, ctxs=ctxs, groups=groups, places=tuple(places)
        ),
        grid_spec=pltpu.PrefetchScalarGridSpec(
            num_scalar_prefetch=1,
            grid=(shards // 2, 2),
            in_specs=[whole(a.shape) for a in args],
            out_specs=[
                pl.BlockSpec((1,) + side[1:], lambda i, c, n: (i, 0, 0, 0, 0)) for side in sides
            ],
            scratch_shapes=[pltpu.VMEM((width, left.shape[0]), BF16) for left in lefts],
        ),
        out_shape=[shape_of(side, BF16) for side in sides],
        compiler_params=params(),
        cost_estimate=cost(2 * width * sum(a.size for a in args), width * width * 8),
        name="square_grads",
    )(info, *args)


def input_grad_kernel(
    info_ref, dq_ref, down_ref, dtrunk_ref, came_ref, low_ref, w_ref, *rest, ctxs, tensors
):
    part_refs = rest[:tensors]
    near_ref, far_ref, dw_ref = rest[tensors:]
    b = pl.program_id(0)

    @pl.when(b == 0)
    def _():
        dw_ref[...] = jnp.zeros_like(dw_ref)

    trunk = dtrunk_ref[...].astype(F32) + came_ref[...].astype(F32)
    dkv = (down_ref[...] + jnp.where(info_ref[1] == 0, trunk, 0.0)).astype(BF16)
    grads = jnp.concatenate([dq_ref[...], dkv], axis=1)
    dw_ref[...] += tn(low_ref[...], grads)
    put_slot(b ^ info_ref[2], nt(grads, w_ref[...]), part_refs)

    @pl.when(b == pl.num_programs(0) - 1)
    def _():
        halves, _, share, _ = near_ref.shape
        for other, ref in ((0, near_ref), (1, far_ref)):
            for i in range(halves):
                s = ((i ^ (info_ref[0] >> 1)) << 1) + ((info_ref[0] & 1) ^ other)
                for r in range(ctxs):
                    start = (s * ctxs + (info_ref[1] ^ r)) * share
                    ref[i, r] = dw_ref[pl.ds(pl.multiple_of(start, share), share), :].astype(BF16)


def input_grad(info, dq, down, dtrunk, came, low, w, sizes):
    shards, ctxs, tensors = sizes
    rows, columns = dq.shape
    width = low.shape[1]
    share = width // shards // ctxs
    side = (shards // 2, ctxs, share, 3 * columns)

    def tile(n):
        return pl.BlockSpec((TILE, n), lambda b, i: (b, 0))

    return pl.pallas_call(
        functools.partial(input_grad_kernel, ctxs=ctxs, tensors=tensors),
        grid_spec=pltpu.PrefetchScalarGridSpec(
            num_scalar_prefetch=1,
            grid=(rows // TILE,),
            in_specs=[
                tile(columns),
                tile(2 * columns),
                tile(2 * columns),
                tile(2 * columns),
                tile(width),
                whole(w.shape),
            ],
            out_specs=[whole((TILE, width))] * tensors
            + [whole(side), whole(side)],
            scratch_shapes=[pltpu.VMEM((width, 3 * columns), F32)],
        ),
        out_shape=[shape_of((TILE, width), F32)]
        + [shape_of((TILE, width), BF16)] * (tensors - 1)
        + [shape_of(side, BF16)] * 2,
        compiler_params=params(),
        cost_estimate=cost(rows * width * columns * 12, rows * width * 14),
        name="input_grad",
    )(info, dq, down, dtrunk, came, low, w)


def lay_rows_kernel(info_ref, *refs):
    in_refs, out_ref = refs[:-1], refs[-1]
    out_ref[...] = take_slot(pl.program_id(0) ^ info_ref[2], in_refs).astype(F32)


def lay_rows(info, parts):
    rows, width = parts[0].shape
    return pl.pallas_call(
        lay_rows_kernel,
        grid_spec=pltpu.PrefetchScalarGridSpec(
            num_scalar_prefetch=1,
            grid=(len(parts),),
            in_specs=[whole((rows, width))] * len(parts),
            out_specs=pl.BlockSpec((rows, width), lambda b, i: (b, 0)),
        ),
        out_shape=shape_of((rows * len(parts), width), F32),
        compiler_params=params(),
        cost_estimate=cost(0, rows * width * len(parts) * 6),
        name="lay_rows",
    )(info, *parts)


def local(sizes, *args):
    (
        layer_input,
        encoder_out,
        enc_length,
        parent_ids,
        token_segment,
        self_query,
        self_key,
        self_value,
        self_output,
        cross_query,
        cross_key,
        cross_value,
        cross_output,
        ffn_up,
        ffn_down,
        self_qbias,
        self_vbias,
        self_obias,
        cross_qbias,
        cross_vbias,
        cross_obias,
        ffn_upbias,
        ffn_downbias,
        norm1_gain,
        norm1_shift,
        norm2_gain,
        norm2_shift,
        norm3_gain,
        norm3_shift,
        out_grad,
    ) = args
    shards, ctxs, tensors = sizes["shard"], sizes["ctx"], sizes["tensor"]
    me_ctx = lax.axis_index("ctx")
    info = jnp.stack([lax.axis_index("shard"), me_ctx, lax.axis_index("tensor")]).astype(jnp.int32)
    scale = HEAD_DIM ** (-0.5)
    local_rows, width = layer_input.shape[1:]
    piece, columns = self_query.shape
    heads = columns // HEAD_DIM
    seg = token_segment.shape[1] // parent_ids.shape[1]
    assert local_rows == tensors * TILE and ctxs == 2

    def bits_of(axis):
        return [1 << k for k in range(sizes[axis].bit_length() - 1)]

    def swap(a, axis, bit):
        return lax.ppermute(a, axis, [(i, i ^ bit) for i in range(sizes[axis])])

    shard_bits = [("shard", 1 << k) for k in range(1, shards.bit_length() - 1)]

    def over_tensor(a):
        return [a] + [swap(a, "tensor", j) for j in range(1, tensors)]

    def grow(a, axis, bit, *others):
        return jnp.stack(tie([a, swap(a, axis, bit)], *others))

    def add(a, b):
        return (a.astype(F32) + b.astype(F32)).astype(BF16)

    def reduce_levels(near, far):
        came = swap(far, "shard", 1)
        lead = (2,) * len(shard_bits) + near.shape[1:]
        near, came = near.reshape(lead), came.reshape(lead)

        for axis, bit in list(reversed(shard_bits)) + [("ctx", 1)]:
            send = add(near[1], came[1])
            near, came = add(near[0], came[0]), swap(send, axis, bit)
        return add(near, came)

    def join_ctx(mine):
        other = swap(mine, "ctx", 1)
        first = me_ctx == 0
        return jnp.concatenate([jnp.where(first, mine, other), jnp.where(first, other, mine)])

    def row(vector):
        return vector.reshape(1, -1)

    def tie(a, *others):
        return lax.optimization_barrier((a,) + others)[0]

    vectors = jnp.stack(
        [
            self_obias,
            norm1_gain,
            norm1_shift,
            cross_obias,
            norm2_gain,
            norm2_shift,
            ffn_downbias,
            norm3_gain,
            norm3_shift,
        ]
    )

    pack = tensors if piece % (16 * tensors) == 0 else 1
    chunk = piece // pack
    packed_co = jnp.concatenate(
        [cross_output.T[i * chunk : (i + 1) * chunk] for i in range(pack)], axis=1
    )
    packed_co = jnp.pad(packed_co, ((0, 0), (0, width - packed_co.shape[1])))
    ffn_piece = jnp.concatenate([ffn_up, ffn_down.T, packed_co], axis=0)
    bias = jnp.concatenate([cross_qbias, cross_vbias, ffn_upbias])
    bias = jnp.pad(bias, (0, -bias.shape[0] % width)).reshape(-1, width)
    bias_high = lax.reduce_precision(bias, 8, 7)
    bias_rows = 16
    bias = jnp.concatenate([bias_high, bias - bias_high]).astype(BF16)
    bias = jnp.pad(bias, ((0, bias_rows - bias.shape[0]), (0, 0)))
    squares = over_tensor(
        jnp.concatenate(
            [
                jnp.concatenate([cross_key, cross_value, self_output.T, cross_query], axis=1),
                bias,
            ],
            axis=0,
        )
    )
    enc_sent = swap(encoder_out[0].astype(BF16), "ctx", 1)
    qkv_weights = lax.all_gather(
        jnp.concatenate([self_query, self_key, self_value], axis=1), "shard", axis=0, tiled=True
    )

    scalars = (info, parent_ids[0], token_segment[0])
    q, kv, input_low = project(layer_input, qkv_weights, row(self_qbias), row(self_vbias), scale)
    squares = jnp.stack(tie(squares, q))
    ffn_all = lax.all_gather(tie(ffn_piece, squares), ("tensor", "shard"), axis=0, tiled=True)
    kv_sent = lax.ppermute(tie(kv, squares), "ctx", [(0, 1)])
    for axis, bit in shard_bits[:-1]:
        squares = grow(squares, axis, bit, kv_sent)
    kv_sent = tie(kv_sent, squares)
    *mixes, self_logs = self_forward(scalars, q, kv, kv_sent, tensors, heads, seg)
    squares = grow(squares, *shard_bits[-1], self_logs)
    near = squares.reshape((shards // 2,) + squares.shape[-3:])
    far = swap(near, "shard", 1)
    all_heads = mixes[:1] + [swap(mixes[j], "tensor", j) for j in range(1, tensors)]
    weight_ckv, weight_o, weight_cq, bias = assemble(info, near, far, shards, columns, bias_rows)
    enc_low, ckv = encode(info, encoder_out, enc_sent, weight_ckv, bias, columns)
    all_heads = all_heads[:1] + list(tie(all_heads[1:], ckv))
    sum_one, one_low, cq, self_mix = after_self(
        info,
        layer_input,
        weight_o,
        weight_cq,
        vectors[0:1],
        vectors[1:2],
        vectors[2:3],
        bias,
        all_heads,
        scale,
    )

    cross_scalars = (info, enc_length)
    cross_mix, cross_logs = cross_forward(cross_scalars, cq, ckv)

    result, ffn_near, ffn_far, grad_two, two_grad_low, grad_cmix, feed_sums = feed(
        info,
        sum_one,
        vectors,
        cross_mix,
        columns,
        chunk,
        bias,
        out_grad,
        ffn_all.reshape(tensors, shards, -1, width),
        ctxs,
    )
    ffn_came = swap(ffn_far, "shard", 1)
    result_all = lax.all_gather(result, "tensor", axis=0, tiled=True)

    class Path:
        def __init__(self, near, came, order):
            lead = (2,) * len(shard_bits) + near.shape[1:]
            self.dims = list(reversed(shard_bits)) + [("ctx", 1)]
            self.order = list(order)
            self.keep, self.came = near.reshape(lead), came.reshape(lead)

        def fold(self):
            near, came = self.keep, self.came
            if not self.order:
                self.keep = add(near, came)
                return
            dim = self.dims.index(self.order[0])
            self.dims.pop(dim)
            index = (slice(None),) * dim
            self.send = add(near[index + (1,)], came[index + (1,)])
            self.keep = add(near[index + (0,)], came[index + (0,)])

        def go(self):
            axis, bit = self.order.pop(0)
            self.came = swap(self.send, axis, bit)

    high = list(reversed(shard_bits))
    orders = [[("ctx", 1)] + high, high + [("ctx", 1)]]

    dcq, dck, dcv = cross_backward(cross_scalars, cq, ckv, grad_cmix, cross_mix, cross_logs, scale)
    enc_keep, enc_send = encoder_grad(dck, dcv, weight_ckv)
    enc_came = swap(enc_send, "ctx", 1)
    grad_two = tie(grad_two, enc_send)
    grad_one, one_grad_low, self_sums, *grad_mixes = before_self(
        info, grad_two, dcq, weight_cq, sum_one, vectors[1:2], dcv, weight_o
    )
    head_grads = grad_mixes[:1] + [swap(grad_mixes[j], "tensor", j) for j in range(1, tensors)]
    mesh_sizes = (shards, ctxs, tensors)
    early_sums = jnp.concatenate([feed_sums, self_sums], axis=0)
    early_sums = early_sums + swap(early_sums, "tensor", 1)
    ffn_came = tie(ffn_came, one_grad_low)
    ffn_paths = [Path(ffn_near[i], ffn_came[i], order) for i, order in enumerate(orders)]
    sends = []
    for p in ffn_paths:
        p.fold()
        sends += [p.send, p.keep]
        p.go()
    enc_mine = (enc_keep + tie(enc_came, *sends).astype(F32)).astype(BF16)
    grad_encoder = lax.psum(enc_mine, "tensor")
    enc_tied = tie(enc_low, early_sums, enc_mine, result_all)
    near_a, near_b, far_a, far_b = square_grads(
        info,
        [
            (enc_tied, dck),
            (enc_tied, dcv),
            (one_grad_low, self_mix),
            (one_low, dcq),
            (two_grad_low, cross_mix),
        ],
        (2, 3),
        mesh_sizes,
    )
    head_grads, far_a, far_b = tie((head_grads, far_a, far_b), far_b)
    for _ in range(len(high)):
        for p in ffn_paths:
            p.came = tie(p.came, far_b)
            p.fold()
            head_grads = tie(head_grads, p.send, p.keep)
            p.go()
    sums_came = [swap(early_sums, "tensor", bit) for bit in bits_of("tensor")[1:2]]

    dq, down, dtrunk, late_sums = self_backward(
        scalars, q, kv, kv_sent, head_grads, mixes, self_logs, heads, seg, scale, width
    )
    trunk_came = lax.ppermute(dtrunk, "ctx", [(1, 0)])
    paths = [
        Path(near, tie(swap(far, "shard", 1), dtrunk), order)
        for near, far, order in zip((near_a, near_b), (far_a, far_b), orders)
    ]
    for p in paths:
        p.fold()
        trunk_came = tie(trunk_came, p.send, p.keep)
        p.go()
    for p in ffn_paths:
        p.came = tie(p.came, dtrunk, grad_encoder, *(q.keep for q in paths))
        p.fold()
    ffn_blocks = jnp.concatenate([p.keep for p in ffn_paths], axis=1)
    ffn_came = [swap(ffn_blocks[j], "tensor", j) for j in range(1, tensors)]
    for came in tie(sums_came, dtrunk):
        early_sums = early_sums + came
    for bit in bits_of("tensor")[2:]:
        early_sums = early_sums + swap(early_sums, "tensor", bit)
    sums = jnp.concatenate([early_sums, late_sums], axis=0)
    for axis, bit in [("shard", 1)] + shard_bits:
        sums = sums + swap(sums, axis, bit)
    trunk_came = tie(trunk_came, ffn_blocks, sums)
    *parts, near, far = input_grad(
        info, dq, down, dtrunk, trunk_came, input_low, qkv_weights, mesh_sizes
    )
    part_came = [swap(parts[j], "tensor", j) for j in range(1, tensors)]
    for _ in range(len(high)):
        for p in paths:
            p.came = tie(p.came, parts[0])
            p.fold()
            p.go()
    lead = (2,) * len(shard_bits) + near.shape[1:]
    near, far = near.reshape(lead), swap(far, "shard", 1).reshape(lead)
    send, keep = add(near[1], far[1]), add(near[0], far[0])
    for axis, bit in list(reversed(shard_bits))[:-1]:
        came = swap(send, axis, bit)
        send, keep = add(keep[1], came[1]), add(keep[0], came[0])
    came = swap(send, *shard_bits[0])
    keep = add(keep, came)
    ffn_total = ffn_blocks[0].astype(F32)
    for part in tie(ffn_came, parts[0]):
        ffn_total = ffn_total + part.astype(F32)
    ffn_total = ffn_total.astype(BF16)
    sums_came = swap(tie(sums, parts[0]), "ctx", 1)
    for p in paths:
        p.fold()
    squares = jnp.concatenate([p.keep for p in paths], axis=2)
    square_came = [swap(squares[j], "tensor", j) for j in range(1, tensors)]
    part_came, square_came = tie((part_came, square_came), keep, ffn_total)
    square_total = squares[0].astype(F32)
    for part in square_came:
        square_total = square_total + part.astype(F32)
    square_total = square_total.astype(BF16)
    part_came = tie(part_came, square_total)
    input_mine = grad_one + parts[0]
    for part in part_came:
        input_mine = input_mine + part.astype(F32)
    input_mine = input_mine.astype(BF16)
    input_all = over_tensor(input_mine)
    ctx_came = [swap(a, "ctx", 1) for a in (keep, ffn_total, square_total)]
    ctx_came, sums_came = tie((ctx_came, sums_came), input_mine)
    qkv_came, ffn_came, square_came = ctx_came
    sums = sums + sums_came
    qkv_grads = [add(keep[r], qkv_came[r ^ 1]) for r in range(ctxs)]
    first = me_ctx == 0
    qkv_grads = jnp.concatenate(
        [jnp.where(first, qkv_grads[r], qkv_grads[r ^ 1]) for r in range(ctxs)]
    ).astype(F32)
    grad_q, grad_k, grad_v = (qkv_grads[:, i * columns : (i + 1) * columns] for i in range(3))

    def in_order(mine, other):
        return [
            jnp.where(first, mine, other).astype(F32),
            jnp.where(first, other, mine).astype(F32),
        ]

    share = piece // ctxs
    halves = in_order(ffn_total, ffn_came)
    grad_up = jnp.concatenate([half[:share] for half in halves])
    grad_down = jnp.concatenate([half[share:] for half in halves])
    squares = jnp.concatenate(in_order(square_total, square_came))
    grad_ck, grad_cv, grad_o, grad_cq, grad_co = (
        squares[:, i * columns : (i + 1) * columns] for i in range(5)
    )
    grad_encoder = tie(grad_encoder, input_all[1]).astype(F32)
    result_all = tie(result_all, input_all[1]).astype(F32)
    input_all = input_all[:1] + list(tie(input_all[1:], sums, qkv_grads, grad_up, squares))
    grad_input = lay_rows(info, input_all)
    me_tensor = info[2]

    def mine(start, size):
        return lax.dynamic_slice(sums, (start + me_tensor, 0), (1, size)).reshape(-1)

    base = 16 + 8
    later = base + 2 * tensors

    return (
        result_all[None],
        grad_input[None],
        grad_encoder[None],
        grad_q,
        grad_k,
        grad_v,
        grad_o.T,
        grad_cq,
        grad_ck,
        grad_cv,
        grad_co.T,
        grad_up,
        grad_down.T,
        mine(later, columns),
        mine(later + tensors, columns),
        sums[18],
        mine(base, columns),
        mine(base + tensors, columns),
        sums[5],
        mine(8, ffn_upbias.shape[0]),
        sums[2],
        sums[16],
        sums[17],
        sums[3],
        sums[4],
        sums[0],
        sums[1],
    )


def solution(mesh):
    sizes = {axis: mesh.shape[axis] for axis in ("shard", "ctx", "tensor")}
    rows = P("shard", "ctx", None)
    tall, wide = P("shard", "tensor"), P("tensor", "shard")
    mats = (tall, tall, tall, wide, tall, tall, tall, wide, tall, wide)
    part = P("tensor")
    vectors = (part, part, P(), part, part, P(), part) + (P(),) * 7
    tree = P("shard", None)
    return jax.shard_map(
        functools.partial(local, sizes),
        mesh=mesh,
        in_specs=(rows, rows, P("shard"), tree, tree) + mats + vectors + (rows,),
        out_specs=(rows, rows, rows) + mats + vectors,
        check_vma=False,
    )
```
